32 devices in a mesh: dp: 4 (over y, core), fsdp: 8 (over z, x).
Axes of the slice: x: 2, y: 2, z: 4, core: 2. Of those that a mesh axis runs over, the one named last changes fastest.
Arguments:
- tokens: bfloat16 [4096, 768], P(('dp', 'fsdp')), may hold values from -6 to 6
- cotangent: bfloat16 [4096, 768], P(('dp', 'fsdp')), may hold values from -6 to 6
- seq_lens: int32 [32, 8], P(('dp', 'fsdp')), may hold values from 0 to 128, as said below
- routes: int32 [4096, 1], P(('dp', 'fsdp')), may hold values from 0 to 7
- norm_gain: bfloat16 [768], P(('dp', 'fsdp')), may hold values from 0.5 to 1.5
- input_proj: bfloat16 [768, 3072], P(('dp', 'fsdp')), may hold values from -0.21875 to 0.21875
- conv_weight: bfloat16 [4, 1536], P(None, ('dp', 'fsdp')), may hold values from -3 to 3
- conv_bias: bfloat16 [1536], P(('dp', 'fsdp')), may hold values from -1.5 to 1.5
- select_proj: bfloat16 [1536, 80], P(('dp', 'fsdp')), may hold values from -0.15625 to 0.15625
- step_proj: bfloat16 [48, 1536], P(None, ('dp', 'fsdp')), may hold values from -0.875 to 0.875
- step_bias: bfloat16 [1536], P(('dp', 'fsdp')), may hold values from -4 to -1
- decay_log: bfloat16 [16, 1536], P(None, ('dp', 'fsdp')), may hold values from 0 to 2.765625
- skip_gain: bfloat16 [1536], P(('dp', 'fsdp')), may hold values from 0.5 to 1.5
- output_proj: bfloat16 [1536, 768], P(('dp', 'fsdp')), may hold values from -0.3125 to 0.3125
- moe_gain: bfloat16 [768], P(('dp', 'fsdp')), may hold values from 0.5 to 1.5
- router_weight: bfloat16 [768, 8], P(('dp', 'fsdp')), may hold values from -0.21875 to 0.21875
- up_weight: bfloat16 [8, 3072, 768], P('fsdp', 'dp'), may hold values from -0.21875 to 0.21875
- down_weight: bfloat16 [8, 3072, 768], P('fsdp', 'dp'), may hold values from -0.21875 to 0.21875
Outputs:
- block_out: bfloat16 [4096, 768], P(('dp', 'fsdp'))
- tokens_grad: float32 [4096, 768], P(('dp', 'fsdp'))
- norm_gain_grad: float32 [768], P(('dp', 'fsdp'))
- input_proj_grad: float32 [768, 3072], P(('dp', 'fsdp'))
- conv_weight_grad: float32 [4, 1536], P(None, ('dp', 'fsdp'))
- conv_bias_grad: float32 [1536], P(('dp', 'fsdp'))
- select_proj_grad: float32 [1536, 80], P(('dp', 'fsdp'))
- step_proj_grad: float32 [48, 1536], P(None, ('dp', 'fsdp'))
- step_bias_grad: float32 [1536], P(('dp', 'fsdp'))
- decay_log_grad: float32 [16, 1536], P(None, ('dp', 'fsdp'))
- skip_gain_grad: float32 [1536], P(('dp', 'fsdp'))
- output_proj_grad: float32 [1536, 768], P(('dp', 'fsdp'))
- moe_gain_grad: float32 [768], P(('dp', 'fsdp'))
- router_weight_grad: float32 [768, 8], P(('dp', 'fsdp'))
- up_weight_grad: float32 [8, 3072, 768], P('fsdp', 'dp')
- down_weight_grad: float32 [8, 3072, 768], P('fsdp', 'dp')
The draws below stay inside these ranges and needn't reach their ends.
Inputs may be any that keep to these rules, and one draw needn't show every extreme that they name: `seq_lens`: row b lists the lengths of the sequences packed in order from the start of block b; a row sums to at most 128, the rest of the block is padding; in some rows one sequence fills the block.
All inputs are finite; a program needn't handle non-finite values.
Results may differ from the reference program's by a relative error of at most 0.012.
The reference program's roundings to bfloat16 on the way count: a program that leaves them out, or rounds other values in their place, can miss the bound.
Values may be sent and summed in bfloat16 or wider, within the bound.
No kernel may reach another device: no remote copies, remote signals or barrier semaphores. Data moves between devices by JAX's collectives and lax.ppermute only.
A program may use at most 256 MiB of HBM per device.

```python
import jax
import jax.numpy as jnp
from jax import lax

D = 768
E = 1536
N = 16
R = 48
K = 4
F = 3072
TOK_DEV = 128
SEQ_SLOTS = 8
SCAN_BLOCK = 64
EXPERTS = 8
SHARDS = 32
TOKENS = 4096
CAP = 20


def draw_seq_lens(key, part):
    keys = jax.random.split(key, 4)
    raw_lens = jax.random.randint(keys[0], (SHARDS, SEQ_SLOTS), 8, TOK_DEV // 4 + 8, dtype=jnp.int32)
    long_lens = jax.random.randint(keys[1], (SHARDS,), TOK_DEV // 2, TOK_DEV, dtype=jnp.int32)
    row_kind = jax.random.randint(keys[2], (SHARDS,), 0, 8, dtype=jnp.int32)
    row_kind = row_kind.at[0].set(0)
    first_len = jnp.where(row_kind == 1, long_lens, raw_lens[:, 0])
    raw_lens = raw_lens.at[:, 0].set(first_len)
    limit = TOK_DEV - jax.random.randint(keys[3], (SHARDS, 1), 0, TOK_DEV // 4, dtype=jnp.int32)
    seq_ends = jnp.minimum(jnp.cumsum(raw_lens, axis=1, dtype=jnp.int32), limit)
    lengths = jnp.diff(seq_ends, axis=1, prepend=jnp.zeros((SHARDS, 1), jnp.int32))
    whole_row = jnp.zeros_like(lengths).at[:, 0].set(TOK_DEV)
    return jnp.where((row_kind == 0)[:, None], whole_row, lengths).astype(jnp.int32)


def block_levels(own_key, dims, cuts, smallest, top_value):
    gain, own = 1.0, jax.random.fold_in(own_key, 6)
    for dim, parts in cuts:
        heights = jnp.exp(jax.random.uniform(jax.random.fold_in(own, dim), (parts,), jnp.float32, smallest / len(cuts), top_value / len(cuts)))
        gain = gain * jnp.repeat(heights, dims[dim] // parts).reshape([-1 if axis == dim else 1 for axis in range(len(dims))])
    return gain


def choose_distinct(rng, rows, count, top, lift):
    ranking = jax.random.permutation(jax.random.fold_in(rng, 1), count)
    boost = ranking
    for power in range(3):
        boost = boost * boost // count
    boost = boost * lift // count
    chance = jax.random.randint(jax.random.fold_in(rng, 2), (rows, count), 0, 4096) + boost
    holders = jax.random.permutation(jax.random.fold_in(rng, 3), rows)[jnp.arange(count) % rows]
    chance = jnp.where(jnp.arange(rows)[:, None] == holders[None, :], 1 << 14, chance)
    priority = chance * count + jnp.arange(count)
    return lax.top_k(priority.astype(jnp.int32), top)[1].astype(jnp.int32)


def centred(key, extent, deviation, reach, cuts=(), held_as=jnp.bfloat16):
    level = block_levels(key, extent, cuts, -0.22, 0.18) if cuts else 1.0
    drawn = jax.random.normal(key, extent, jnp.float32) * deviation * level
    return jnp.minimum(jnp.maximum(drawn, -reach), reach).astype(held_as)


def setup_inputs(seed: int = 0) -> dict:
    splits = jax.random.split(jax.random.key(seed), 19)
    tokens = centred(splits[0], (TOKENS, D), 1.0, 6.0, ((0, 32),))
    cotangent = centred(splits[1], (TOKENS, D), 1.0, 6.0, ((0, 32),))
    seq_lens = draw_seq_lens(jax.random.fold_in(splits[18], 71), 0)
    routes = choose_distinct(splits[3], TOKENS, EXPERTS, 1, 1024)
    norm_gain = jnp.clip(1.0 + 0.1 * jax.random.normal(splits[4], (D,), jnp.float32), 0.5, 1.5).astype(jnp.bfloat16)
    input_proj = centred(splits[5], (D, 2 * E), D ** -0.5, 0.21875, ((0, 32),))
    conv_weight = centred(splits[6], (K, E), K ** -0.5, 3.0, ((1, 32),))
    conv_bias = centred(splits[7], (E,), 0.3, 1.5, ((0, 32),))
    select_proj = centred(splits[8], (E, R + 2 * N), E ** -0.5, 0.15625, ((0, 32),))
    step_proj = centred(splits[9], (R, E), R ** -0.5, 0.875, ((1, 32),))
    step_bias = jnp.clip(-4.0 + 3.0 * jax.random.uniform(splits[10], (E,), jnp.float32) ** block_levels(splits[10], (E,), ((0, 32),), -0.2, 0.2), -4.0, -1.0).astype(jnp.bfloat16)
    decay_log = jnp.clip(2.765625 * jax.random.uniform(splits[11], (N, E), jnp.float32) ** block_levels(splits[11], (N, E), ((1, 32),), -0.2, 0.2), 0.0, 2.765625).astype(jnp.bfloat16)
    skip_gain = jnp.clip(1.0 + 0.1 * jax.random.normal(splits[12], (E,), jnp.float32), 0.5, 1.5).astype(jnp.bfloat16)
    output_proj = centred(splits[13], (E, D), (E // 4) ** -0.5, 0.3125, ((0, 32),))
    moe_gain = jnp.clip(1.0 + 0.1 * jax.random.normal(splits[14], (D,), jnp.float32), 0.5, 1.5).astype(jnp.bfloat16)
    router_weight = centred(splits[15], (D, EXPERTS), D ** -0.5, 0.21875, ((0, 32),))
    up_weight = centred(splits[16], (EXPERTS, F, D), D ** -0.5, 0.21875, ((0, 8), (1, 4)))
    down_weight = centred(splits[17], (EXPERTS, F, D), (F // 4) ** -0.5, 0.21875, ((0, 8), (1, 4)))
    return {"tokens": tokens, "cotangent": cotangent, "seq_lens": seq_lens, "routes": routes, "norm_gain": norm_gain, "input_proj": input_proj, "conv_weight": conv_weight, "conv_bias": conv_bias, "select_proj": select_proj, "step_proj": step_proj, "step_bias": step_bias, "decay_log": decay_log, "skip_gain": skip_gain, "output_proj": output_proj, "moe_gain": moe_gain, "router_weight": router_weight, "up_weight": up_weight, "down_weight": down_weight}


EPS = 1e-05

@jax.custom_vjp
def low(v):
    return lax.optimization_barrier(v.astype(jnp.bfloat16)).astype(jnp.float32)

@jax.custom_vjp
def low_back(v):
    return v

def low_keep(v):
    return (low(v), None)

def low_pass(kept, grad):
    return (grad,)

def back_keep(v):
    return (v, None)

def back_low(kept, grad):
    return (low(grad),)
low.defvjp(low_keep, low_pass)
low_back.defvjp(back_keep, back_low)

def matmul_high(left, right):
    return jnp.dot(left, right, precision=lax.Precision.HIGHEST)

def scale_norm(values, gain_row):
    return values * lax.rsqrt(lax.optimization_barrier(jnp.mean(values * values, axis=-1, keepdims=True)) + EPS) * gain_row

def causal_conv(inner_vals, conv_taps, conv_shift, offset):
    tap_count = conv_taps.shape[0]
    result = conv_shift[None, :] + conv_taps[tap_count - 1][None, :] * inner_vals
    for lag_steps in range(1, tap_count):
        moved = jnp.concatenate([jnp.zeros((lag_steps, inner_vals.shape[1]), inner_vals.dtype), inner_vals[:-lag_steps]], axis=0)
        allowed = (offset >= lag_steps).astype(inner_vals.dtype)[:, None]
        result = result + conv_taps[tap_count - 1 - lag_steps][None, :] * moved * allowed
    return result

def pair_combine(earlier, later):
    return (earlier[0] * later[0], later[0] * earlier[1] + later[1])

def block_scan(carried, pieces, a_neg):
    step_dt, write_in, read_out, drive_x, keep_on = pieces
    decay = jnp.exp(step_dt[:, None, :] * a_neg[None]) * keep_on[:, None, None]
    drive = write_in[:, :, None] * (step_dt * drive_x)[:, None, :]
    total_decay, total_drive = lax.associative_scan(pair_combine, (decay, drive), axis=0)
    states = total_decay * carried[None] + total_drive
    return (states[-1], lax.optimization_barrier(jnp.sum(states * read_out[:, :, None], axis=1)))

def selective_scan(step_dt, write_in, read_out, drive_x, keep_on, a_neg):
    blocks = step_dt.shape[0] // SCAN_BLOCK

    def to_blocks(array):
        return array.reshape((blocks, SCAN_BLOCK) + array.shape[1:])
    stepper = jax.checkpoint(lambda carried, pieces: block_scan(carried, pieces, a_neg))
    zero_state = jnp.zeros(a_neg.shape, step_dt.dtype)
    final_state, block_outs = lax.scan(stepper, zero_state, (to_blocks(step_dt), to_blocks(write_in), to_blocks(read_out), to_blocks(drive_x), to_blocks(keep_on)))
    return block_outs.reshape(step_dt.shape)

def mixer_tail(drive_x, write_in, read_out, step_pre, gate_half, decay_log, skip_gain, keep_on):
    step_dt = jax.nn.softplus(step_pre)
    a_neg = -jnp.exp(decay_log)
    scanned = selective_scan(step_dt, write_in, read_out, drive_x, keep_on, a_neg)
    return (scanned + skip_gain[None, :] * drive_x) * jax.nn.silu(gate_half)

def routing_tables(lens_row, route_row, experts, capacity, tok_count):
    position = jnp.arange(tok_count, dtype=jnp.int32)
    seq_ends = jnp.cumsum(lens_row, dtype=jnp.int32)
    seq_starts = lax.optimization_barrier(jnp.sum((position[:, None] >= seq_ends[None, :]).astype(jnp.int32) * lens_row[None, :], axis=1, dtype=jnp.int32))
    offset = position - seq_starts
    valid_mask = position < seq_ends[-1]
    route_hot = (route_row[:, None] == jnp.arange(experts, dtype=jnp.int32)[None, :]).astype(jnp.int32)
    live_hot = route_hot * valid_mask.astype(jnp.int32)[:, None]
    before = jnp.cumsum(live_hot, axis=0, dtype=jnp.int32) - live_hot
    rank_in = lax.optimization_barrier(jnp.sum(before * route_hot, axis=1, dtype=jnp.int32))
    kept_mask = valid_mask & (rank_in < capacity)
    slot_raw = route_row * capacity + rank_in
    target = jnp.where(kept_mask, slot_raw, experts * capacity)
    slot_index = jnp.full((experts * capacity,), tok_count, jnp.int32).at[target].set(position, mode='drop')
    slot_pick = jnp.where(kept_mask, slot_raw, 0).astype(jnp.int32)
    return (offset, valid_mask, route_hot, slot_index, slot_pick, kept_mask)

def row_forward(params, inputs, offset, keep_on, valid_f, route_hot, slot_index, slot_pick, kept_f):
    norm_gain, input_proj, conv_weight, conv_bias, select_proj, step_proj, step_bias, decay_log, skip_gain, output_proj, moe_gain, router_weight, up_weight, down_weight = params
    inner_width = step_proj.shape[1]
    step_rank = step_proj.shape[0]
    state_count = decay_log.shape[0]
    model_width = inputs.shape[1]
    normed = low(scale_norm(inputs, norm_gain))
    both_halves = low_back(matmul_high(normed, input_proj))
    mixed_in = both_halves[:, :inner_width]
    gate_half = both_halves[:, inner_width:]
    conv_low = low(jax.nn.silu(causal_conv(mixed_in, conv_weight, conv_bias, offset)))
    selected = low_back(matmul_high(conv_low, select_proj))
    step_low = low(selected[:, :step_rank])
    write_in = selected[:, step_rank:step_rank + state_count]
    read_out = selected[:, step_rank + state_count:]
    step_pre = low_back(matmul_high(step_low, step_proj)) + step_bias[None, :]
    gated_out = low(mixer_tail(conv_low, write_in, read_out, step_pre, gate_half, decay_log, skip_gain, keep_on))
    branch = low_back(matmul_high(gated_out, output_proj))
    hidden = inputs + branch
    moe_in = low(scale_norm(hidden, moe_gain))
    logits = low_back(matmul_high(moe_in, router_weight))
    gate_value = jax.nn.sigmoid(lax.optimization_barrier(jnp.sum(logits * route_hot, axis=1)))
    sent = low_back(moe_in)
    padded = jnp.concatenate([sent, jnp.zeros((1, model_width), sent.dtype)], axis=0)
    experts = up_weight.shape[0]
    slots = padded[slot_index].reshape(experts, -1, model_width)
    pre_act = low_back(jnp.einsum('ecd,efd->ecf', slots, up_weight, precision=lax.Precision.HIGHEST))
    act_low = low(jax.nn.gelu(pre_act, approximate=True))
    returned = low(low_back(jnp.einsum('ecf,efd->ecd', act_low, down_weight, precision=lax.Precision.HIGHEST)))
    picked = returned.reshape(-1, model_width)[slot_pick] * kept_f[:, None]
    return valid_f[:, None] * (hidden + gate_value[:, None] * picked)

def reference(tokens, cotangent, seq_lens, routes, norm_gain, input_proj, conv_weight, conv_bias, select_proj, step_proj, step_bias, decay_log, skip_gain, output_proj, moe_gain, router_weight, up_weight, down_weight):
    params = tuple((weight.astype(jnp.float32) for weight in (norm_gain, input_proj, conv_weight, conv_bias, select_proj, step_proj, step_bias, decay_log, skip_gain, output_proj, moe_gain, router_weight, up_weight, down_weight)))
    token_rows = tokens.astype(jnp.float32).reshape(SHARDS, TOK_DEV, D)
    cot_rows = cotangent.astype(jnp.float32).reshape(SHARDS, TOK_DEV, D)
    route_rows = routes.reshape(SHARDS, TOK_DEV)

    def one_row(totals, pieces):
        token_row, cot_row, lens_row, route_row = pieces
        offset, valid_mask, route_hot, slot_index, slot_pick, kept_mask = routing_tables(lens_row, route_row, EXPERTS, CAP, TOK_DEV)
        keep_on = (offset > 0).astype(jnp.float32)
        valid_f = valid_mask.astype(jnp.float32)
        kept_f = kept_mask.astype(jnp.float32)
        hot_f = route_hot.astype(jnp.float32)

        def forward(inputs, weights):
            return row_forward(weights, inputs, offset, keep_on, valid_f, hot_f, slot_index, slot_pick, kept_f)
        row_out, pullback = jax.vjp(forward, token_row, params)
        grad_row, grad_params = pullback(cot_row)
        totals = jax.tree.map(lambda left, right: left + right, totals, grad_params)
        return (totals, (row_out.astype(jnp.bfloat16), grad_row))
    zero_grads = jax.tree.map(jnp.zeros_like, params)
    totals, (out_rows, grad_rows) = lax.scan(one_row, zero_grads, (token_rows, cot_rows, seq_lens, route_rows))
    return (out_rows.reshape(TOKENS, D), grad_rows.reshape(TOKENS, D), totals[0], totals[1], totals[2], totals[3], totals[4], totals[5], totals[6], totals[7], totals[8], totals[9], totals[10], totals[11], totals[12], totals[13])
```

```python
import functools

import jax
import jax.numpy as jnp
import numpy as np
from jax import lax
from jax.experimental import pallas as pl
from jax.experimental.pallas import tpu as pltpu
from jax.sharding import Mesh
from jax.sharding import PartitionSpec as P

EPS = 1e-05
F32 = jnp.float32
BF16 = jnp.bfloat16
LANES = 128
LOG2E = 1.4426950408889634
LN2 = 0.6931471805599453
GELU_C = 0.7978845608028654
GELU_K = 0.044715
ALL = ("y", "c", "z", "x")
GROUP = ("y", "z", "x")
ROW_BIAS, ROW_STEP, ROW_SKIP, ROW_DECAY = 4, 5, 6, 8
NN = (((1,), (0,)), ((), ()))
NT = (((1,), (1,)), ((), ()))
TN = (((0,), (0,)), ((), ()))


def mm(left, right, dims=NN):
    return lax.dot_general(left, right, dims, preferred_element_type=F32)


def split_mm(left, right, dims=NN):
    high = left.astype(BF16)
    rest = left - high.astype(F32)
    mid = rest.astype(BF16)
    low = (rest - mid.astype(F32)).astype(BF16)
    return mm(high, right, dims) + (mm(mid, right, dims) + mm(low, right, dims))


def iota(shape, dim):
    return lax.broadcasted_iota(jnp.int32, shape, dim)


def sigmoid(v):
    return 1.0 / (1.0 + jnp.exp(-v))


def softplus(v):
    return jnp.maximum(v, 0.0) + jnp.log1p(jnp.exp(-jnp.abs(v)))


def positions(lens_ref, row, tok):
    pos = iota((tok, 1), 0)
    end = jnp.int32(0)
    start = jnp.zeros((tok, 1), jnp.int32)
    for j in range(lens_ref.shape[1]):
        length = lens_ref[row, j]
        end = end + length
        start = start + jnp.where(pos >= end, length, 0)
    return pos - start, pos < end


def both_offsets(lens_ref, tok):
    return jnp.concatenate([positions(lens_ref, row, tok)[0] for row in range(2)], axis=0)


def fold(parts):
    rows = iota((8, LANES), 0)
    step = 1
    while len(parts) > 1:
        first = (rows & step) == 0
        merged = []
        for k in range(0, len(parts), 2):
            a, b = parts[k], parts[k + 1]
            merged.append(jnp.where(first, a, b) + pltpu.roll(jnp.where(first, b, a), step, 0))
        parts = merged
        step *= 2
    return parts[0]


def call(kernel, outs, args, specs=None, scratch=(), name=None, cost=None, vmem=60):
    whole = pl.BlockSpec(memory_space=pltpu.VMEM)
    windowed = specs is not None and any(s is not None and s.block_shape is not None for s in specs)
    return pl.pallas_call(
        kernel,
        grid=(1,) if windowed else (),
        out_shape=[jax.ShapeDtypeStruct(s, d) for s, d in outs],
        in_specs=[whole] * len(args) if specs is None else [whole if s is None else s for s in specs],
        out_specs=[whole] * len(outs),
        scratch_shapes=list(scratch),
        name=name,
        cost_estimate=cost,
        compiler_params=pltpu.CompilerParams(vmem_limit_bytes=vmem << 20),
    )(*args)


SMEM = pl.BlockSpec(memory_space=pltpu.SMEM)


def perm_matrix(nat_ref):
    width = nat_ref.shape[1]
    return (iota((width, width), 0) == nat_ref[...]).astype(F32).astype(BF16)


def enter_kernel(lens, tok2, nat, g1, u_o, xin_o, xc_o, sel_o, small_o, dnat_o):
    rows, width = tok2.shape
    tok = rows // 2
    inner = xin_o.shape[1]
    at = inner
    perm = perm_matrix(nat)
    dnat = mm(g1[:, at : at + LANES], perm, (((0,), (1,)), ((), ())))
    dnat_o[...] = dnat[: dnat_o.shape[0]]
    vals = tok2[...].astype(F32)
    scale = lax.rsqrt(jnp.mean(vals * vals, axis=1, keepdims=True) + EPS)
    u = (vals * scale * dnat[0:1]).astype(BF16)
    u = mm(u, perm).astype(BF16)
    u_o[...] = u
    xin = mm(u, g1[:, :inner])
    xin_o[...] = xin
    small = jnp.transpose(g1[:, at + 2 * LANES : at + 3 * LANES].astype(F32))
    small_o[...] = small[: small_o.shape[0]]
    offset = both_offsets(lens, tok)
    conv = conv_of(xin, small, offset)
    xc = (conv * sigmoid(conv)).astype(BF16)
    xc_o[...] = xc
    sel_o[...] = mm(xc, g1[:, at + LANES : at + 2 * LANES])


def conv_of(xin, small, offset):
    conv = small[ROW_BIAS : ROW_BIAS + 1] + small[3:4] * xin
    for lag in range(1, 4):
        moved = pltpu.roll(xin, lag, 0)
        conv = conv + jnp.where(offset >= lag, small[3 - lag : 4 - lag] * moved, 0.0)
    return conv


def swap_halves(rows):
    half = rows.shape[0] // 2
    return jnp.concatenate([rows[half:], rows[:half]], axis=0)


def scan_kernel(
    rank, states, lens, sel_a, sel_b, u, xc, g1sel, g2, small,
    gated_o, ys_o, zg_o, step_o, sel_o, keep_o, mine_o, send_o, check_o,
    dm_s, dx_s, wr_s, rd_s, rate_s, h_s,
):
    rows, inner = ys_o.shape
    tok = rows // 2
    sel = sel_a[...] + swap_halves(sel_b[...])
    sel_o[...] = sel
    lane = iota((rows, LANES), 1)
    tail = LANES - rank
    q = jnp.where(lane >= tail, pltpu.roll(sel, tail, 1), 0.0).astype(BF16)
    step_pre = mm(q, g1sel[...], NT) + small[ROW_STEP : ROW_STEP + 1]
    step_o[...] = step_pre
    delta = softplus(step_pre)
    offset = both_offsets(lens, tok)
    xcf = xc[...].astype(F32)
    dm_s[...] = jnp.where(offset > 0, delta, 1e30)
    keep_o[...] = jnp.broadcast_to((offset > 0).astype(F32), keep_o.shape)
    dx_s[...] = delta * xcf
    for b in range(2):
        turned = jnp.transpose(sel[b * tok : (b + 1) * tok])
        wr_s[b] = turned[rank : rank + states]
        rd_s[b] = turned[rank + states : rank + 2 * states]
    rate_s[...] = jnp.exp(small[ROW_DECAY : ROW_DECAY + states]) * (-LOG2E)
    h_s[...] = jnp.zeros_like(h_s)
    half = states // 2

    def chunk(ci, carry):
        t0 = pl.multiple_of(ci * 8, 8)
        for b in range(2):
            at = pl.multiple_of(b * tok + t0, 8)
            wr8 = pltpu.roll(wr_s[b], tok - t0, 1)
            rd8 = pltpu.roll(rd_s[b], tok - t0, 1)
            wcol = [jnp.broadcast_to(wr8[:, j : j + 1], (states, LANES)) for j in range(8)]
            rcol = [jnp.broadcast_to(rd8[:, j : j + 1], (states, LANES)) for j in range(8)]
            for g in range(inner // LANES):
                lanes = slice(g * LANES, (g + 1) * LANES)
                h = h_s[b, :, lanes]
                check_o[ci * 2 + b, :, lanes] = h
                rate = rate_s[:, lanes]
                dm8 = dm_s[pl.ds(at, 8), lanes]
                dx8 = dx_s[pl.ds(at, 8), lanes]
                parts = []
                for j in range(8):
                    d = jnp.broadcast_to(dm8[j : j + 1], (states, LANES))
                    x = jnp.broadcast_to(dx8[j : j + 1], (states, LANES))
                    h = jnp.exp2(d * rate) * h + wcol[j] * x
                    p = rcol[j] * h
                    parts.append(p[:half] + p[half:])
                ys_o[pl.ds(at, 8), lanes] = fold(parts)
                h_s[b, :, lanes] = h
        return carry

    lax.fori_loop(0, tok // 8, chunk, 0)
    zg = mm(u[...], g2[:, :inner])
    zg_o[...] = zg
    gated = (ys_o[...] + small[ROW_SKIP : ROW_SKIP + 1] * xcf) * (zg * sigmoid(zg))
    gated = gated.astype(BF16)
    gated_o[...] = gated
    branch = mm(gated, g2[:, inner:])
    mine_o[...] = branch[:tok]
    send_o[...] = branch[tok:]


def route_tables(lens, routes, experts, capacity, tok):
    _, valid = positions(lens, 0, tok)
    valid_f = valid.astype(F32)
    width = max(LANES, experts)
    hot = (routes[...] == iota((tok, width), 1)).astype(F32)
    live = hot * valid_f
    earlier = (iota((tok, tok), 1) < iota((tok, tok), 0)).astype(F32).astype(BF16)
    before = mm(earlier, live.astype(BF16))
    rank = jnp.sum(before * hot, axis=1, keepdims=True).astype(jnp.int32)
    kept = valid & (rank < capacity)
    return valid_f, hot, rank, kept


def slot_hot(k, routes, rank, kept, capacity, tok):
    inside = kept & (routes[...] == k)
    return (inside & (rank == iota((tok, capacity), 1))).astype(F32).astype(BF16)


def moe_enter_kernel(experts, capacity, lens, tok, cot, routes, mine, got, dnat, disp_o, hidden_o, gate_o):
    rows, width = tok.shape
    hidden = tok[...].astype(F32) + (mine[...] + got[...])
    hidden_o[...] = hidden
    scale = lax.rsqrt(jnp.mean(hidden * hidden, axis=1, keepdims=True) + EPS)
    mv = (hidden * scale * dnat[1:2]).astype(BF16)
    logits = mm(mv, dnat[...].astype(BF16), NT)
    hot = (routes[...] + 2 == iota(logits.shape, 1)).astype(F32)
    gate = sigmoid(jnp.sum(logits * hot, axis=1, keepdims=True))
    gate_o[...] = jnp.broadcast_to(gate, gate_o.shape)
    valid_f, _, rank, kept = route_tables(lens, routes, experts, capacity, rows)
    back = (cot[...].astype(F32) * valid_f * (gate * kept.astype(F32))).astype(BF16)
    both = jnp.concatenate([mv, back], axis=1)
    for k in range(experts):
        disp_o[k] = mm(slot_hot(k, routes, rank, kept, capacity, rows), both, TN).astype(BF16)


def expert_kernel(width, own, peer, up, down, out_own, out_peer, up_g, down_g, rows_s, acc_s):
    half = own.shape[0]
    total = rows_s.shape[0]
    rows_s[:half] = own[...]
    rows_s[half:] = peer[...]
    hidden = up.shape[1]
    part = 256
    for f in range(0, hidden, part):
        x = rows_s[:, :width]
        g = rows_s[:, width:]
        pre = mm(x, up[0, f : f + part], NT)
        g_act = mm(g, down[0, f : f + part], NT)
        sq = pre * pre
        th = jnp.tanh(GELU_C * (pre + GELU_K * sq * pre))
        act = (0.5 * pre * (1.0 + th)).astype(BF16)
        slope = 0.5 * (1.0 + th) + 0.5 * pre * (1.0 - th * th) * (GELU_C * (1.0 + 3.0 * GELU_K * sq))
        g_pre = (g_act * slope).astype(BF16)
        down_g[0, f : f + part] = mm(act, g, TN)
        up_g[0, f : f + part] = mm(g_pre, x, TN)
        e_part = mm(act, down[0, f : f + part])
        i_part = mm(g_pre, up[0, f : f + part])
        if f == 0:
            acc_s[:, :width] = e_part
            acc_s[:, width:] = i_part
        else:
            acc_s[:, :width] += e_part
            acc_s[:, width:] += i_part
    out_own[...] = acc_s[:half]
    out_peer[...] = acc_s[half:].astype(BF16)


def moe_leave_kernel(
    experts, capacity, lens, routes, cot, hidden, gate_in, dnat, back,
    out_o, ghid_o, gbr_o, dgrad_o,
):
    rows, width = hidden.shape
    valid_f, _, rank, kept = route_tables(lens, routes, experts, capacity, rows)
    kept_f = kept.astype(F32)
    gate = gate_in[:, 0:1]
    picked = jnp.zeros((rows, 2 * width), F32)
    for k in range(experts):
        picked = picked + mm(slot_hot(k, routes, rank, kept, capacity, rows), back[k])
    ex_out = picked[:, :width]
    sent = picked[:, width:]
    hid = hidden[...]
    out_o[...] = (valid_f * (hid + gate * ex_out)).astype(BF16)
    gy = cot[...].astype(F32) * valid_f
    g_gate = jnp.sum(gy * ex_out, axis=1, keepdims=True)
    chosen = g_gate * gate * (1.0 - gate)
    small_rows = dnat.shape[0]
    hot = (routes[...] + 2 == iota((rows, small_rows), 1)).astype(F32)
    g_logit = (chosen * hot).astype(BF16)
    g_mv = mm(g_logit, dnat[...].astype(BF16)) + sent
    scale = lax.rsqrt(jnp.mean(hid * hid, axis=1, keepdims=True) + EPS)
    hat = hid * scale
    gain = dnat[1:2]
    mv = (hat * gain).astype(BF16)
    router_g = mm(g_logit, mv, TN)
    gain_g = jnp.sum(g_mv * hat, axis=0, keepdims=True)
    dgrad_o[...] = jnp.where(iota(dgrad_o.shape, 0) == 1, gain_g, router_g)
    gg = g_mv * gain
    mean = jnp.sum(gg * hat, axis=1, keepdims=True) * (1.0 / width)
    ghid = gy + scale * (gg - hat * mean)
    ghid_o[...] = ghid
    gbr_o[...] = ghid.astype(BF16)


def scan_back_kernel(
    rank, states, gbr_a, gbr_b, g2, gated, xc, ys, zg, step_pre, sel, keep, small, g1sel, check,
    gsel_o, gxcs_o, gzg_o, gsr_o, q_o, smallg_o, outg_o,
    dm_s, dx_s, gy_s, gdx_s, gdl_s, wr_s, rd_s, gwr_s, grd_s, rate_s, lam_s, ga_s,
):
    rows, inner = ys.shape
    tok = rows // 2
    half = states // 2
    gbr = jnp.concatenate([gbr_a[...], gbr_b[...]], axis=0)
    outg_o[...] = mm(gated[...], gbr, TN).astype(BF16)
    g_gated = mm(gbr, g2[:, inner:], NT)
    xcf = xc[...].astype(F32)
    skip = small[ROW_SKIP : ROW_SKIP + 1]
    sig = sigmoid(zg[...])
    gy = g_gated * (zg[...] * sig)
    gy_s[...] = gy
    gzg_o[...] = (g_gated * (ys[...] + skip * xcf) * (sig * (1.0 + zg[...] * (1.0 - sig)))).astype(BF16)
    delta = softplus(step_pre[...])
    dm_s[...] = jnp.where(keep[:, 0:1] > 0.0, delta, 1e30)
    dx_s[...] = delta * xcf
    for b in range(2):
        turned = jnp.transpose(sel[b * tok : (b + 1) * tok])
        wr_s[b] = turned[rank : rank + states]
        rd_s[b] = turned[rank + states : rank + 2 * states]
    rate_s[...] = jnp.exp(small[ROW_DECAY : ROW_DECAY + states]) * (-LOG2E)
    lam_s[...] = jnp.zeros_like(lam_s)
    ga_s[...] = jnp.zeros_like(ga_s)
    gwr_s[...] = jnp.zeros_like(gwr_s)
    grd_s[...] = jnp.zeros_like(grd_s)
    shape = (states, LANES)

    def chunk(i, carry):
        ci = tok // 8 - 1 - i
        t0 = pl.multiple_of(ci * 8, 8)
        for b in range(2):
            at = pl.multiple_of(b * tok + t0, 8)
            wr8 = pltpu.roll(wr_s[b], tok - t0, 1)
            rd8 = pltpu.roll(rd_s[b], tok - t0, 1)
            wcol = [jnp.broadcast_to(wr8[:, j : j + 1], shape) for j in range(8)]
            rcol = [jnp.broadcast_to(rd8[:, j : j + 1], shape) for j in range(8)]
            grd = [jnp.zeros(shape, F32)] * 8
            gwr = [jnp.zeros(shape, F32)] * 8
            for g in range(inner // LANES):
                lanes = slice(g * LANES, (g + 1) * LANES)
                h = check[ci * 2 + b, :, lanes]
                rate = rate_s[:, lanes]
                dm8 = dm_s[pl.ds(at, 8), lanes]
                dx8 = dx_s[pl.ds(at, 8), lanes]
                gy8 = gy_s[pl.ds(at, 8), lanes]
                decays, olds = [], []
                for j in range(8):
                    d = jnp.broadcast_to(dm8[j : j + 1], shape)
                    x = jnp.broadcast_to(dx8[j : j + 1], shape)
                    a = jnp.exp2(d * rate)
                    old = a * h
                    h = old + wcol[j] * x
                    grd[j] = grd[j] + h * jnp.broadcast_to(gy8[j : j + 1], shape)
                    decays.append(a)
                    olds.append(old)
                lam_in = lam_s[b, :, lanes]
                ga = ga_s[:, lanes]
                to_dx, to_dl = [None] * 8, [None] * 8
                for j in range(7, -1, -1):
                    lam = rcol[j] * jnp.broadcast_to(gy8[j : j + 1], shape) + lam_in
                    lam_in = decays[j] * lam
                    w = lam * olds[j]
                    ga = ga + w * jnp.broadcast_to(dm8[j : j + 1], shape)
                    p = lam * wcol[j]
                    to_dx[j] = p[:half] + p[half:]
                    p = w * rate
                    to_dl[j] = p[:half] + p[half:]
                    gwr[j] = gwr[j] + lam * jnp.broadcast_to(dx8[j : j + 1], shape)
                lam_s[b, :, lanes] = lam_in
                ga_s[:, lanes] = ga
                gdx_s[pl.ds(at, 8), lanes] = fold(to_dx)
                gdl_s[pl.ds(at, 8), lanes] = fold(to_dl)
            lane = iota(shape, 1)
            all_wr, all_rd = gwr_s[b], grd_s[b]
            for j in range(8):
                here = lane == t0 + j
                all_wr = jnp.where(here, jnp.sum(gwr[j], axis=1, keepdims=True), all_wr)
                all_rd = jnp.where(here, jnp.sum(grd[j], axis=1, keepdims=True), all_rd)
            gwr_s[b] = all_wr
            grd_s[b] = all_rd
        return carry

    lax.fori_loop(0, tok // 8, chunk, 0)
    delta = softplus(step_pre[...])
    gdx = gdx_s[...]
    xcf = xc[...].astype(F32)
    gy = gy_s[...]
    gxcs_o[...] = gy * skip + gdx * delta
    g_step = (gdx * xcf + LN2 * gdl_s[...]) * sigmoid(step_pre[...])
    gsr = g_step.astype(BF16)
    gsr_o[...] = gsr
    lane = iota((rows, LANES), 1)
    tail = LANES - rank
    q_o[...] = jnp.where(lane >= tail, pltpu.roll(sel[...], tail, 1), 0.0).astype(BF16)
    back = jnp.where(lane >= tail, mm(gsr, g1sel[...]), 0.0)
    back = pltpu.roll(back, rank, 1)
    zeros_top = jnp.zeros((rank, tok), F32)
    zeros_end = jnp.zeros((LANES - rank - 2 * states, tok), F32)
    for b in range(2):
        stack = jnp.concatenate([zeros_top, gwr_s[b], grd_s[b], zeros_end], axis=0)
        span = slice(b * tok, (b + 1) * tok)
        gsel_o[span] = back[span] + jnp.transpose(stack)
    smallg_o[0:ROW_STEP] = jnp.zeros((ROW_STEP, inner), F32)
    smallg_o[ROW_STEP : ROW_STEP + 1] = jnp.sum(g_step, axis=0, keepdims=True)
    smallg_o[ROW_SKIP : ROW_SKIP + 1] = jnp.sum(gy * xcf, axis=0, keepdims=True)
    smallg_o[ROW_SKIP + 1 : ROW_DECAY] = jnp.zeros((ROW_DECAY - ROW_SKIP - 1, inner), F32)
    smallg_o[ROW_DECAY : ROW_DECAY + states] = ga_s[...] * rate_s[...] * LN2
    rest = smallg_o.shape[0] - ROW_DECAY - states
    if rest:
        smallg_o[ROW_DECAY + states :] = jnp.zeros((rest, inner), F32)


def leave_kernel(
    lens, nat, gsel_a, gsel_b, gxcs, gzg, gsr, q, smallg, xin, xc, u, small, g1, g2z, tok2, dnat, dgrad,
    mine_o, send_o, gx_o, gz_o, gsmall_o,
):
    rows, inner = xin.shape
    tok = rows // 2
    width = tok2.shape[1]
    perm = perm_matrix(nat)
    g_sel = (gsel_a[...] + swap_halves(gsel_b[...])).astype(BF16)
    selblk = g1[:, inner + LANES : inner + 2 * LANES]
    block = mm(xc[...], g_sel, TN) + mm(gsr[...], q[...], TN)
    gsmall_o[:, LANES : 2 * LANES] = block.astype(BF16)
    g_xc = mm(g_sel, selblk, NT) + gxcs[...]
    offset = both_offsets(lens, tok)
    x = xin[...]
    sm = small[...]
    conv = conv_of(x, sm, offset)
    sig = sigmoid(conv)
    g_conv = g_xc * (sig * (1.0 + conv * (1.0 - sig)))
    g_xin = sm[3:4] * g_conv
    taps = [None, None, None, jnp.sum(g_conv * x, axis=0, keepdims=True)]
    for lag in range(1, 4):
        held = jnp.where(offset >= lag, g_conv, 0.0)
        g_xin = g_xin + sm[3 - lag : 4 - lag] * pltpu.roll(held, rows - lag, 0)
        taps[3 - lag] = jnp.sum(held * pltpu.roll(x, lag, 0), axis=0, keepdims=True)
    g_bias = jnp.sum(g_conv, axis=0, keepdims=True)
    top = jnp.concatenate(taps + [g_bias, jnp.zeros((3, inner), F32)], axis=0)
    full = jnp.concatenate([smallg[0:8] + top, smallg[8:]], axis=0)
    pad = jnp.zeros((LANES - full.shape[0], inner), F32)
    gsmall_o[:, 2 * LANES : 3 * LANES] = jnp.transpose(jnp.concatenate([full, pad], axis=0)).astype(BF16)
    g_xin = g_xin.astype(BF16)
    gx_o[...] = mm(u[...], g_xin, TN).astype(BF16)
    gz_o[...] = mm(u[...], gzg[...], TN).astype(BF16)
    gn = mm(g_xin, g1[:, :inner], NT) + mm(gzg[...], g2z[...], NT)
    gn = split_mm(gn, perm, NT)
    vals = tok2[...].astype(F32)
    scale = lax.rsqrt(jnp.mean(vals * vals, axis=1, keepdims=True) + EPS)
    gain_g = jnp.sum(gn * (vals * scale), axis=0, keepdims=True)
    dg = jnp.where(iota(dgrad.shape, 0) == 0, gain_g, dgrad[...])
    dg = split_mm(dg, perm)
    dpad = jnp.zeros((LANES - dg.shape[0], width), F32)
    gsmall_o[:, :LANES] = jnp.transpose(jnp.concatenate([dg, dpad], axis=0)).astype(BF16)
    mine_o[...] = gn[:tok]
    send_o[...] = gn[tok:]


def final_kernel(tok, mine, got, ghid, dnat, out_o):
    width = tok.shape[1]
    vals = tok[...].astype(F32)
    scale = lax.rsqrt(jnp.mean(vals * vals, axis=1, keepdims=True) + EPS)
    hat = vals * scale
    gg = (mine[...] + got[...]) * dnat[0:1]
    mean = jnp.sum(gg * hat, axis=1, keepdims=True) * (1.0 / width)
    out_o[...] = ghid[...] + scale * (gg - hat * mean)


def swap(values, axis):
    return lax.ppermute(values, axis, [(0, 1), (1, 0)])


def gather_group(piece, count):
    many = jnp.broadcast_to(piece[None], (count,) + piece.shape)
    many = lax.all_to_all(many, GROUP, split_axis=0, concat_axis=0, tiled=True)
    return many.reshape((count * piece.shape[0],) + piece.shape[1:])


def reduce_group(array, count):
    parts = array.reshape((count, array.shape[0] // count) + array.shape[1:])
    parts = lax.all_to_all(parts, GROUP, split_axis=0, concat_axis=0, tiled=True)
    return jnp.sum(parts.astype(F32), axis=0)


def body(
    sizes,
    tokens,
    cotangent,
    seq_lens,
    routes,
    norm_gain,
    input_proj,
    conv_weight,
    conv_bias,
    select_proj,
    step_proj,
    step_bias,
    decay_log,
    skip_gain,
    output_proj,
    moe_gain,
    router_weight,
    up_weight,
    down_weight,
):
    ny, nz, nx = sizes
    nf = nz * nx
    ng = ny * nf
    tok, width = tokens.shape
    rank, er = step_proj.shape
    states = decay_log.shape[0]
    experts = router_weight.shape[1]
    capacity = 5 * tok // (4 * experts)
    dr = norm_gain.shape[0]
    inner = ng * er
    core = lax.axis_index("c")
    rows = 2 * tok
    small_n = -(-(ROW_DECAY + states) // 8) * 8
    dn = -(-(2 + experts) // 8) * 8

    nat = np.arange(width).reshape(ny, 2, nf, dr).transpose(0, 2, 1, 3).reshape(1, width)
    nat = jnp.asarray(nat, jnp.int32)

    tok_peer = swap(tokens, "c")
    lens2 = jnp.concatenate([seq_lens, swap(seq_lens, "c")], axis=0)
    tok2 = jnp.concatenate([tokens, tok_peer], axis=0)

    cols = input_proj.reshape(dr, 2, ny, 2, nf * er)
    mine_w = lax.dynamic_index_in_dim(cols, core, 3, keepdims=False).reshape(dr, 2 * inner)
    other_w = lax.dynamic_index_in_dim(cols, 1 - core, 3, keepdims=False).reshape(dr, 2 * inner)
    dsmall = jnp.concatenate([norm_gain[:, None], moe_gain[:, None], router_weight], axis=1)
    dsmall = jnp.pad(dsmall, ((0, 0), (0, LANES - dsmall.shape[1])))
    got = swap(jnp.concatenate([other_w, dsmall], axis=1), "c")
    mine_a = jnp.concatenate([mine_w, dsmall], axis=1)
    first = jnp.where(core == 0, mine_a, got)
    second = jnp.where(core == 0, got, mine_a)
    pack_a = jnp.concatenate([first, second], axis=0)
    small = jnp.concatenate(
        [
            conv_weight.T,
            conv_bias[:, None],
            step_bias[:, None],
            skip_gain[:, None],
            jnp.zeros((er, 1), BF16),
            decay_log.T,
        ],
        axis=1,
    )
    small = jnp.pad(small, ((0, 0), (0, LANES - small.shape[1])))
    gap = jnp.zeros((er, LANES - rank - select_proj.shape[1]), BF16)
    pack_b = jnp.concatenate([select_proj, gap, step_proj.T, small], axis=1)
    group1 = jnp.concatenate([pack_a[:, :inner], pack_a[:, 2 * inner :], pack_b], axis=1)
    group2 = jnp.concatenate([pack_a[:, inner : 2 * inner], output_proj], axis=1)
    g1 = gather_group(group1, ng)
    g2 = gather_group(group2, ng)

    u, xin, xc, selp, small_t, dnat = call(
        enter_kernel,
        [((rows, width), BF16), ((rows, inner), F32), ((rows, inner), BF16), ((rows, LANES), F32), ((small_n, inner), F32), ((dn, width), F32)],
        [lens2, tok2, nat, g1],
        [SMEM, None, None, None],
        name="enter",
    )
    selq = swap(selp, "c")
    g1sel_spec = pl.BlockSpec((inner, LANES), lambda i: (0, inner // LANES + 1))
    chunks = tok // 8
    gated, ys, zg, step_pre, sel, keep, br_mine, br_send, check = call(
        functools.partial(scan_kernel, rank, states),
        [((rows, inner), BF16), ((rows, inner), F32), ((rows, inner), F32), ((rows, inner), F32), ((rows, LANES), F32), ((rows, LANES), F32), ((tok, width), F32), ((tok, width), F32), ((2 * chunks, states, inner), F32)],
        [lens2, selp, selq, u, xc, g1, g2, small_t],
        [SMEM, None, None, None, None, g1sel_spec, None, None],
        scratch=[pltpu.VMEM((rows, inner), F32), pltpu.VMEM((rows, inner), F32), pltpu.VMEM((2, states, tok), F32), pltpu.VMEM((2, states, tok), F32), pltpu.VMEM((states, inner), F32), pltpu.VMEM((2, states, inner), F32)],
        name="scan",
    )
    br_got = swap(br_send, "c")
    disp, hidden, gate = call(
        functools.partial(moe_enter_kernel, experts, capacity),
        [((experts, capacity, 2 * width), BF16), ((tok, width), F32), ((tok, LANES), F32)],
        [seq_lens, tokens, cotangent, routes, br_mine, br_got, dnat],
        [SMEM] + [None] * 6,
        name="moe_enter",
    )
    line = lax.all_to_all(disp, ("z", "x"), split_axis=0, concat_axis=0, tiled=True)
    line = line.reshape(nf * capacity, 2 * width)
    if ny > 1:
        line = jnp.concatenate([line, swap(line, "y")], axis=0)
    peer = swap(line, "c")
    total = 2 * line.shape[0]
    hid = up_weight.shape[1]
    out_own, out_peer, up_grad, down_grad = call(
        functools.partial(expert_kernel, width),
        [((total // 2, 2 * width), F32), ((total // 2, 2 * width), BF16), ((1, hid, width), F32), ((1, hid, width), F32)],
        [line, peer, up_weight, down_weight],
        scratch=[pltpu.VMEM((total, 2 * width), BF16), pltpu.VMEM((total, 2 * width), F32)],
        name="expert",
    )
    summed = out_own + swap(out_peer, "c").astype(F32)
    if ny > 1:
        cut = nf * capacity
        summed = summed[:cut] + swap(summed[cut:].astype(BF16), "y").astype(F32)
    back = lax.all_to_all(
        summed.astype(BF16).reshape(nf, capacity, 2 * width), ("z", "x"), split_axis=0, concat_axis=0, tiled=True
    )
    result, ghid, gbr, dgrad = call(
        functools.partial(moe_leave_kernel, experts, capacity),
        [((tok, width), BF16), ((tok, width), F32), ((tok, width), BF16), ((dn, width), F32)],
        [seq_lens, routes, cotangent, hidden, gate, dnat, back],
        [SMEM] + [None] * 6,
        name="moe_leave",
    )
    gbr_got = swap(gbr, "c")
    gsel, gxcs, gzg, gsr, q, smallg, outg = call(
        functools.partial(scan_back_kernel, rank, states),
        [((rows, LANES), F32), ((rows, inner), F32), ((rows, inner), BF16), ((rows, inner), BF16), ((rows, LANES), BF16), ((small_n, inner), F32), ((inner, width), BF16)],
        [gbr, gbr_got, g2, gated, xc, ys, zg, step_pre, sel, keep, small_t, g1, check],
        [None] * 11 + [g1sel_spec, None],
        scratch=[pltpu.VMEM((rows, inner), F32)] * 5 + [pltpu.VMEM((2, states, tok), F32)] * 4 + [pltpu.VMEM((states, inner), F32), pltpu.VMEM((2, states, inner), F32), pltpu.VMEM((states, inner), F32)],
        name="scan_back",
    )
    gsel_got = swap(gsel, "c")
    g2z_spec = pl.BlockSpec((inner, inner), lambda i: (0, 0))
    gn_mine, gn_send, gx, gz, gsmall = call(
        leave_kernel,
        [((tok, width), F32), ((tok, width), F32), ((width, inner), BF16), ((width, inner), BF16), ((inner, 3 * LANES), BF16)],
        [lens2, nat, gsel, gsel_got, gxcs, gzg, gsr, q, smallg, xin, xc, u, small_t, g1, g2, tok2, dnat, dgrad],
        [SMEM] + [None] * 13 + [g2z_spec, None, None, None],
        name="leave",
    )
    gn_got = swap(gn_send, "c")
    (input_grad,) = call(
        final_kernel, [((tok, width), F32)], [tokens, gn_mine, gn_got, ghid, dnat], name="final"
    )
    packed = jnp.concatenate([gx, gz, gsmall, outg], axis=1)
    share = reduce_group(packed, ng)
    wide = jnp.concatenate([share[:, : 2 * inner], share[:, 2 * inner : 2 * inner + LANES]], axis=1)
    keep_rows = lax.dynamic_slice_in_dim(wide, core * dr, dr, 0)
    send_rows = lax.dynamic_slice_in_dim(wide, (1 - core) * dr, dr, 0)
    got_rows = swap(send_rows, "c")
    own_cols = keep_rows[:, : 2 * inner].reshape(dr, 2, ny, 1, nf * er)
    got_cols = got_rows[:, : 2 * inner].reshape(dr, 2, ny, 1, nf * er)
    lo = jnp.where(core == 0, own_cols, got_cols)
    hi = jnp.where(core == 0, got_cols, own_cols)
    in_grad = jnp.concatenate([lo, hi], axis=3).reshape(dr, 4 * inner)
    dsum = keep_rows[:, 2 * inner :] + got_rows[:, 2 * inner :]
    at = 2 * inner + LANES
    sel_n = select_proj.shape[1]
    select_grad = share[:, at : at + sel_n]
    step_grad = share[:, at + LANES - rank : at + LANES].T
    ch = share[:, at + LANES : at + 2 * LANES]
    out_grad = share[:, at + 2 * LANES :]
    return (
        result,
        input_grad,
        dsum[:, 0],
        in_grad,
        ch[:, 0:4].T,
        ch[:, ROW_BIAS],
        select_grad,
        step_grad,
        ch[:, ROW_STEP],
        ch[:, ROW_DECAY : ROW_DECAY + states].T,
        ch[:, ROW_SKIP],
        out_grad,
        dsum[:, 1],
        dsum[:, 2 : 2 + experts],
        up_grad,
        down_grad,
    )


def solution(mesh):
    dp, fsdp = mesh.shape["dp"], mesh.shape["fsdp"]
    ny, nx = dp // 2, 2
    nz = fsdp // nx
    fine = Mesh(mesh.devices.reshape(ny, 2, nz, nx), ALL)
    tok = P(ALL, None)
    vec = P(ALL)
    col = P(None, ALL)
    exp = P(("z", "x"), ("y", "c"), None)
    in_specs = (tok, tok, tok, tok, vec, tok, col, vec, tok, col, vec, col, vec, tok, vec, tok, exp, exp)
    out_specs = (tok, tok, vec, tok, col, vec, tok, col, vec, col, vec, tok, vec, tok, exp, exp)
    return jax.shard_map(
        functools.partial(body, (ny, nz, nx)), mesh=fine, in_specs=in_specs, out_specs=out_specs, check_vma=False
    )
```

```python
import functools

import jax
import jax.numpy as jnp
import numpy as np
from jax import lax
from jax.experimental import pallas as pl
from jax.experimental.pallas import tpu as pltpu
from jax.sharding import Mesh
from jax.sharding import PartitionSpec as P

EPS = 1e-05
F32 = jnp.float32
BF16 = jnp.bfloat16
LANES = 128
LOG2E = 1.4426950408889634
LN2 = 0.6931471805599453
GELU_C = 0.7978845608028654
GELU_K = 0.044715
ALL = ("y", "c", "z", "x")
GROUP = ("y", "z", "x")
ROW_BIAS, ROW_STEP, ROW_SKIP, ROW_DECAY = 4, 5, 6, 8
ROW_FEATURE = 64
NN = (((1,), (0,)), ((), ()))
NT = (((1,), (1,)), ((), ()))
TN = (((0,), (0,)), ((), ()))


def mm(left, right, dims=NN):
    return lax.dot_general(left, right, dims, preferred_element_type=F32)


def split_mm(left, right, dims=NN):
    high = left.astype(BF16)
    rest = left - high.astype(F32)
    mid = rest.astype(BF16)
    low = (rest - mid.astype(F32)).astype(BF16)
    return mm(high, right, dims) + (mm(mid, right, dims) + mm(low, right, dims))


def iota(shape, dim):
    return lax.broadcasted_iota(jnp.int32, shape, dim)


def sigmoid(v):
    return 1.0 / (1.0 + jnp.exp(-v))


def softplus(v):
    return jnp.maximum(v, 0.0) + jnp.log1p(jnp.exp(-jnp.abs(v)))


def positions(lens_ref, row, tok):
    pos = iota((tok, 1), 0)
    end = jnp.int32(0)
    start = jnp.zeros((tok, 1), jnp.int32)
    for j in range(lens_ref.shape[1]):
        length = lens_ref[row, j]
        end = end + length
        start = start + jnp.where(pos >= end, length, 0)
    return pos - start, pos < end


def both_offsets(lens_ref, tok):
    return jnp.concatenate([positions(lens_ref, row, tok)[0] for row in range(2)], axis=0)


def fold(parts):
    rows = iota((8, LANES), 0)
    step = 1
    while len(parts) > 1:
        first = (rows & step) == 0
        merged = []
        for k in range(0, len(parts), 2):
            a, b = parts[k], parts[k + 1]
            merged.append(jnp.where(first, a, b) + pltpu.roll(jnp.where(first, b, a), step, 0))
        parts = merged
        step *= 2
    return parts[0]


def call(kernel, outs, args, specs=None, scratch=(), name=None, us=5, vmem=60):
    whole = pl.BlockSpec(memory_space=pltpu.VMEM)
    specs = [None] * len(args) if specs is None else specs
    windowed = any(s is not None and s.block_shape is not None for s in specs)
    return pl.pallas_call(
        kernel,
        grid=(1,) if windowed else (),
        out_shape=[jax.ShapeDtypeStruct(o[0], o[1]) for o in outs],
        in_specs=[whole if s is None else s for s in specs],
        out_specs=[o[2] if len(o) > 2 else whole for o in outs],
        scratch_shapes=list(scratch),
        name=name,
        cost_estimate=pl.CostEstimate(flops=us * 1000000000, bytes_accessed=us * 3000000, transcendentals=0),
        compiler_params=pltpu.CompilerParams(vmem_limit_bytes=vmem << 20),
    )(*args)


SMEM = pl.BlockSpec(memory_space=pltpu.SMEM)
HBM = pl.BlockSpec(memory_space=pl.ANY)


def perm_matrix(idx, nat_ref):
    width = nat_ref.shape[1]
    nat = jnp.where(idx[3] == 0, nat_ref[0:1], nat_ref[1:2])
    return (iota((width, width), 0) == nat).astype(F32).astype(BF16)


class Plan:
    def __init__(self, ny, nz, nx, piece):
        self.ny, self.nz, self.nx, self.piece = ny, nz, nx, piece
        self.count = ny * nz * nx
        self.fast = (ny, nz, nx) == (2, 4, 2) and piece % 16 == 0

    def place(self, idx, yr, zr, xr):
        y = jnp.bitwise_xor(idx[0], yr)
        x = jnp.bitwise_xor(idx[2], xr)
        z = lax.rem(idx[1] - zr + self.nz, self.nz)
        return pl.multiple_of(((y * self.nz + z) * self.nx + x) * self.piece, self.piece)

    def gather(self, piece):
        if not self.fast:
            return [lax.all_gather(piece, GROUP, axis=0, tiled=True)]
        rots = [lax.ppermute(piece, "z", [(i, (i + k) % 4) for i in range(4)]) for k in (1, 2, 3)]
        line = jnp.concatenate([piece] + rots, axis=0)
        by_x, by_y = swap(line, "x"), swap(line, "y")
        half = 2 * self.piece
        return [line, by_x, by_y, swap(by_x[:half], "y"), swap(by_y[half:], "x")]

    def pieces(self):
        n, out = self.piece, []
        for z in range(4):
            out.append((0, z * n, 0, z, 0))
            out.append((1, z * n, 0, z, 1))
            out.append((2, z * n, 1, z, 0))
            out.append((3 + z // 2, z % 2 * n, 1, z, 1))
        return out

    def n_gathered(self):
        return 5 if self.fast else 1

    def fetch(self, idx, refs, dst, sem):
        if not self.fast:
            copies = [pltpu.make_async_copy(refs[0], dst, sem.at[0])]
        else:
            copies = []
            for k, (r, row, yr, zr, xr) in enumerate(self.pieces()):
                to = dst.at[pl.ds(self.place(idx, yr, zr, xr), self.piece)]
                copies.append(pltpu.make_async_copy(refs[r].at[pl.ds(row, self.piece)], to, sem.at[k]))
        for copy in copies:
            copy.start()
        return copies

    def shared_outs(self, width):
        if not self.fast:
            return [((self.count * self.piece, width), BF16, HBM)]
        return [((8 * self.piece, width // 2), BF16, HBM)] * 4

    def n_shared(self):
        return 4 if self.fast else 1

    def emit(self, idx, src, refs, sem):
        if not self.fast:
            copies = [pltpu.make_async_copy(src, refs[0], sem.at[0])]
        else:
            copies, n, half = [], self.piece, src.shape[1] // 2
            for zr in range(4):
                for yr in range(2):
                    for xr in range(2):
                        at = self.place(idx, yr, zr, xr)
                        for lanes, ref, row in (
                            (0, refs[1 - xr], yr * 4 + zr),
                            (half, refs[3 - yr], xr * 4 + zr),
                        ):
                            copies.append(
                                pltpu.make_async_copy(
                                    src.at[pl.ds(at, n), pl.ds(lanes, half)],
                                    ref.at[pl.ds(row * n, n)],
                                    sem.at[len(copies)],
                                )
                            )
        for copy in copies:
            copy.start()
        return copies

    def reduce(self, shared, tag):
        if not self.fast:
            parts = shared[0].reshape(self.count, self.piece, -1)
            parts = lax.all_to_all(parts, GROUP, split_axis=0, concat_axis=0, tiled=True)
            return [parts.astype(F32).sum(axis=0)]
        a_send, a_keep, b_send, b_keep = shared
        n, half = self.piece, a_send.shape[1]
        a_got, b_got = swap(a_send, "x"), swap(b_send, "y")
        shape = ((4 * n, half), BF16)
        a_send, a_keep, b_send, b_keep = call(
            add_kernel, [shape] * 4, [a_keep, a_got, b_keep, b_got], name="add1_" + tag, us=2
        )
        a_got, b_got = swap(a_send, "y"), swap(b_send, "x")
        parts = call(
            line_kernel, [((n, 2 * half), BF16)] * 4, [a_keep, a_got, b_keep, b_got], name="add2_" + tag, us=1
        )
        rots = [lax.ppermute(parts[k], "z", [(i, (i - k) % 4) for i in range(4)]) for k in (1, 2, 3)]
        return [parts[0]] + rots


def add_kernel(a, a_in, b, b_in, a_send, a_keep, b_send, b_keep):
    cut = a_send.shape[0]
    for one, two, send, keep in ((a, a_in, a_send, a_keep), (b, b_in, b_send, b_keep)):
        send[...] = (one[cut:].astype(F32) + two[cut:].astype(F32)).astype(BF16)
        keep[...] = (one[:cut].astype(F32) + two[:cut].astype(F32)).astype(BF16)


def line_kernel(a, a_in, b, b_in, *outs):
    n, half = outs[0].shape[0], a.shape[1]
    for k, out in enumerate(outs):
        span = slice(k * n, (k + 1) * n)
        out[:, :half] = (a[span].astype(F32) + a_in[span].astype(F32)).astype(BF16)
        out[:, half:] = (b[span].astype(F32) + b_in[span].astype(F32)).astype(BF16)


def pack_kernel(
    span, idx, in_proj, norm, moe, router, taps, cbias, select, step, sbias, decay, skip,
    mine_o, send_o, ch_o, rows_s, block_s,
):
    dr = in_proj.shape[0]
    er, sel_n = select.shape
    rank, states = step.shape[0], decay.shape[0]
    inner2 = mine_o.shape[1] - LANES
    first = idx[3] == 0
    for k in range(inner2 // span):
        low = in_proj[:, 2 * k * span : (2 * k + 1) * span]
        high = in_proj[:, (2 * k + 1) * span : (2 * k + 2) * span]
        mine_o[:, k * span : (k + 1) * span] = jnp.where(first, low, high)
        send_o[:, k * span : (k + 1) * span] = jnp.where(first, high, low)
    rows_s[...] = jnp.zeros_like(rows_s)
    rows_s[0:4, :er] = taps[...].astype(F32)
    rows_s[ROW_BIAS : ROW_BIAS + 1, :er] = cbias[...].astype(F32)
    rows_s[ROW_STEP : ROW_STEP + 1, :er] = sbias[...].astype(F32)
    rows_s[ROW_SKIP : ROW_SKIP + 1, :er] = skip[...].astype(F32)
    rows_s[ROW_DECAY : ROW_DECAY + states, :er] = decay[...].astype(F32)
    ch_o[:, LANES:] = jnp.transpose(rows_s[...])[:er].astype(BF16)
    rows_s[...] = jnp.zeros_like(rows_s)
    rows_s[LANES - rank :, :er] = step[...].astype(F32)
    block_s[...] = jnp.zeros_like(block_s)
    block_s[:er, :sel_n] = select[...].astype(F32)
    ch_o[:, :LANES] = (block_s[:er] + jnp.transpose(rows_s[...])[:er]).astype(BF16)
    rows_s[...] = jnp.zeros_like(rows_s)
    rows_s[ROW_FEATURE : ROW_FEATURE + 1, :dr] = norm[...].astype(F32)
    rows_s[ROW_FEATURE + 1 : ROW_FEATURE + 2, :dr] = moe[...].astype(F32)
    block_s[...] = jnp.zeros_like(block_s)
    block_s[:dr, ROW_FEATURE + 2 : ROW_FEATURE + 2 + router.shape[1]] = router[...].astype(F32)
    feature = (block_s[:dr] + jnp.transpose(rows_s[...])[:dr]).astype(BF16)
    mine_o[:, inner2:] = feature
    send_o[:, inner2:] = feature


def merge_kernel(mine, got, ch, out_proj, one_o, two_o):
    inner = out_proj.shape[1]
    both = jnp.concatenate([mine[...].astype(F32), got[...].astype(F32)], axis=0).astype(BF16)
    one_o[:, :inner] = both[:, :inner]
    one_o[:, inner : inner + LANES] = ch[:, :LANES]
    one_o[:, inner + LANES :] = ch[:, LANES:] + both[:, 2 * inner :]
    two_o[:, :inner] = both[:, inner : 2 * inner]
    two_o[:, inner:] = out_proj[...]


def enter_kernel(plan, idx, lens, tok2, nat, *refs):
    n = plan.n_gathered()
    pieces = refs[:n]
    u_o, xin_o, xc_o, sel_o, small_o, dnat_o, g1, sem = refs[n:]
    copies = plan.fetch(idx, pieces, g1, sem)
    rows, width = tok2.shape
    tok = rows // 2
    inner = xin_o.shape[1]
    perm = perm_matrix(idx, nat)
    vals = tok2[...].astype(F32)
    scale = lax.rsqrt(jnp.mean(vals * vals, axis=1, keepdims=True) + EPS)
    offset = both_offsets(lens, tok)
    for copy in copies:
        copy.wait()
    table = g1[:, inner + LANES :]
    dnat = mm(table, perm, (((0,), (1,)), ((), ())))[ROW_FEATURE:]
    dnat_o[...] = dnat[: dnat_o.shape[0]]
    u = (vals * scale * dnat[0:1]).astype(BF16)
    u = mm(u, perm).astype(BF16)
    u_o[...] = u
    xin = mm(u, g1[:, :inner])
    xin_o[...] = xin
    small = jnp.transpose(table.astype(F32))[: small_o.shape[0]]
    small_o[...] = small
    conv = conv_of(xin, small, offset)
    xc = (conv * sigmoid(conv)).astype(BF16)
    xc_o[...] = xc
    sel_o[...] = mm(xc, g1[:, inner : inner + LANES])


def conv_of(xin, small, offset):
    conv = small[ROW_BIAS : ROW_BIAS + 1] + small[3:4] * xin
    for lag in range(1, 4):
        moved = pltpu.roll(xin, lag, 0)
        conv = conv + jnp.where(offset >= lag, small[3 - lag : 4 - lag] * moved, 0.0)
    return conv


def swap_halves(rows):
    half = rows.shape[0] // 2
    return jnp.concatenate([rows[half:], rows[:half]], axis=0)


def scan_kernel(
    rank, states, lens, sel_a, sel_b, xc, g1sel, small,
    ys_o, step_o, sel_o, keep_o, check_o,
    dm_s, dx_s, wr_s, rd_s, rate_s, h_s,
):
    rows, inner = ys_o.shape
    tok = rows // 2
    sel = sel_a[...] + swap_halves(sel_b[...])
    sel_o[...] = sel
    lane = iota((rows, LANES), 1)
    tail = LANES - rank
    q = jnp.where(lane >= tail, pltpu.roll(sel, tail, 1), 0.0).astype(BF16)
    step_pre = mm(q, g1sel[...], NT) + small[ROW_STEP : ROW_STEP + 1]
    step_o[...] = step_pre
    delta = softplus(step_pre)
    offset = both_offsets(lens, tok)
    xcf = xc[...].astype(F32)
    dm_s[...] = jnp.where(offset > 0, delta, 1e30)
    keep_o[...] = jnp.broadcast_to((offset > 0).astype(F32), keep_o.shape)
    dx_s[...] = delta * xcf
    for b in range(2):
        turned = jnp.transpose(sel[b * tok : (b + 1) * tok])
        wr_s[b] = turned[rank : rank + states]
        rd_s[b] = turned[rank + states : rank + 2 * states]
    rate_s[...] = jnp.exp(small[ROW_DECAY : ROW_DECAY + states]) * (-LOG2E)
    h_s[...] = jnp.zeros_like(h_s)
    half = states // 2

    def chunk(ci, carry):
        t0 = pl.multiple_of(ci * 8, 8)
        for b in range(2):
            at = pl.multiple_of(b * tok + t0, 8)
            wr8 = pltpu.roll(wr_s[b], tok - t0, 1)
            rd8 = pltpu.roll(rd_s[b], tok - t0, 1)
            wcol = [jnp.broadcast_to(wr8[:, j : j + 1], (states, LANES)) for j in range(8)]
            rcol = [jnp.broadcast_to(rd8[:, j : j + 1], (states, LANES)) for j in range(8)]
            for g in range(inner // LANES):
                lanes = slice(g * LANES, (g + 1) * LANES)
                h = h_s[b, :, lanes]
                check_o[ci * 2 + b, :, lanes] = h
                rate = rate_s[:, lanes]
                dm8 = dm_s[pl.ds(at, 8), lanes]
                dx8 = dx_s[pl.ds(at, 8), lanes]
                parts = []
                for j in range(8):
                    d = jnp.broadcast_to(dm8[j : j + 1], (states, LANES))
                    x = jnp.broadcast_to(dx8[j : j + 1], (states, LANES))
                    h = jnp.exp2(d * rate) * h + wcol[j] * x
                    p = rcol[j] * h
                    parts.append(p[:half] + p[half:])
                ys_o[pl.ds(at, 8), lanes] = fold(parts)
                h_s[b, :, lanes] = h
        return carry

    lax.fori_loop(0, tok // 8, chunk, 0)


def gate_kernel(plan, idx, u, xc, ys, small, *refs):
    n = plan.n_gathered()
    pieces = refs[:n]
    gated_o, zg_o, mine_o, send_o, g2, sem = refs[n:]
    copies = plan.fetch(idx, pieces, g2, sem)
    for copy in copies:
        copy.wait()
    inner = ys.shape[1]
    tok = mine_o.shape[0]
    zg = mm(u[...], g2[:, :inner])
    zg_o[...] = zg
    gated = (ys[...] + small[ROW_SKIP : ROW_SKIP + 1] * xc[...].astype(F32)) * (zg * sigmoid(zg))
    gated = gated.astype(BF16)
    gated_o[...] = gated
    branch = mm(gated, g2[:, inner:])
    mine_o[...] = branch[:tok]
    send_o[...] = branch[tok:]


def route_tables(lens, routes, experts, capacity, tok):
    _, valid = positions(lens, 0, tok)
    valid_f = valid.astype(F32)
    width = max(LANES, experts)
    hot = (routes[...] == iota((tok, width), 1)).astype(F32)
    live = hot * valid_f
    earlier = (iota((tok, tok), 1) < iota((tok, tok), 0)).astype(F32).astype(BF16)
    before = mm(earlier, live.astype(BF16))
    rank = jnp.sum(before * hot, axis=1, keepdims=True).astype(jnp.int32)
    kept = valid & (rank < capacity)
    return valid_f, hot, rank, kept


def slot_hot(k, routes, rank, kept, capacity, tok):
    inside = kept & (routes[...] == k)
    return (inside & (rank == iota((tok, capacity), 1))).astype(F32).astype(BF16)


def moe_enter_kernel(experts, capacity, lens, tok, cot, routes, mine, got, dnat, disp_o, hidden_o, gate_o):
    rows, width = tok.shape
    hidden = tok[...].astype(F32) + (mine[...] + got[...])
    hidden_o[...] = hidden
    scale = lax.rsqrt(jnp.mean(hidden * hidden, axis=1, keepdims=True) + EPS)
    mv = (hidden * scale * dnat[1:2]).astype(BF16)
    logits = mm(mv, dnat[...].astype(BF16), NT)
    hot = (routes[...] + 2 == iota(logits.shape, 1)).astype(F32)
    gate = sigmoid(jnp.sum(logits * hot, axis=1, keepdims=True))
    gate_o[...] = jnp.broadcast_to(gate, gate_o.shape)
    valid_f, _, rank, kept = route_tables(lens, routes, experts, capacity, rows)
    back = (cot[...].astype(F32) * valid_f * (gate * kept.astype(F32))).astype(BF16)
    both = jnp.concatenate([mv, back], axis=1)
    for k in range(experts):
        disp_o[k] = mm(slot_hot(k, routes, rank, kept, capacity, rows), both, TN).astype(BF16)


def expert_kernel(width, own, peer, up, down, out_own, out_peer, up_g, down_g, rows_s, acc_s):
    half = own.shape[0]
    total = rows_s.shape[0]
    rows_s[:half] = own[...]
    rows_s[half:] = peer[...]
    hidden = up.shape[1]
    part = 256
    for f in range(0, hidden, part):
        x = rows_s[:, :width]
        g = rows_s[:, width:]
        pre = mm(x, up[0, f : f + part], NT)
        g_act = mm(g, down[0, f : f + part], NT)
        sq = pre * pre
        th = jnp.tanh(GELU_C * (pre + GELU_K * sq * pre))
        act = (0.5 * pre * (1.0 + th)).astype(BF16)
        slope = 0.5 * (1.0 + th) + 0.5 * pre * (1.0 - th * th) * (GELU_C * (1.0 + 3.0 * GELU_K * sq))
        g_pre = (g_act * slope).astype(BF16)
        down_g[0, f : f + part] = mm(act, g, TN)
        up_g[0, f : f + part] = mm(g_pre, x, TN)
        e_part = mm(act, down[0, f : f + part])
        i_part = mm(g_pre, up[0, f : f + part])
        if f == 0:
            acc_s[:, :width] = e_part
            acc_s[:, width:] = i_part
        else:
            acc_s[:, :width] += e_part
            acc_s[:, width:] += i_part
    out_own[...] = acc_s[:half]
    out_peer[...] = acc_s[half:].astype(BF16)


def moe_leave_kernel(
    experts, capacity, lens, routes, cot, hidden, gate_in, dnat, back,
    out_o, ghid_o, gbr_o, dgrad_o,
):
    rows, width = hidden.shape
    valid_f, _, rank, kept = route_tables(lens, routes, experts, capacity, rows)
    kept_f = kept.astype(F32)
    gate = gate_in[:, 0:1]
    picked = jnp.zeros((rows, 2 * width), F32)
    for k in range(experts):
        picked = picked + mm(slot_hot(k, routes, rank, kept, capacity, rows), back[k])
    ex_out = picked[:, :width]
    sent = picked[:, width:]
    hid = hidden[...]
    out_o[...] = (valid_f * (hid + gate * ex_out)).astype(BF16)
    gy = cot[...].astype(F32) * valid_f
    g_gate = jnp.sum(gy * ex_out, axis=1, keepdims=True)
    chosen = g_gate * gate * (1.0 - gate)
    small_rows = dnat.shape[0]
    hot = (routes[...] + 2 == iota((rows, small_rows), 1)).astype(F32)
    g_logit = (chosen * hot).astype(BF16)
    g_mv = mm(g_logit, dnat[...].astype(BF16)) + sent
    scale = lax.rsqrt(jnp.mean(hid * hid, axis=1, keepdims=True) + EPS)
    hat = hid * scale
    gain = dnat[1:2]
    mv = (hat * gain).astype(BF16)
    router_g = mm(g_logit, mv, TN)
    gain_g = jnp.sum(g_mv * hat, axis=0, keepdims=True)
    dgrad_o[...] = jnp.where(iota(dgrad_o.shape, 0) == 1, gain_g, router_g)
    gg = g_mv * gain
    mean = jnp.sum(gg * hat, axis=1, keepdims=True) * (1.0 / width)
    ghid = gy + scale * (gg - hat * mean)
    ghid_o[...] = ghid
    gbr_o[...] = ghid.astype(BF16)


def gate_back_kernel(plan, idx, gbr_a, gbr_b, g2, gated, xc, ys, zg, small, u, *refs):
    n = plan.n_shared()
    gy_o, gzg_o = refs[:2]
    shared = refs[2 : 2 + n]
    grad_s, sem = refs[2 + n :]
    inner = ys.shape[1]
    gbr = jnp.concatenate([gbr_a[...], gbr_b[...]], axis=0)
    g_gated = mm(gbr, g2[:, inner:], NT)
    skip = small[ROW_SKIP : ROW_SKIP + 1]
    sig = sigmoid(zg[...])
    gy_o[...] = g_gated * (zg[...] * sig)
    gzg = g_gated * (ys[...] + skip * xc[...].astype(F32)) * (sig * (1.0 + zg[...] * (1.0 - sig)))
    gzg = gzg.astype(BF16)
    gzg_o[...] = gzg
    grad_s[:, :inner] = mm(u[...], gzg, TN).astype(BF16)
    grad_s[:, inner:] = mm(gated[...], gbr, TN).astype(BF16)
    for copy in plan.emit(idx, grad_s, shared, sem):
        copy.wait()


def scan_back_kernel(
    rank, states, gy_s, xc, step_pre, sel, keep, small, g1sel, check,
    gsel_o, gxcs_o, gsr_o, q_o, smallg_o,
    dm_s, dx_s, gdx_s, gdl_s, wr_s, rd_s, gwr_s, grd_s, rate_s, lam_s, ga_s,
):
    rows, inner = gy_s.shape
    tok = rows // 2
    half = states // 2
    xcf = xc[...].astype(F32)
    skip = small[ROW_SKIP : ROW_SKIP + 1]
    delta = softplus(step_pre[...])
    dm_s[...] = jnp.where(keep[:, 0:1] > 0.0, delta, 1e30)
    dx_s[...] = delta * xcf
    for b in range(2):
        turned = jnp.transpose(sel[b * tok : (b + 1) * tok])
        wr_s[b] = turned[rank : rank + states]
        rd_s[b] = turned[rank + states : rank + 2 * states]
    rate_s[...] = jnp.exp(small[ROW_DECAY : ROW_DECAY + states]) * (-LOG2E)
    lam_s[...] = jnp.zeros_like(lam_s)
    ga_s[...] = jnp.zeros_like(ga_s)
    gwr_s[...] = jnp.zeros_like(gwr_s)
    grd_s[...] = jnp.zeros_like(grd_s)
    shape = (states, LANES)

    def chunk(i, carry):
        ci = tok // 8 - 1 - i
        t0 = pl.multiple_of(ci * 8, 8)
        for b in range(2):
            at = pl.multiple_of(b * tok + t0, 8)
            wr8 = pltpu.roll(wr_s[b], tok - t0, 1)
            rd8 = pltpu.roll(rd_s[b], tok - t0, 1)
            wcol = [jnp.broadcast_to(wr8[:, j : j + 1], shape) for j in range(8)]
            rcol = [jnp.broadcast_to(rd8[:, j : j + 1], shape) for j in range(8)]
            grd = [jnp.zeros(shape, F32)] * 8
            gwr = [jnp.zeros(shape, F32)] * 8
            for g in range(inner // LANES):
                lanes = slice(g * LANES, (g + 1) * LANES)
                h = check[ci * 2 + b, :, lanes]
                rate = rate_s[:, lanes]
                dm8 = dm_s[pl.ds(at, 8), lanes]
                dx8 = dx_s[pl.ds(at, 8), lanes]
                gy8 = gy_s[pl.ds(at, 8), lanes]
                decays, olds = [], []
                for j in range(8):
                    d = jnp.broadcast_to(dm8[j : j + 1], shape)
                    x = jnp.broadcast_to(dx8[j : j + 1], shape)
                    a = jnp.exp2(d * rate)
                    old = a * h
                    h = old + wcol[j] * x
                    grd[j] = grd[j] + h * jnp.broadcast_to(gy8[j : j + 1], shape)
                    decays.append(a)
                    olds.append(old)
                lam_in = lam_s[b, :, lanes]
                ga = ga_s[:, lanes]
                to_dx, to_dl = [None] * 8, [None] * 8
                for j in range(7, -1, -1):
                    lam = rcol[j] * jnp.broadcast_to(gy8[j : j + 1], shape) + lam_in
                    lam_in = decays[j] * lam
                    w = lam * olds[j]
                    ga = ga + w * jnp.broadcast_to(dm8[j : j + 1], shape)
                    p = lam * wcol[j]
                    to_dx[j] = p[:half] + p[half:]
                    p = w * rate
                    to_dl[j] = p[:half] + p[half:]
                    gwr[j] = gwr[j] + lam * jnp.broadcast_to(dx8[j : j + 1], shape)
                lam_s[b, :, lanes] = lam_in
                ga_s[:, lanes] = ga
                gdx_s[pl.ds(at, 8), lanes] = fold(to_dx)
                gdl_s[pl.ds(at, 8), lanes] = fold(to_dl)
            lane = iota(shape, 1)
            all_wr, all_rd = gwr_s[b], grd_s[b]
            for j in range(8):
                here = lane == t0 + j
                all_wr = jnp.where(here, jnp.sum(gwr[j], axis=1, keepdims=True), all_wr)
                all_rd = jnp.where(here, jnp.sum(grd[j], axis=1, keepdims=True), all_rd)
            gwr_s[b] = all_wr
            grd_s[b] = all_rd
        return carry

    lax.fori_loop(0, tok // 8, chunk, 0)
    delta = softplus(step_pre[...])
    gdx = gdx_s[...]
    xcf = xc[...].astype(F32)
    gy = gy_s[...]
    gxcs_o[...] = gy * skip + gdx * delta
    g_step = (gdx * xcf + LN2 * gdl_s[...]) * sigmoid(step_pre[...])
    gsr = g_step.astype(BF16)
    gsr_o[...] = gsr
    lane = iota((rows, LANES), 1)
    tail = LANES - rank
    q_o[...] = jnp.where(lane >= tail, pltpu.roll(sel[...], tail, 1), 0.0).astype(BF16)
    back = jnp.where(lane >= tail, mm(gsr, g1sel[...]), 0.0)
    back = pltpu.roll(back, rank, 1)
    zeros_top = jnp.zeros((rank, tok), F32)
    zeros_end = jnp.zeros((LANES - rank - 2 * states, tok), F32)
    for b in range(2):
        stack = jnp.concatenate([zeros_top, gwr_s[b], grd_s[b], zeros_end], axis=0)
        span = slice(b * tok, (b + 1) * tok)
        gsel_o[span] = back[span] + jnp.transpose(stack)
    smallg_o[0:ROW_STEP] = jnp.zeros((ROW_STEP, inner), F32)
    smallg_o[ROW_STEP : ROW_STEP + 1] = jnp.sum(g_step, axis=0, keepdims=True)
    smallg_o[ROW_SKIP : ROW_SKIP + 1] = jnp.sum(gy * xcf, axis=0, keepdims=True)
    smallg_o[ROW_SKIP + 1 : ROW_DECAY] = jnp.zeros((ROW_DECAY - ROW_SKIP - 1, inner), F32)
    smallg_o[ROW_DECAY : ROW_DECAY + states] = ga_s[...] * rate_s[...] * LN2
    rest = smallg_o.shape[0] - ROW_DECAY - states
    if rest:
        smallg_o[ROW_DECAY + states :] = jnp.zeros((rest, inner), F32)


def leave_kernel(
    plan, idx, lens, nat, gsel_a, gsel_b, gxcs, gzg, gsr, q, smallg, xin, xc, u, small, g1, g2z, tok2, dnat, dgrad, *refs
):
    n = plan.n_shared()
    mine_o, send_o = refs[:2]
    shared = refs[2 : 2 + n]
    grad_s, sem = refs[2 + n :]
    rows, inner = xin.shape
    tok = rows // 2
    width = tok2.shape[1]
    perm = perm_matrix(idx, nat)
    g_sel = (gsel_a[...] + swap_halves(gsel_b[...])).astype(BF16)
    selblk = g1[:, inner : inner + LANES]
    block = mm(xc[...], g_sel, TN) + mm(gsr[...], q[...], TN)
    grad_s[:, inner : inner + LANES] = block.astype(BF16)
    g_xc = mm(g_sel, selblk, NT) + gxcs[...]
    offset = both_offsets(lens, tok)
    x = xin[...]
    sm = small[...]
    conv = conv_of(x, sm, offset)
    sig = sigmoid(conv)
    g_conv = g_xc * (sig * (1.0 + conv * (1.0 - sig)))
    g_xin = sm[3:4] * g_conv
    taps = [None, None, None, jnp.sum(g_conv * x, axis=0, keepdims=True)]
    for lag in range(1, 4):
        held = jnp.where(offset >= lag, g_conv, 0.0)
        g_xin = g_xin + sm[3 - lag : 4 - lag] * pltpu.roll(held, rows - lag, 0)
        taps[3 - lag] = jnp.sum(held * pltpu.roll(x, lag, 0), axis=0, keepdims=True)
    g_bias = jnp.sum(g_conv, axis=0, keepdims=True)
    g_xin = g_xin.astype(BF16)
    grad_s[:, :inner] = mm(u[...], g_xin, TN).astype(BF16)
    gn = mm(g_xin, g1[:, :inner], NT) + mm(gzg[...], g2z[...], NT)
    gn = split_mm(gn, perm, NT)
    mine_o[...] = gn[:tok]
    send_o[...] = gn[tok:]
    vals = tok2[...].astype(F32)
    scale = lax.rsqrt(jnp.mean(vals * vals, axis=1, keepdims=True) + EPS)
    gain_g = jnp.sum(gn * (vals * scale), axis=0, keepdims=True)
    dg = jnp.where(iota(dgrad.shape, 0) == 0, gain_g, dgrad[...])
    dg = split_mm(dg, perm)
    top = jnp.concatenate(taps + [g_bias, jnp.zeros((3, inner), F32)], axis=0)
    gap = jnp.zeros((ROW_FEATURE - smallg.shape[0], inner), F32)
    end = jnp.zeros((LANES - ROW_FEATURE - dg.shape[0], inner), F32)
    table = jnp.concatenate([smallg[0:8] + top, smallg[8:], gap, dg, end], axis=0)
    grad_s[:, inner + LANES :] = jnp.transpose(table).astype(BF16)
    for copy in plan.emit(idx, grad_s, shared, sem):
        copy.wait()


def final_kernel(tok, mine, got, ghid, dnat, out_o):
    width = tok.shape[1]
    vals = tok[...].astype(F32)
    scale = lax.rsqrt(jnp.mean(vals * vals, axis=1, keepdims=True) + EPS)
    hat = vals * scale
    gg = (mine[...] + got[...]) * dnat[0:1]
    mean = jnp.sum(gg * hat, axis=1, keepdims=True) * (1.0 / width)
    out_o[...] = ghid[...] + scale * (gg - hat * mean)


def swap(values, axis):
    return lax.ppermute(values, axis, [(0, 1), (1, 0)])


def share_kernel(n1, n2, rank, states, *refs):
    one, two = refs[:n1], refs[n1 : n1 + n2]
    keep_o, send_o, outg_o, select_o, step_o, taps_o, cbias_o, sbias_o, skip_o, decay_o, square_s = refs[n1 + n2 :]
    er = outg_o.shape[0]
    dr = keep_o.shape[0]

    def total(parts):
        acc = parts[0][...].astype(F32)
        for part in parts[1:]:
            acc = acc + part[...].astype(F32)
        return acc

    x = total(one)
    inner = x.shape[1] - 2 * LANES
    z = total(two)
    for out, at in ((keep_o, 0), (send_o, dr)):
        out[:, :inner] = x[at : at + dr, :inner]
        out[:, inner : 2 * inner] = z[at : at + dr, :inner]
        out[:, 2 * inner :] = x[at : at + dr, inner + LANES :]
    outg_o[...] = z[:, inner:]
    select_o[...] = x[:, inner : inner + select_o.shape[1]]
    square_s[...] = jnp.zeros_like(square_s)
    square_s[:er] = x[:, inner : inner + LANES]
    step_o[...] = jnp.transpose(square_s[...])[LANES - rank :, :er]
    square_s[:er] = x[:, inner + LANES :]
    table = jnp.transpose(square_s[...])[:, :er]
    taps_o[...] = table[0:4]
    cbias_o[...] = table[ROW_BIAS : ROW_BIAS + 1]
    sbias_o[...] = table[ROW_STEP : ROW_STEP + 1]
    skip_o[...] = table[ROW_SKIP : ROW_SKIP + 1]
    decay_o[...] = table[ROW_DECAY : ROW_DECAY + states]


def spread_kernel(span, idx, keep, got, in_o, norm_o, moe_o, router_o, square_s):
    dr = keep.shape[0]
    inner2 = keep.shape[1] - LANES
    first = idx[3] == 0
    for k in range(inner2 // span):
        mine = keep[:, k * span : (k + 1) * span]
        peer = got[:, k * span : (k + 1) * span]
        in_o[:, 2 * k * span : (2 * k + 1) * span] = jnp.where(first, mine, peer)
        in_o[:, (2 * k + 1) * span : (2 * k + 2) * span] = jnp.where(first, peer, mine)
    table = keep[:, inner2:] + got[:, inner2:]
    at = ROW_FEATURE
    router_o[...] = table[:, at + 2 : at + 2 + router_o.shape[1]]
    square_s[...] = jnp.zeros_like(square_s)
    square_s[:dr] = table
    flat = jnp.transpose(square_s[...])[:, :dr]
    norm_o[...] = flat[at : at + 1]
    moe_o[...] = flat[at + 1 : at + 2]


def body(
    sizes,
    tokens,
    cotangent,
    seq_lens,
    routes,
    norm_gain,
    input_proj,
    conv_weight,
    conv_bias,
    select_proj,
    step_proj,
    step_bias,
    decay_log,
    skip_gain,
    output_proj,
    moe_gain,
    router_weight,
    up_weight,
    down_weight,
):
    ny, nz, nx = sizes
    nf = nz * nx
    ng = ny * nf
    tok, width = tokens.shape
    rank, er = step_proj.shape
    states = decay_log.shape[0]
    experts = router_weight.shape[1]
    capacity = 5 * tok // (4 * experts)
    dr = norm_gain.shape[0]
    inner = ng * er
    rows = 2 * tok
    small_n = -(-(ROW_DECAY + states) // 8) * 8
    dn = -(-(2 + experts) // 8) * 8
    plan = Plan(ny, nz, nx, er)
    idx = jnp.stack([lax.axis_index(a) for a in ("y", "z", "x", "c")]).astype(jnp.int32)

    order = np.arange(width).reshape(ny, 2, nf, dr).transpose(0, 2, 1, 3)
    nat = np.stack([order.reshape(width), order[:, :, ::-1].reshape(width)])
    nat = jnp.asarray(nat, jnp.int32)

    span = nf * er
    mine_w, send_w, ch = call(
        functools.partial(pack_kernel, span),
        [((dr, 2 * inner + LANES), BF16), ((dr, 2 * inner + LANES), BF16), ((er, 2 * LANES), BF16)],
        [idx, input_proj, norm_gain[None], moe_gain[None], router_weight, conv_weight, conv_bias[None], select_proj, step_proj, step_bias[None], decay_log, skip_gain[None]],
        [SMEM] + [None] * 11,
        scratch=[pltpu.VMEM((LANES, LANES), F32), pltpu.VMEM((LANES, LANES), F32)],
        name="pack",
        us=1,
    )
    got_w = swap(send_w, "c")
    group1, group2 = call(
        merge_kernel,
        [((er, inner + 2 * LANES), BF16), ((er, inner + width), BF16)],
        [mine_w, got_w, ch, output_proj],
        name="merge",
        us=1,
    )
    tok2 = jnp.concatenate([tokens, swap(tokens, "c")], axis=0)
    lens2 = jnp.concatenate([seq_lens, swap(seq_lens, "c")], axis=0)
    pieces1 = plan.gather(group1)
    pieces2 = plan.gather(group2)

    fetch_sem = pltpu.SemaphoreType.DMA((ng,))
    emit_sem = pltpu.SemaphoreType.DMA((2 * ng,))
    u, xin, xc, selp, small_t, dnat, g1 = call(
        functools.partial(enter_kernel, plan),
        [((rows, width), BF16), ((rows, inner), F32), ((rows, inner), BF16), ((rows, LANES), F32), ((small_n, inner), F32), ((dn, width), F32), ((inner, inner + 2 * LANES), BF16)],
        [idx, lens2, tok2, nat] + pieces1,
        [SMEM, SMEM, None, None] + [HBM] * len(pieces1),
        scratch=[fetch_sem],
        name="enter",
    )
    selq = swap(selp, "c")
    g1sel_spec = pl.BlockSpec((inner, LANES), lambda i: (0, inner // LANES))
    chunks = tok // 8
    ys, step_pre, sel, keep, check = call(
        functools.partial(scan_kernel, rank, states),
        [((rows, inner), F32), ((rows, inner), F32), ((rows, LANES), F32), ((rows, LANES), F32), ((2 * chunks, states, inner), F32)],
        [lens2, selp, selq, xc, g1, small_t],
        [SMEM, None, None, None, g1sel_spec, None],
        scratch=[pltpu.VMEM((rows, inner), F32), pltpu.VMEM((rows, inner), F32), pltpu.VMEM((2, states, tok), F32), pltpu.VMEM((2, states, tok), F32), pltpu.VMEM((states, inner), F32), pltpu.VMEM((2, states, inner), F32)],
        name="scan",
        us=9,
    )
    gated, zg, br_mine, br_send, g2 = call(
        functools.partial(gate_kernel, plan),
        [((rows, inner), BF16), ((rows, inner), F32), ((tok, width), F32), ((tok, width), F32), ((inner, inner + width), BF16)],
        [idx, u, xc, ys, small_t] + pieces2,
        [SMEM] + [None] * 4 + [HBM] * len(pieces2),
        scratch=[fetch_sem],
        name="gate",
    )
    br_got = swap(br_send, "c")
    disp, hidden, gate = call(
        functools.partial(moe_enter_kernel, experts, capacity),
        [((experts, capacity, 2 * width), BF16), ((tok, width), F32), ((tok, LANES), F32)],
        [seq_lens, tokens, cotangent, routes, br_mine, br_got, dnat],
        [SMEM] + [None] * 6,
        name="moe_enter",
    )
    line = lax.all_to_all(disp, ("z", "x"), split_axis=0, concat_axis=0, tiled=True)
    line = line.reshape(nf * capacity, 2 * width)
    if ny > 1:
        line = jnp.concatenate([line, swap(line, "y")], axis=0)
    peer = swap(line, "c")
    total = 2 * line.shape[0]
    hid = up_weight.shape[1]
    out_own, out_peer, up_grad, down_grad = call(
        functools.partial(expert_kernel, width),
        [((total // 2, 2 * width), F32), ((total // 2, 2 * width), BF16), ((1, hid, width), F32), ((1, hid, width), F32)],
        [line, peer, up_weight, down_weight],
        scratch=[pltpu.VMEM((total, 2 * width), BF16), pltpu.VMEM((total, 2 * width), F32)],
        name="expert",
    )
    summed = out_own + swap(out_peer, "c").astype(F32)
    if ny > 1:
        cut = nf * capacity
        summed = summed[:cut] + swap(summed[cut:].astype(BF16), "y").astype(F32)
    back = lax.all_to_all(
        summed.astype(BF16).reshape(nf, capacity, 2 * width), ("z", "x"), split_axis=0, concat_axis=0, tiled=True
    )
    result, ghid, gbr, dgrad = call(
        functools.partial(moe_leave_kernel, experts, capacity),
        [((tok, width), BF16), ((tok, width), F32), ((tok, width), BF16), ((dn, width), F32)],
        [seq_lens, routes, cotangent, hidden, gate, dnat, back],
        [SMEM] + [None] * 6,
        name="moe_leave",
    )
    gbr_got = swap(gbr, "c")
    gy, gzg, *shared2 = call(
        functools.partial(gate_back_kernel, plan),
        [((rows, inner), F32), ((rows, inner), BF16)] + plan.shared_outs(inner + width),
        [idx, gbr, gbr_got, g2, gated, xc, ys, zg, small_t, u],
        [SMEM] + [None] * 9,
        scratch=[pltpu.VMEM((inner, inner + width), BF16), emit_sem],
        name="gate_back",
    )
    gsel, gxcs, gsr, q, smallg = call(
        functools.partial(scan_back_kernel, rank, states),
        [((rows, LANES), F32), ((rows, inner), F32), ((rows, inner), BF16), ((rows, LANES), BF16), ((small_n, inner), F32)],
        [gy, xc, step_pre, sel, keep, small_t, g1, check],
        [None] * 6 + [g1sel_spec, None],
        scratch=[pltpu.VMEM((rows, inner), F32)] * 4 + [pltpu.VMEM((2, states, tok), F32)] * 4 + [pltpu.VMEM((states, inner), F32), pltpu.VMEM((2, states, inner), F32), pltpu.VMEM((states, inner), F32)],
        name="scan_back",
        us=16,
    )
    parts2 = plan.reduce(shared2, "two")
    gsel_got = swap(gsel, "c")
    g2z_spec = pl.BlockSpec((inner, inner), lambda i: (0, 0))
    gn_mine, gn_send, *shared1 = call(
        functools.partial(leave_kernel, plan),
        [((tok, width), F32), ((tok, width), F32)] + plan.shared_outs(inner + 2 * LANES),
        [idx, lens2, nat, gsel, gsel_got, gxcs, gzg, gsr, q, smallg, xin, xc, u, small_t, g1, g2, tok2, dnat, dgrad],
        [SMEM, SMEM] + [None] * 13 + [g2z_spec, None, None, None],
        scratch=[pltpu.VMEM((inner, inner + 2 * LANES), BF16), emit_sem],
        name="leave",
        us=9,
    )
    parts1 = plan.reduce(shared1, "one")
    gn_got = swap(gn_send, "c")
    (input_grad,) = call(
        final_kernel, [((tok, width), F32)], [tokens, gn_mine, gn_got, ghid, dnat], name="final", us=2
    )
    sel_n = select_proj.shape[1]
    keep_w, send_back, out_grad, select_grad, step_grad, taps_grad, cb, sb, sk, decay_grad = call(
        functools.partial(share_kernel, len(parts1), len(parts2), rank, states),
        [((dr, 2 * inner + LANES), F32)] * 2
        + [((er, width), F32), ((er, sel_n), F32), ((rank, er), F32), ((4, er), F32), ((1, er), F32), ((1, er), F32), ((1, er), F32), ((states, er), F32)],
        list(parts1) + list(parts2),
        scratch=[pltpu.VMEM((LANES, LANES), F32)],
        name="share",
        us=1,
    )
    in_grad, norm_grad, moe_grad, router_grad = call(
        functools.partial(spread_kernel, span),
        [((dr, 4 * inner), F32), ((1, dr), F32), ((1, dr), F32), ((dr, experts), F32)],
        [idx, keep_w, swap(send_back, "c")],
        [SMEM, None, None],
        scratch=[pltpu.VMEM((LANES, LANES), F32)],
        name="spread",
        us=1,
    )
    return (
        result,
        input_grad,
        norm_grad[0],
        in_grad,
        taps_grad,
        cb[0],
        select_grad,
        step_grad,
        sb[0],
        decay_grad,
        sk[0],
        out_grad,
        moe_grad[0],
        router_grad,
        up_grad,
        down_grad,
    )


def solution(mesh):
    dp, fsdp = mesh.shape["dp"], mesh.shape["fsdp"]
    ny, nx = dp // 2, 2
    nz = fsdp // nx
    fine = Mesh(mesh.devices.reshape(ny, 2, nz, nx), ALL)
    tok = P(ALL, None)
    vec = P(ALL)
    col = P(None, ALL)
    exp = P(("z", "x"), ("y", "c"), None)
    in_specs = (tok, tok, tok, tok, vec, tok, col, vec, tok, col, vec, col, vec, tok, vec, tok, exp, exp)
    out_specs = (tok, tok, vec, tok, col, vec, tok, col, vec, col, vec, tok, vec, tok, exp, exp)
    return jax.shard_map(
        functools.partial(body, (ny, nz, nx)), mesh=fine, in_specs=in_specs, out_specs=out_specs, check_vma=False
    )
```

```python
import functools

import jax
import jax.numpy as jnp
import numpy as np
from jax import lax
from jax.experimental import pallas as pl
from jax.experimental.pallas import tpu as pltpu
from jax.sharding import Mesh
from jax.sharding import PartitionSpec as P

EPS = 1e-05
F32 = jnp.float32
BF16 = jnp.bfloat16
LANES = 128
LOG2E = 1.4426950408889634
LN2 = 0.6931471805599453
GELU_C = 0.7978845608028654
GELU_K = 0.044715
ALL = ("y", "c", "z", "x")
GROUP = ("y", "z", "x")
ROW_BIAS, ROW_STEP, ROW_SKIP, ROW_DECAY = 4, 5, 6, 8
ROW_FEATURE = 64
NN = (((1,), (0,)), ((), ()))
NT = (((1,), (1,)), ((), ()))
TN = (((0,), (0,)), ((), ()))


def mm(left, right, dims=NN):
    return lax.dot_general(left, right, dims, preferred_element_type=F32)


def split_mm(left, right, dims=NN):
    high = left.astype(BF16)
    rest = left - high.astype(F32)
    mid = rest.astype(BF16)
    low = (rest - mid.astype(F32)).astype(BF16)
    return mm(high, right, dims) + (mm(mid, right, dims) + mm(low, right, dims))


def iota(shape, dim):
    return lax.broadcasted_iota(jnp.int32, shape, dim)


def sigmoid(v):
    return 1.0 / (1.0 + jnp.exp(-v))


def softplus(v):
    return jnp.maximum(v, 0.0) + jnp.log1p(jnp.exp(-jnp.abs(v)))


def positions(lens_ref, row, tok):
    pos = iota((tok, 1), 0)
    end = jnp.int32(0)
    start = jnp.zeros((tok, 1), jnp.int32)
    for j in range(lens_ref.shape[1]):
        length = lens_ref[row, j]
        end = end + length
        start = start + jnp.where(pos >= end, length, 0)
    return pos - start, pos < end


def both_offsets(lens_ref, tok):
    return jnp.concatenate([positions(lens_ref, row, tok)[0] for row in range(2)], axis=0)


def fold(parts):
    rows = iota((8, LANES), 0)
    step = 1
    while len(parts) > 1:
        first = (rows & step) == 0
        merged = []
        for k in range(0, len(parts), 2):
            a, b = parts[k], parts[k + 1]
            merged.append(jnp.where(first, a, b) + pltpu.roll(jnp.where(first, b, a), step, 0))
        parts = merged
        step *= 2
    return parts[0]


def call(kernel, outs, args, specs=None, scratch=(), name=None, us=5, vmem=32):
    whole = pl.BlockSpec(memory_space=pltpu.VMEM)
    specs = [None] * len(args) if specs is None else specs
    windowed = any(s is not None and s.block_shape is not None for s in specs)
    results = pl.pallas_call(
        kernel,
        grid=(1,) if windowed else (),
        out_shape=[(pltpu.HBM if len(o) > 3 else jax.ShapeDtypeStruct)(o[0], o[1]) for o in outs],
        in_specs=[whole if s is None else s for s in specs],
        out_specs=[whole if len(o) < 3 or o[2] is None else o[2] for o in outs],
        scratch_shapes=list(scratch),
        name=name,
        cost_estimate=pl.CostEstimate(flops=us * 300000000, bytes_accessed=us * 900000, transcendentals=0),
        compiler_params=pltpu.CompilerParams(vmem_limit_bytes=vmem << 20),
    )(*args)
    return list(results)


SMEM = pl.BlockSpec(memory_space=pltpu.SMEM)
HBM = pl.BlockSpec(memory_space=pl.ANY)


def perm_matrix(idx, nat_ref):
    width = nat_ref.shape[1]
    nat = jnp.where(idx[3] == 0, nat_ref[0:1], nat_ref[1:2])
    return (iota((width, width), 0) == nat).astype(F32).astype(BF16)


def kept(shape, dtype):
    return (shape, dtype, None, True)


def in_hbm(value):
    return pltpu.with_memory_space_constraint(value, pltpu.HBM)


def after(value, other):
    if other is None:
        return value
    return lax.optimization_barrier((value, other))[0]


class Plan:
    def __init__(self, ny, nz, nx, piece):
        self.ny, self.nz, self.nx, self.piece = ny, nz, nx, piece
        self.count = ny * nz * nx
        self.fast = (ny, nz, nx) == (2, 4, 2) and piece % 16 == 0

    def place(self, idx, yr, zr, xr):
        y = jnp.bitwise_xor(idx[0], yr)
        x = jnp.bitwise_xor(idx[2], xr)
        z = lax.rem(idx[1] - zr + self.nz, self.nz)
        return pl.multiple_of(((y * self.nz + z) * self.nx + x) * self.piece, self.piece)

    def gather(self, groups, first):
        if not self.fast:
            return [[lax.all_gather(piece, GROUP, axis=0, tiled=True)] for piece in groups]
        half = 2 * self.piece
        out, before_line, before_last = [], None, None
        for piece in groups:
            piece = after(piece, before_line)
            rots = [lax.ppermute(piece, "z", [(i, (i + k) % 4) for i in range(4)]) for k in (1, 2, 3)]
            line = jnp.concatenate([piece] + rots, axis=0)
            line = after(line, first if before_line is None else before_last)
            before_line = line
            by_x, by_y = swap(line, "x"), swap(line, "y")
            out.append([line, by_x, by_y, swap(by_x[:half], "y"), swap(by_y[half:], "x")])
            before_last = tuple(out[-1][3:])
        return out

    def pieces(self):
        n, out = self.piece, []
        for z in range(4):
            out.append((0, z * n, 0, z, 0))
            out.append((1, z * n, 0, z, 1))
            out.append((2, z * n, 1, z, 0))
            out.append((3 + z // 2, z % 2 * n, 1, z, 1))
        return out

    def n_gathered(self):
        return 5 if self.fast else 1

    def fetch(self, idx, refs, dst, sem):
        if not self.fast:
            copies = [pltpu.make_async_copy(refs[0], dst, sem.at[0])]
        else:
            copies = []
            for k, (r, row, yr, zr, xr) in enumerate(self.pieces()):
                to = dst.at[pl.ds(self.place(idx, yr, zr, xr), self.piece)]
                copies.append(pltpu.make_async_copy(refs[r].at[pl.ds(row, self.piece)], to, sem.at[k]))
        for copy in copies:
            copy.start()
        return copies

    def shared_outs(self, width):
        if not self.fast:
            return [((self.count * self.piece, width), BF16, HBM)]
        return [((8 * self.piece, width // 2), BF16, HBM)] * 4

    def n_shared(self):
        return 4 if self.fast else 1

    def emit(self, idx, src, refs, sem):
        if not self.fast:
            copies = [pltpu.make_async_copy(src, refs[0], sem.at[0])]
        else:
            copies, n, half = [], self.piece, src.shape[1] // 2
            for zr in range(4):
                for yr in range(2):
                    for xr in range(2):
                        at = self.place(idx, yr, zr, xr)
                        for lanes, ref, row in (
                            (0, refs[2 - 2 * xr], yr * 4 + zr),
                            (half, refs[3 - 2 * yr], xr * 4 + zr),
                        ):
                            copies.append(
                                pltpu.make_async_copy(
                                    src.at[pl.ds(at, n), pl.ds(lanes, half)],
                                    ref.at[pl.ds(row * n, n)],
                                    sem.at[len(copies)],
                                )
                            )
        for copy in copies:
            copy.start()
        return copies

    def reduce1(self, shared, tag):
        if not self.fast:
            return shared
        a_send, b_send, a_keep, b_keep = shared
        n, half = self.piece, a_send.shape[1]
        a_got, b_got = swap(a_send, "x"), swap(b_send, "y")
        shape = ((4 * n, half), BF16)
        return call(add_kernel, [shape] * 4, [a_keep, a_got, b_keep, b_got], name="add1_" + tag, us=1)

    def reduce2(self, sums, tag):
        if not self.fast:
            return sums
        a_send, a_keep, b_send, b_keep = sums
        n, half = self.piece, a_send.shape[1]
        a_got, b_got = swap(a_send, "y"), swap(b_send, "x")
        outs = [((n, 2 * half), BF16)] * 4
        return call(line_kernel, outs, [a_keep, a_got, b_keep, b_got], name="add2_" + tag, us=1)

    def reduce3(self, parts):
        if not self.fast:
            shares = parts[0].reshape(self.count, self.piece, -1)
            shares = lax.all_to_all(shares, GROUP, split_axis=0, concat_axis=0, tiled=True)
            return [shares.astype(F32).sum(axis=0)]
        rots = [lax.ppermute(parts[k], "z", [(i, (i - k) % 4) for i in range(4)]) for k in (1, 2, 3)]
        return [parts[0]] + rots


def add_kernel(a, a_in, b, b_in, a_send, a_keep, b_send, b_keep):
    cut = a_send.shape[0]
    for one, two, send, keep in ((a, a_in, a_send, a_keep), (b, b_in, b_send, b_keep)):
        send[...] = (one[cut:].astype(F32) + two[cut:].astype(F32)).astype(BF16)
        keep[...] = (one[:cut].astype(F32) + two[:cut].astype(F32)).astype(BF16)


def line_kernel(a, a_in, b, b_in, *outs):
    n, half = outs[0].shape[0], a.shape[1]
    for k, out in enumerate(outs):
        span = slice(k * n, (k + 1) * n)
        out[:, :half] = (a[span].astype(F32) + a_in[span].astype(F32)).astype(BF16)
        out[:, half:] = (b[span].astype(F32) + b_in[span].astype(F32)).astype(BF16)


def pack_kernel(
    span, idx, in_proj, norm, moe, router, taps, cbias, select, step, sbias, decay, skip, up,
    mine_o, send_o, ch_o, up_o, rows_s, block_s, sem,
):
    copy = pltpu.make_async_copy(up.at[:, pl.ds(0, up_o.shape[1])], up_o, sem)
    copy.start()
    dr = in_proj.shape[0]
    er, sel_n = select.shape
    rank, states = step.shape[0], decay.shape[0]
    inner2 = mine_o.shape[1] - LANES
    first = idx[3] == 0
    for k in range(inner2 // span):
        low = in_proj[:, 2 * k * span : (2 * k + 1) * span]
        high = in_proj[:, (2 * k + 1) * span : (2 * k + 2) * span]
        mine_o[:, k * span : (k + 1) * span] = jnp.where(first, low, high)
        send_o[:, k * span : (k + 1) * span] = jnp.where(first, high, low)
    rows_s[...] = jnp.zeros_like(rows_s)
    rows_s[0:4, :er] = taps[...].astype(F32)
    rows_s[ROW_BIAS : ROW_BIAS + 1, :er] = cbias[...].astype(F32)
    rows_s[ROW_STEP : ROW_STEP + 1, :er] = sbias[...].astype(F32)
    rows_s[ROW_SKIP : ROW_SKIP + 1, :er] = skip[...].astype(F32)
    rows_s[ROW_DECAY : ROW_DECAY + states, :er] = decay[...].astype(F32)
    ch_o[:, LANES:] = jnp.transpose(rows_s[...])[:er].astype(BF16)
    rows_s[...] = jnp.zeros_like(rows_s)
    rows_s[LANES - rank :, :er] = step[...].astype(F32)
    block_s[...] = jnp.zeros_like(block_s)
    block_s[:er, :sel_n] = select[...].astype(F32)
    ch_o[:, :LANES] = (block_s[:er] + jnp.transpose(rows_s[...])[:er]).astype(BF16)
    rows_s[...] = jnp.zeros_like(rows_s)
    rows_s[ROW_FEATURE : ROW_FEATURE + 1, :dr] = norm[...].astype(F32)
    rows_s[ROW_FEATURE + 1 : ROW_FEATURE + 2, :dr] = moe[...].astype(F32)
    rows_s[ROW_FEATURE + 2 : ROW_FEATURE + 2 + router.shape[0], :dr] = router[...].astype(F32)
    feature = jnp.transpose(rows_s[...])[:dr].astype(BF16)
    mine_o[:, inner2:] = feature
    send_o[:, inner2:] = feature
    copy.wait()


def split_kernel(up, down, up_o, down_a, down_b, sem):
    copies = [
        pltpu.make_async_copy(up.at[:, pl.ds(up.shape[1] - up_o.shape[1], up_o.shape[1])], up_o, sem.at[0]),
        pltpu.make_async_copy(down.at[:, pl.ds(0, down_a.shape[1])], down_a, sem.at[1]),
        pltpu.make_async_copy(down.at[:, pl.ds(down_a.shape[1], down_b.shape[1])], down_b, sem.at[2]),
    ]
    for copy in copies:
        copy.start()
    for copy in copies:
        copy.wait()


def merge_kernel(mine, got, ch, out_proj, one_o, two_o):
    inner = out_proj.shape[1]
    both = jnp.concatenate([mine[...].astype(F32), got[...].astype(F32)], axis=0).astype(BF16)
    one_o[:, :inner] = both[:, :inner]
    one_o[:, inner : inner + LANES] = ch[:, :LANES]
    one_o[:, inner + LANES :] = ch[:, LANES:] + both[:, 2 * inner :]
    two_o[:, :inner] = both[:, inner : 2 * inner]
    two_o[:, inner:] = out_proj[...]


def enter_kernel(plan, idx, lens, tok2, nat, *refs):
    n = plan.n_gathered()
    pieces = refs[:n]
    u_o, xin_o, xc_o, sel_o, small_o, dnat_o, g1, sem = refs[n:]
    copies = plan.fetch(idx, pieces, g1, sem)
    rows, width = tok2.shape
    tok = rows // 2
    inner = xin_o.shape[1]
    perm = perm_matrix(idx, nat)
    vals = tok2[...].astype(F32)
    scale = lax.rsqrt(jnp.mean(vals * vals, axis=1, keepdims=True) + EPS)
    offset = both_offsets(lens, tok)
    for copy in copies:
        copy.wait()
    table = g1[:, inner + LANES :]
    dnat = mm(table, perm, (((0,), (1,)), ((), ())))[ROW_FEATURE:]
    dnat_o[...] = dnat[: dnat_o.shape[0]]
    u = (vals * scale * dnat[0:1]).astype(BF16)
    u = mm(u, perm).astype(BF16)
    u_o[...] = u
    xin = mm(u, g1[:, :inner])
    xin_o[...] = xin
    small = jnp.transpose(table.astype(F32))[: small_o.shape[0]]
    small_o[...] = small
    conv = conv_of(xin, small, offset)
    xc = (conv * sigmoid(conv)).astype(BF16)
    xc_o[...] = xc
    sel_o[...] = mm(xc, g1[:, inner : inner + LANES])


def conv_of(xin, small, offset):
    conv = small[ROW_BIAS : ROW_BIAS + 1] + small[3:4] * xin
    for lag in range(1, 4):
        moved = pltpu.roll(xin, lag, 0)
        conv = conv + jnp.where(offset >= lag, small[3 - lag : 4 - lag] * moved, 0.0)
    return conv


def swap_halves(rows):
    half = rows.shape[0] // 2
    return jnp.concatenate([rows[half:], rows[:half]], axis=0)


def scan_kernel(
    rank, states, lens, sel_a, sel_b, xc, g1sel, small,
    ys_o, step_o, sel_o, keep_o, check_o,
    dm_s, dx_s, wr_s, rd_s, rate_s, h_s,
):
    rows, inner = ys_o.shape
    tok = rows // 2
    sel = sel_a[...] + swap_halves(sel_b[...])
    sel_o[...] = sel
    lane = iota((rows, LANES), 1)
    tail = LANES - rank
    q = jnp.where(lane >= tail, pltpu.roll(sel, tail, 1), 0.0).astype(BF16)
    step_pre = mm(q, g1sel[...], NT) + small[ROW_STEP : ROW_STEP + 1]
    step_o[...] = step_pre
    delta = softplus(step_pre)
    offset = both_offsets(lens, tok)
    xcf = xc[...].astype(F32)
    dm_s[...] = jnp.where(offset > 0, delta, 1e30)
    keep_o[...] = jnp.broadcast_to((offset > 0).astype(F32), keep_o.shape)
    dx_s[...] = delta * xcf
    for b in range(2):
        turned = jnp.transpose(sel[b * tok : (b + 1) * tok])
        wr_s[b] = turned[rank : rank + states]
        rd_s[b] = turned[rank + states : rank + 2 * states]
    rate_s[...] = jnp.exp(small[ROW_DECAY : ROW_DECAY + states]) * (-LOG2E)
    h_s[...] = jnp.zeros_like(h_s)
    half = states // 2

    def chunk(ci, carry):
        t0 = pl.multiple_of(ci * 8, 8)
        for b in range(2):
            at = pl.multiple_of(b * tok + t0, 8)
            wr8 = pltpu.roll(wr_s[b], tok - t0, 1)
            rd8 = pltpu.roll(rd_s[b], tok - t0, 1)
            wcol = [jnp.broadcast_to(wr8[:, j : j + 1], (states, LANES)) for j in range(8)]
            rcol = [jnp.broadcast_to(rd8[:, j : j + 1], (states, LANES)) for j in range(8)]
            for g in range(inner // LANES):
                lanes = slice(g * LANES, (g + 1) * LANES)
                h = h_s[b, :, lanes]
                check_o[ci * 2 + b, :, lanes] = h
                rate = rate_s[:, lanes]
                dm8 = dm_s[pl.ds(at, 8), lanes]
                dx8 = dx_s[pl.ds(at, 8), lanes]
                parts = []
                for j in range(8):
                    d = jnp.broadcast_to(dm8[j : j + 1], (states, LANES))
                    x = jnp.broadcast_to(dx8[j : j + 1], (states, LANES))
                    h = jnp.exp2(d * rate) * h + wcol[j] * x
                    p = rcol[j] * h
                    parts.append(p[:half] + p[half:])
                ys_o[pl.ds(at, 8), lanes] = fold(parts)
                h_s[b, :, lanes] = h
        return carry

    lax.fori_loop(0, tok // 8, chunk, 0)


def gate_kernel(plan, idx, u, xc, ys, small, *refs):
    n = plan.n_gathered()
    pieces = refs[:n]
    gated_o, zg_o, mine_o, send_o, g2, sem = refs[n:]
    copies = plan.fetch(idx, pieces, g2, sem)
    for copy in copies:
        copy.wait()
    inner = ys.shape[1]
    tok = mine_o.shape[0]
    zg = mm(u[...], g2[:, :inner])
    zg_o[...] = zg
    gated = (ys[...] + small[ROW_SKIP : ROW_SKIP + 1] * xc[...].astype(F32)) * (zg * sigmoid(zg))
    gated = gated.astype(BF16)
    gated_o[...] = gated
    branch = mm(gated, g2[:, inner:])
    mine_o[...] = branch[:tok]
    send_o[...] = branch[tok:]


def route_tables(lens, routes, experts, capacity, tok):
    _, valid = positions(lens, 0, tok)
    valid_f = valid.astype(F32)
    width = max(LANES, experts)
    hot = (routes == iota((tok, width), 1)).astype(F32)
    live = hot * valid_f
    earlier = (iota((tok, tok), 1) < iota((tok, tok), 0)).astype(F32).astype(BF16)
    before = mm(earlier, live.astype(BF16))
    rank = jnp.sum(before * hot, axis=1, keepdims=True).astype(jnp.int32)
    kept = valid & (rank < capacity)
    return valid_f, hot, rank, kept


def column_of(row):
    n = row.shape[1]
    square = iota((n, n), 0) == iota((n, n), 1)
    return jnp.sum(jnp.where(square, row[...].astype(F32), 0.0), axis=1, keepdims=True).astype(jnp.int32)


def slot_hot(k, routes, rank, kept, capacity, tok):
    inside = kept & (routes == k)
    return (inside & (rank == iota((tok, capacity), 1))).astype(F32).astype(BF16)


def moe_enter_kernel(experts, capacity, lens, tok, cot, routes, mine, got, dnat, disp_o, hidden_o, gate_o):
    rows, width = tok.shape
    routes = column_of(routes)
    hidden = tok[...].astype(F32) + (mine[...] + got[...])
    hidden_o[...] = hidden
    scale = lax.rsqrt(jnp.mean(hidden * hidden, axis=1, keepdims=True) + EPS)
    mv = (hidden * scale * dnat[1:2]).astype(BF16)
    logits = mm(mv, dnat[...].astype(BF16), NT)
    hot = (routes + 2 == iota(logits.shape, 1)).astype(F32)
    gate = sigmoid(jnp.sum(logits * hot, axis=1, keepdims=True))
    gate_o[...] = jnp.broadcast_to(gate, gate_o.shape)
    valid_f, _, rank, kept = route_tables(lens, routes, experts, capacity, rows)
    back = (cot[...].astype(F32) * valid_f * (gate * kept.astype(F32))).astype(BF16)
    both = jnp.concatenate([mv, back], axis=1)
    for k in range(experts):
        disp_o[k] = mm(slot_hot(k, routes, rank, kept, capacity, rows), both, TN).astype(BF16)


def fill_rows(groups, rows_s, both_s):
    at = 0
    for group in groups:
        for i in range(group.shape[0]):
            rows_s[at : at + group.shape[1]] = group[i].astype(F32)
            at += group.shape[1]
    both_s[...] = rows_s[...].astype(BF16)


def hidden_units(both_s, up, down):
    width = up.shape[1]
    pre = mm(both_s[:, :width], up, NT)
    g_act = mm(both_s[:, width:], down, NT)
    sq = pre * pre
    th = jnp.tanh(GELU_C * (pre + GELU_K * sq * pre))
    act = (0.5 * pre * (1.0 + th)).astype(BF16)
    slope = 0.5 * (1.0 + th) + 0.5 * pre * (1.0 - th * th) * (GELU_C * (1.0 + 3.0 * GELU_K * sq))
    return act, (g_act * slope).astype(BF16)


def expert_kernel(
    own, peer, up, down, up_a, up_b, down_a, down_b,
    out_own, out_peer, rows_s, both_s, acc_s, up_s, down_s, sem,
):
    copies = []
    for parts, held in (((up, up_a, up_b), up_s), ((down, down_a, down_b), down_s)):
        at = 0
        for part in parts:
            to = held.at[pl.ds(at, part.shape[1])]
            copies.append(pltpu.make_async_copy(part.at[0], to, sem.at[len(copies)]))
            at += part.shape[1]
    for copy in copies:
        copy.start()
    hidden = down.shape[1]
    count, capacity = own.shape[:2]
    fill_rows((own, peer), rows_s, both_s)
    width = own.shape[2] // 2
    part = 256
    for copy in copies:
        copy.wait()
    for f in range(0, 2 * hidden, part):
        span = slice(f, f + part)
        act, g_pre = hidden_units(both_s, up_s[span], down_s[span])
        e_part = mm(act, down_s[span])
        i_part = mm(g_pre, up_s[span])
        if f == 0:
            acc_s[:, :width] = e_part
            acc_s[:, width:] = i_part
        else:
            acc_s[:, :width] += e_part
            acc_s[:, width:] += i_part
    for i in range(count):
        out_own[i] = acc_s[i * capacity : (i + 1) * capacity]
        out_peer[i] = acc_s[(count + i) * capacity : (count + i + 1) * capacity].astype(BF16)


def expert_grad_kernel(own, peer, own_y, peer_y, up, down, up_g, down_g, rows_s, both_s):
    fill_rows((own, peer, own_y, peer_y), rows_s, both_s)
    width = own.shape[2] // 2
    part = 256
    for f in range(0, up.shape[1], part):
        span = slice(f, f + part)
        act, g_pre = hidden_units(both_s, up[0, span], down[0, span])
        down_g[0, span] = mm(act, both_s[:, width:], TN)
        up_g[0, span] = mm(g_pre, both_s[:, :width], TN)


def moe_leave_kernel(
    experts, capacity, lens, routes, cot, hidden, gate_in, dnat, back,
    out_o, ghid_o, gbr_o, dgrad_o,
):
    rows, width = hidden.shape
    routes = column_of(routes)
    valid_f, _, rank, kept = route_tables(lens, routes, experts, capacity, rows)
    kept_f = kept.astype(F32)
    gate = gate_in[:, 0:1]
    picked = jnp.zeros((rows, 2 * width), F32)
    for k in range(experts):
        picked = picked + mm(slot_hot(k, routes, rank, kept, capacity, rows), back[k])
    ex_out = picked[:, :width]
    sent = picked[:, width:]
    hid = hidden[...]
    out_o[...] = (valid_f * (hid + gate * ex_out)).astype(BF16)
    gy = cot[...].astype(F32) * valid_f
    g_gate = jnp.sum(gy * ex_out, axis=1, keepdims=True)
    chosen = g_gate * gate * (1.0 - gate)
    small_rows = dnat.shape[0]
    hot = (routes + 2 == iota((rows, small_rows), 1)).astype(F32)
    g_logit = (chosen * hot).astype(BF16)
    g_mv = mm(g_logit, dnat[...].astype(BF16)) + sent
    scale = lax.rsqrt(jnp.mean(hid * hid, axis=1, keepdims=True) + EPS)
    hat = hid * scale
    gain = dnat[1:2]
    mv = (hat * gain).astype(BF16)
    router_g = mm(g_logit, mv, TN)
    gain_g = jnp.sum(g_mv * hat, axis=0, keepdims=True)
    dgrad_o[...] = jnp.where(iota(dgrad_o.shape, 0) == 1, gain_g, router_g)
    gg = g_mv * gain
    mean = jnp.sum(gg * hat, axis=1, keepdims=True) * (1.0 / width)
    ghid = gy + scale * (gg - hat * mean)
    ghid_o[...] = ghid
    gbr_o[...] = ghid.astype(BF16)


def gate_back_kernel(plan, idx, gbr_a, gbr_b, g2, gated, xc, ys, zg, small, u, *refs):
    n = plan.n_shared()
    gy_o, gzg_o = refs[:2]
    shared = refs[2 : 2 + n]
    grad_s, sem = refs[2 + n :]
    inner = ys.shape[1]
    gbr = jnp.concatenate([gbr_a[...], gbr_b[...]], axis=0)
    g_gated = mm(gbr, g2[:, inner:], NT)
    skip = small[ROW_SKIP : ROW_SKIP + 1]
    sig = sigmoid(zg[...])
    gy_o[...] = g_gated * (zg[...] * sig)
    gzg = g_gated * (ys[...] + skip * xc[...].astype(F32)) * (sig * (1.0 + zg[...] * (1.0 - sig)))
    gzg = gzg.astype(BF16)
    gzg_o[...] = gzg
    grad_s[:, :inner] = mm(u[...], gzg, TN).astype(BF16)
    grad_s[:, inner:] = mm(gated[...], gbr, TN).astype(BF16)
    for copy in plan.emit(idx, grad_s, shared, sem):
        copy.wait()


def scan_back_kernel(
    rank, states, gy_s, xc, step_pre, sel, keep, small, g1sel, check,
    gsel_o, gxcs_o, gsr_o, q_o, smallg_o,
    dm_s, dx_s, gdx_s, gdl_s, wr_s, rd_s, gwr_s, grd_s, rate_s, lam_s, ga_s,
):
    rows, inner = gy_s.shape
    tok = rows // 2
    half = states // 2
    xcf = xc[...].astype(F32)
    skip = small[ROW_SKIP : ROW_SKIP + 1]
    delta = softplus(step_pre[...])
    dm_s[...] = jnp.where(keep[:, 0:1] > 0.0, delta, 1e30)
    dx_s[...] = delta * xcf
    for b in range(2):
        turned = jnp.transpose(sel[b * tok : (b + 1) * tok])
        wr_s[b] = turned[rank : rank + states]
        rd_s[b] = turned[rank + states : rank + 2 * states]
    rate_s[...] = jnp.exp(small[ROW_DECAY : ROW_DECAY + states]) * (-LOG2E)
    lam_s[...] = jnp.zeros_like(lam_s)
    ga_s[...] = jnp.zeros_like(ga_s)
    gwr_s[...] = jnp.zeros_like(gwr_s)
    grd_s[...] = jnp.zeros_like(grd_s)
    shape = (states, LANES)

    def chunk(i, carry):
        ci = tok // 8 - 1 - i
        t0 = pl.multiple_of(ci * 8, 8)
        for b in range(2):
            at = pl.multiple_of(b * tok + t0, 8)
            wr8 = pltpu.roll(wr_s[b], tok - t0, 1)
            rd8 = pltpu.roll(rd_s[b], tok - t0, 1)
            wcol = [jnp.broadcast_to(wr8[:, j : j + 1], shape) for j in range(8)]
            rcol = [jnp.broadcast_to(rd8[:, j : j + 1], shape) for j in range(8)]
            grd = [jnp.zeros(shape, F32)] * 8
            gwr = [jnp.zeros(shape, F32)] * 8
            for g in range(inner // LANES):
                lanes = slice(g * LANES, (g + 1) * LANES)
                h = check[ci * 2 + b, :, lanes]
                rate = rate_s[:, lanes]
                dm8 = dm_s[pl.ds(at, 8), lanes]
                dx8 = dx_s[pl.ds(at, 8), lanes]
                gy8 = gy_s[pl.ds(at, 8), lanes]
                decays, olds = [], []
                for j in range(8):
                    d = jnp.broadcast_to(dm8[j : j + 1], shape)
                    x = jnp.broadcast_to(dx8[j : j + 1], shape)
                    a = jnp.exp2(d * rate)
                    old = a * h
                    h = old + wcol[j] * x
                    grd[j] = grd[j] + h * jnp.broadcast_to(gy8[j : j + 1], shape)
                    decays.append(a)
                    olds.append(old)
                lam_in = lam_s[b, :, lanes]
                ga = ga_s[:, lanes]
                to_dx, to_dl = [None] * 8, [None] * 8
                for j in range(7, -1, -1):
                    lam = rcol[j] * jnp.broadcast_to(gy8[j : j + 1], shape) + lam_in
                    lam_in = decays[j] * lam
                    w = lam * olds[j]
                    ga = ga + w * jnp.broadcast_to(dm8[j : j + 1], shape)
                    p = lam * wcol[j]
                    to_dx[j] = p[:half] + p[half:]
                    p = w * rate
                    to_dl[j] = p[:half] + p[half:]
                    gwr[j] = gwr[j] + lam * jnp.broadcast_to(dx8[j : j + 1], shape)
                lam_s[b, :, lanes] = lam_in
                ga_s[:, lanes] = ga
                gdx_s[pl.ds(at, 8), lanes] = fold(to_dx)
                gdl_s[pl.ds(at, 8), lanes] = fold(to_dl)
            lane = iota(shape, 1)
            all_wr, all_rd = gwr_s[b], grd_s[b]
            for j in range(8):
                here = lane == t0 + j
                all_wr = jnp.where(here, jnp.sum(gwr[j], axis=1, keepdims=True), all_wr)
                all_rd = jnp.where(here, jnp.sum(grd[j], axis=1, keepdims=True), all_rd)
            gwr_s[b] = all_wr
            grd_s[b] = all_rd
        return carry

    lax.fori_loop(0, tok // 8, chunk, 0)
    delta = softplus(step_pre[...])
    gdx = gdx_s[...]
    xcf = xc[...].astype(F32)
    gy = gy_s[...]
    gxcs_o[...] = gy * skip + gdx * delta
    g_step = (gdx * xcf + LN2 * gdl_s[...]) * sigmoid(step_pre[...])
    gsr = g_step.astype(BF16)
    gsr_o[...] = gsr
    lane = iota((rows, LANES), 1)
    tail = LANES - rank
    q_o[...] = jnp.where(lane >= tail, pltpu.roll(sel[...], tail, 1), 0.0).astype(BF16)
    back = jnp.where(lane >= tail, mm(gsr, g1sel[...]), 0.0)
    back = pltpu.roll(back, rank, 1)
    zeros_top = jnp.zeros((rank, tok), F32)
    zeros_end = jnp.zeros((LANES - rank - 2 * states, tok), F32)
    for b in range(2):
        stack = jnp.concatenate([zeros_top, gwr_s[b], grd_s[b], zeros_end], axis=0)
        span = slice(b * tok, (b + 1) * tok)
        gsel_o[span] = back[span] + jnp.transpose(stack)
    smallg_o[0:ROW_STEP] = jnp.zeros((ROW_STEP, inner), F32)
    smallg_o[ROW_STEP : ROW_STEP + 1] = jnp.sum(g_step, axis=0, keepdims=True)
    smallg_o[ROW_SKIP : ROW_SKIP + 1] = jnp.sum(gy * xcf, axis=0, keepdims=True)
    smallg_o[ROW_SKIP + 1 : ROW_DECAY] = jnp.zeros((ROW_DECAY - ROW_SKIP - 1, inner), F32)
    smallg_o[ROW_DECAY : ROW_DECAY + states] = ga_s[...] * rate_s[...] * LN2
    rest = smallg_o.shape[0] - ROW_DECAY - states
    if rest:
        smallg_o[ROW_DECAY + states :] = jnp.zeros((rest, inner), F32)


def leave_kernel(
    plan, idx, lens, nat, gsel_a, gsel_b, gxcs, gsr, q, smallg, xin, xc, u, small, g1, dgrad, gxin_o, *refs
):
    n = plan.n_shared()
    shared = refs[:n]
    grad_s, sem = refs[n:]
    rows, inner = xin.shape
    tok = rows // 2
    perm = perm_matrix(idx, nat)
    g_sel = (gsel_a[...] + swap_halves(gsel_b[...])).astype(BF16)
    selblk = g1[:, inner : inner + LANES]
    block = mm(xc[...], g_sel, TN) + mm(gsr[...], q[...], TN)
    grad_s[:, inner : inner + LANES] = block.astype(BF16)
    g_xc = mm(g_sel, selblk, NT) + gxcs[...]
    offset = both_offsets(lens, tok)
    x = xin[...]
    sm = small[...]
    conv = conv_of(x, sm, offset)
    sig = sigmoid(conv)
    g_conv = g_xc * (sig * (1.0 + conv * (1.0 - sig)))
    g_xin = sm[3:4] * g_conv
    taps = [None, None, None, jnp.sum(g_conv * x, axis=0, keepdims=True)]
    for lag in range(1, 4):
        held = jnp.where(offset >= lag, g_conv, 0.0)
        g_xin = g_xin + sm[3 - lag : 4 - lag] * pltpu.roll(held, rows - lag, 0)
        taps[3 - lag] = jnp.sum(held * pltpu.roll(x, lag, 0), axis=0, keepdims=True)
    g_bias = jnp.sum(g_conv, axis=0, keepdims=True)
    g_xin = g_xin.astype(BF16)
    gxin_o[...] = g_xin
    grad_s[:, :inner] = mm(u[...], g_xin, TN).astype(BF16)
    dg = split_mm(dgrad[...], perm)
    top = jnp.concatenate(taps + [g_bias, jnp.zeros((3, inner), F32)], axis=0)
    gap = jnp.zeros((ROW_FEATURE - smallg.shape[0], inner), F32)
    end = jnp.zeros((LANES - ROW_FEATURE - dg.shape[0], inner), F32)
    table = jnp.concatenate([smallg[0:8] + top, smallg[8:], gap, dg, end], axis=0)
    grad_s[:, inner + LANES :] = jnp.transpose(table).astype(BF16)
    for copy in plan.emit(idx, grad_s, shared, sem):
        copy.wait()


def back_kernel(idx, nat, gxin, gzg, g1x, g2z, mine_o, send_o):
    tok = mine_o.shape[0]
    gn = mm(gxin[...], g1x[...], NT) + mm(gzg[...], g2z[...], NT)
    gn = split_mm(gn, perm_matrix(idx, nat), NT)
    mine_o[...] = gn[:tok]
    send_o[...] = gn[tok:]


def final_kernel(tok, mine, got, ghid, dnat, out_o):
    width = tok.shape[1]
    vals = tok[...].astype(F32)
    scale = lax.rsqrt(jnp.mean(vals * vals, axis=1, keepdims=True) + EPS)
    hat = vals * scale
    gg = (mine[...] + got[...]) * dnat[0:1]
    mean = jnp.sum(gg * hat, axis=1, keepdims=True) * (1.0 / width)
    out_o[...] = ghid[...] + scale * (gg - hat * mean)


def swap(values, axis):
    return lax.ppermute(values, axis, [(0, 1), (1, 0)])


def share_kernel(n1, n2, rank, states, *refs):
    one, two = refs[:n1], refs[n1 : n1 + n2]
    keep_o, send_o, outg_o, select_o, step_o, taps_o, cbias_o, sbias_o, skip_o, decay_o, square_s = refs[n1 + n2 :]
    er = outg_o.shape[0]
    dr = keep_o.shape[0]

    def total(parts):
        acc = parts[0][...].astype(F32)
        for part in parts[1:]:
            acc = acc + part[...].astype(F32)
        return acc

    x = total(one)
    inner = x.shape[1] - 2 * LANES
    z = total(two)
    for out, at in ((keep_o, 0), (send_o, dr)):
        out[:, :inner] = x[at : at + dr, :inner]
        out[:, inner : 2 * inner] = z[at : at + dr, :inner]
        out[:, 2 * inner :] = x[at : at + dr, inner + LANES :]
    outg_o[...] = z[:, inner:]
    select_o[...] = x[:, inner : inner + select_o.shape[1]]
    square_s[...] = jnp.zeros_like(square_s)
    square_s[:er] = x[:, inner : inner + LANES]
    step_o[...] = jnp.transpose(square_s[...])[LANES - rank :, :er]
    square_s[:er] = x[:, inner + LANES :]
    table = jnp.transpose(square_s[...])[:, :er]
    taps_o[...] = table[0:4]
    cbias_o[...] = table[ROW_BIAS : ROW_BIAS + 1]
    sbias_o[...] = table[ROW_STEP : ROW_STEP + 1]
    skip_o[...] = table[ROW_SKIP : ROW_SKIP + 1]
    decay_o[...] = table[ROW_DECAY : ROW_DECAY + states]


def spread_kernel(span, idx, keep, got, in_proj, norm, in_o, norm_o, moe_o, router_o, square_s):
    dr = keep.shape[0]
    inner2 = keep.shape[1] - LANES
    first = idx[3] == 0
    acc = jnp.zeros((dr, LANES), F32)
    for k in range(inner2 // span):
        mine = keep[:, k * span : (k + 1) * span]
        peer = got[:, k * span : (k + 1) * span]
        for at, part in ((2 * k * span, jnp.where(first, mine, peer)), ((2 * k + 1) * span, jnp.where(first, peer, mine))):
            in_o[:, at : at + span] = part
            terms = part * in_proj[:, at : at + span].astype(F32)
            for j in range(0, span, LANES):
                acc = acc + terms[:, j : j + LANES]
    table = keep[:, inner2:] + got[:, inner2:]
    at = ROW_FEATURE
    total = jnp.sum(acc, axis=1, keepdims=True)
    square_s[...] = jnp.zeros_like(square_s)
    square_s[:dr] = jnp.where(iota(table.shape, 1) == at, total, table)
    flat = jnp.transpose(square_s[...])[:, :dr]
    norm_o[...] = flat[at : at + 1] / norm[...].astype(F32)
    moe_o[...] = flat[at + 1 : at + 2]
    router_o[...] = flat[at + 2 : at + 2 + router_o.shape[0]]


def body(
    sizes,
    tokens,
    cotangent,
    seq_lens,
    routes,
    norm_gain,
    input_proj,
    conv_weight,
    conv_bias,
    select_proj,
    step_proj,
    step_bias,
    decay_log,
    skip_gain,
    output_proj,
    moe_gain,
    router_weight,
    up_weight,
    down_weight,
):
    ny, nz, nx = sizes
    nf = nz * nx
    ng = ny * nf
    tok, width = tokens.shape
    rank, er = step_proj.shape
    states = decay_log.shape[0]
    experts = router_weight.shape[1]
    capacity = 5 * tok // (4 * experts)
    dr = norm_gain.shape[0]
    inner = ng * er
    rows = 2 * tok
    small_n = -(-(ROW_DECAY + states) // 8) * 8
    dn = -(-(2 + experts) // 8) * 8
    plan = Plan(ny, nz, nx, er)
    idx = jnp.stack([lax.axis_index(a) for a in ("y", "z", "x", "c")]).astype(jnp.int32)

    order = np.arange(width).reshape(ny, 2, nf, dr).transpose(0, 2, 1, 3)
    nat = np.stack([order.reshape(width), order[:, :, ::-1].reshape(width)])
    nat = jnp.asarray(nat, jnp.int32)

    span = nf * er
    hid = up_weight.shape[1]
    first, second = hid // 2, hid // 6
    mine_w, send_w, ch, up_send = call(
        functools.partial(pack_kernel, span),
        [((dr, 2 * inner + LANES), BF16), ((dr, 2 * inner + LANES), BF16), ((er, 2 * LANES), BF16), ((1, first, width), BF16, HBM)],
        [idx]
        + [
            in_hbm(v)
            for v in (input_proj, norm_gain[None], moe_gain[None], router_weight.T, conv_weight, conv_bias[None], select_proj, step_proj, step_bias[None], decay_log, skip_gain[None], up_weight)
        ],
        [SMEM] + [None] * 11 + [HBM],
        scratch=[pltpu.VMEM((LANES, LANES), F32), pltpu.VMEM((LANES, LANES), F32), pltpu.SemaphoreType.DMA],
        name="pack",
        us=1,
    )
    got_w = swap(send_w, "c")
    group1, group2 = call(
        merge_kernel,
        [((er, inner + 2 * LANES), BF16), ((er, inner + width), BF16)],
        [mine_w, got_w, ch, output_proj],
        name="merge",
        us=1,
    )
    tok2 = jnp.concatenate([tokens, swap(tokens, "c")], axis=0)
    lens2 = jnp.concatenate([seq_lens, swap(seq_lens, "c")], axis=0)
    up_one = swap(up_send, "y")
    up_send, down_send, down_rest = call(
        split_kernel,
        [((1, hid - first, width), BF16, HBM), ((1, second, width), BF16, HBM), ((1, hid - second, width), BF16, HBM)],
        [in_hbm(up_weight), in_hbm(down_weight)],
        [HBM, HBM],
        scratch=[pltpu.SemaphoreType.DMA((3,))],
        name="split",
        us=2,
    )
    up_one = after(up_one, up_send)
    pieces1, pieces2 = plan.gather([group1, group2], up_one)
    fetch_sem = pltpu.SemaphoreType.DMA((ng,))
    emit_sem = pltpu.SemaphoreType.DMA((2 * ng,))
    u, xin, xc, selp, small_t, dnat, g1 = call(
        functools.partial(enter_kernel, plan),
        [((rows, width), BF16), kept((rows, inner), F32), ((rows, inner), BF16), ((rows, LANES), F32), ((small_n, inner), F32), kept((dn, width), F32), ((inner, inner + 2 * LANES), BF16)],
        [idx, lens2, tok2, nat] + pieces1,
        [SMEM, SMEM, None, None] + [HBM] * len(pieces1),
        scratch=[fetch_sem],
        name="enter",
    )
    selq = swap(selp, "c")
    middle = (pieces2[min(2, len(pieces2) - 1)], xc)
    up_two = swap(after(up_send, middle), "y")
    down_one = swap(after(down_send, middle), "y")
    down_two = swap(after(down_rest, (up_two, down_one)), "y")
    g1sel_spec = pl.BlockSpec((inner, LANES), lambda i: (0, inner // LANES))
    chunks = tok // 8
    ys, step_pre, sel, keep, check = call(
        functools.partial(scan_kernel, rank, states),
        [((rows, inner), F32), kept((rows, inner), F32), kept((rows, LANES), F32), kept((rows, LANES), F32), kept((2 * chunks, states, inner), F32)],
        [lens2, selp, selq, xc, g1, small_t],
        [SMEM, None, None, None, g1sel_spec, None],
        scratch=[pltpu.VMEM((rows, inner), F32), pltpu.VMEM((rows, inner), F32), pltpu.VMEM((2, states, tok), F32), pltpu.VMEM((2, states, tok), F32), pltpu.VMEM((states, inner), F32), pltpu.VMEM((2, states, inner), F32)],
        name="scan",
        us=9,
    )
    gated, zg, br_mine, br_send, g2 = call(
        functools.partial(gate_kernel, plan),
        [kept((rows, inner), BF16), kept((rows, inner), F32), ((tok, width), F32), ((tok, width), F32), ((inner, inner + width), BF16)],
        [idx, u, xc, ys, small_t] + pieces2,
        [SMEM] + [None] * 4 + [HBM] * len(pieces2),
        scratch=[fetch_sem],
        name="gate",
    )
    br_got = after(swap(br_send, "c"), (up_two, down_one))
    disp, hidden, gate = call(
        functools.partial(moe_enter_kernel, experts, capacity),
        [((experts, capacity, 2 * width), BF16), kept((tok, width), F32), kept((tok, LANES), F32)],
        [seq_lens, tokens, in_hbm(cotangent), routes.T, br_mine, br_got, in_hbm(dnat)],
        [SMEM] + [None] * 6,
        name="moe_enter",
    )
    line = lax.all_to_all(disp, ("z", "x"), split_axis=0, concat_axis=0, tiled=True)
    peer = swap(line, "c")
    line_y = swap(line, "y")
    peer_y = swap(line_y, "c")
    total = 2 * nf * capacity
    out_own, out_peer = call(
        expert_kernel,
        [(line.shape, F32), (line.shape, BF16)],
        [line, peer] + [in_hbm(w) for w in (up_weight, down_weight, up_one, up_two, down_one, down_two)],
        [None, None] + [HBM] * 6,
        scratch=[pltpu.VMEM((total, 2 * width), F32), pltpu.VMEM((total, 2 * width), BF16), pltpu.VMEM((total, 2 * width), F32), pltpu.VMEM((2 * hid, width), BF16), pltpu.VMEM((2 * hid, width), BF16), pltpu.SemaphoreType.DMA((6,))],
        name="expert",
        us=5,
    )
    up_grad, down_grad = call(
        expert_grad_kernel,
        [((1, hid, width), F32)] * 2,
        [line, peer, line_y, peer_y, in_hbm(up_weight), in_hbm(down_weight)],
        scratch=[pltpu.VMEM((2 * total, 2 * width), F32), pltpu.VMEM((2 * total, 2 * width), BF16)],
        name="expert_grad",
        us=7,
    )
    summed = (out_own + swap(after(out_peer, line_y), "c").astype(F32)).astype(BF16)
    back = lax.all_to_all(summed, ("z", "x"), split_axis=0, concat_axis=0, tiled=True)
    back = after(back, up_grad)
    result, ghid, gbr, dgrad = call(
        functools.partial(moe_leave_kernel, experts, capacity),
        [((tok, width), BF16), ((tok, width), F32), ((tok, width), BF16), ((dn, width), F32)],
        [in_hbm(seq_lens), in_hbm(routes.T), in_hbm(cotangent), in_hbm(hidden), in_hbm(gate), in_hbm(dnat), back],
        [SMEM] + [None] * 6,
        name="moe_leave",
    )
    gbr_got = swap(gbr, "c")
    gy, gzg, *shared2 = call(
        functools.partial(gate_back_kernel, plan),
        [((rows, inner), F32), ((rows, inner), BF16)] + plan.shared_outs(inner + width),
        [idx, gbr, gbr_got, g2, gated, xc, ys, zg, small_t, u],
        [SMEM] + [None] * 9,
        scratch=[pltpu.VMEM((inner, inner + width), BF16), emit_sem],
        name="gate_back",
    )
    gsel, gxcs, gsr, q, smallg = call(
        functools.partial(scan_back_kernel, rank, states),
        [((rows, LANES), F32), ((rows, inner), F32), ((rows, inner), BF16), ((rows, LANES), BF16), ((small_n, inner), F32)],
        [gy, xc, step_pre, sel, keep, small_t, g1, in_hbm(check)],
        [None] * 6 + [g1sel_spec, None],
        scratch=[pltpu.VMEM((rows, inner), F32)] * 4 + [pltpu.VMEM((2, states, tok), F32)] * 4 + [pltpu.VMEM((states, inner), F32), pltpu.VMEM((2, states, inner), F32), pltpu.VMEM((states, inner), F32)],
        name="scan_back",
        us=16,
    )
    shared2[-1] = after(shared2[-1], gsel)
    sums2 = plan.reduce1(shared2, "two")
    gsel = after(gsel, sums2[0])
    gsel_got = swap(gsel, "c")
    gxin, *shared1 = call(
        functools.partial(leave_kernel, plan),
        [((rows, inner), BF16)] + plan.shared_outs(inner + 2 * LANES),
        [idx, lens2, nat, gsel, gsel_got, gxcs, gsr, q, smallg, xin, xc, u, small_t, g1, dgrad],
        [SMEM, SMEM] + [None] * 13,
        scratch=[pltpu.VMEM((inner, inner + 2 * LANES), BF16), emit_sem],
        name="leave",
        us=5,
    )
    square_spec = pl.BlockSpec((inner, inner), lambda i: (0, 0))
    gn_mine, gn_send = call(
        back_kernel,
        [((tok, width), F32), ((tok, width), F32)],
        [idx, nat, gxin, gzg, g1, g2],
        [SMEM, None, None, None, square_spec, square_spec],
        name="back",
        us=3,
    )
    sums2 = plan.reduce2(sums2, "two")
    parts2 = plan.reduce3(sums2)
    shared1 = [after(part, sums2[0]) for part in shared1]
    sums1 = plan.reduce1(shared1, "one")
    if plan.fast:
        sums1[-1] = after(sums1[-1], tuple(parts2))
    parts1 = plan.reduce3(plan.reduce2(sums1, "one"))
    gn_got = swap(gn_send, "c")
    (input_grad,) = call(
        final_kernel, [((tok, width), F32)], [tokens, gn_mine, gn_got, ghid, dnat], name="final", us=2
    )
    sel_n = select_proj.shape[1]
    keep_w, send_back, out_grad, select_grad, step_grad, taps_grad, cb, sb, sk, decay_grad = call(
        functools.partial(share_kernel, len(parts1), len(parts2), rank, states),
        [((dr, 2 * inner + LANES), F32)] * 2
        + [((er, width), F32), ((er, sel_n), F32), ((rank, er), F32), ((4, er), F32), ((1, er), F32), ((1, er), F32), ((1, er), F32), ((states, er), F32)],
        list(parts1) + list(parts2),
        scratch=[pltpu.VMEM((LANES, LANES), F32)],
        name="share",
        us=1,
    )
    in_grad, norm_grad, moe_grad, router_grad = call(
        functools.partial(spread_kernel, span),
        [((dr, 4 * inner), F32), ((1, dr), F32), ((1, dr), F32), ((experts, dr), F32)],
        [idx, keep_w, swap(send_back, "c"), input_proj, norm_gain[None]],
        [SMEM, None, None, None, None],
        scratch=[pltpu.VMEM((LANES, LANES), F32)],
        name="spread",
        us=1,
    )
    return (
        result,
        input_grad,
        norm_grad[0],
        in_grad,
        taps_grad,
        cb[0],
        select_grad,
        step_grad,
        sb[0],
        decay_grad,
        sk[0],
        out_grad,
        moe_grad[0],
        router_grad.T,
        up_grad,
        down_grad,
    )


def solution(mesh):
    dp, fsdp = mesh.shape["dp"], mesh.shape["fsdp"]
    ny, nx = dp // 2, 2
    nz = fsdp // nx
    fine = Mesh(mesh.devices.reshape(ny, 2, nz, nx), ALL)
    tok = P(ALL, None)
    vec = P(ALL)
    col = P(None, ALL)
    exp = P(("z", "x"), ("y", "c"), None)
    in_specs = (tok, tok, tok, tok, vec, tok, col, vec, tok, col, vec, col, vec, tok, vec, tok, exp, exp)
    out_specs = (tok, tok, vec, tok, col, vec, tok, col, vec, col, vec, tok, vec, tok, exp, exp)
    return jax.shard_map(
        functools.partial(body, (ny, nz, nx)), mesh=fine, in_specs=in_specs, out_specs=out_specs, check_vma=False
    )
```

```python
import functools

import jax
import jax.numpy as jnp
import numpy as np
from jax import lax
from jax.experimental import pallas as pl
from jax.experimental.pallas import tpu as pltpu
from jax.sharding import Mesh
from jax.sharding import PartitionSpec as P

EPS = 1e-05
F32 = jnp.float32
BF16 = jnp.bfloat16
LANES = 128
LOG2E = 1.4426950408889634
LN2 = 0.6931471805599453
GELU_C = 0.7978845608028654
GELU_K = 0.044715
ALL = ("y", "c", "z", "x")
GROUP = ("y", "z", "x")
ROW_BIAS, ROW_STEP, ROW_SKIP, ROW_DECAY = 4, 5, 6, 8
ROW_FEATURE = 64
NN = (((1,), (0,)), ((), ()))
NT = (((1,), (1,)), ((), ()))
TN = (((0,), (0,)), ((), ()))


def mm(left, right, dims=NN):
    return lax.dot_general(left, right, dims, preferred_element_type=F32)


def split_mm(left, right, dims=NN):
    high = left.astype(BF16)
    rest = left - high.astype(F32)
    mid = rest.astype(BF16)
    low = (rest - mid.astype(F32)).astype(BF16)
    return mm(high, right, dims) + (mm(mid, right, dims) + mm(low, right, dims))


def iota(shape, dim):
    return lax.broadcasted_iota(jnp.int32, shape, dim)


def sigmoid(v):
    return 1.0 / (1.0 + jnp.exp(-v))


def softplus(v):
    return jnp.maximum(v, 0.0) + jnp.log1p(jnp.exp(-jnp.abs(v)))


def positions(lens_ref, row, tok):
    pos = iota((tok, 1), 0)
    end = jnp.int32(0)
    start = jnp.zeros((tok, 1), jnp.int32)
    for j in range(lens_ref.shape[1]):
        length = lens_ref[row, j]
        end = end + length
        start = start + jnp.where(pos >= end, length, 0)
    return pos - start, pos < end


def both_offsets(lens_ref, tok):
    return jnp.concatenate([positions(lens_ref, row, tok)[0] for row in range(2)], axis=0)


def fold(parts):
    rows = iota((8, LANES), 0)
    step = 1
    while len(parts) > 1:
        first = (rows & step) == 0
        merged = []
        for k in range(0, len(parts), 2):
            a, b = parts[k], parts[k + 1]
            merged.append(jnp.where(first, a, b) + pltpu.roll(jnp.where(first, b, a), step, 0))
        parts = merged
        step *= 2
    return parts[0]


def call(kernel, outs, args, specs=None, scratch=(), name=None, us=5, vmem=32):
    whole = pl.BlockSpec(memory_space=pltpu.VMEM)
    specs = [None] * len(args) if specs is None else specs
    windowed = any(s is not None and s.block_shape is not None for s in specs)
    results = pl.pallas_call(
        kernel,
        grid=(1,) if windowed else (),
        out_shape=[(pltpu.HBM if len(o) > 3 else jax.ShapeDtypeStruct)(o[0], o[1]) for o in outs],
        in_specs=[whole if s is None else s for s in specs],
        out_specs=[whole if len(o) < 3 or o[2] is None else o[2] for o in outs],
        scratch_shapes=list(scratch),
        name=name,
        cost_estimate=pl.CostEstimate(flops=us * 300000000, bytes_accessed=us * 900000, transcendentals=0),
        compiler_params=pltpu.CompilerParams(vmem_limit_bytes=vmem << 20),
    )(*args)
    return list(results)


SMEM = pl.BlockSpec(memory_space=pltpu.SMEM)
HBM = pl.BlockSpec(memory_space=pl.ANY)


def perm_matrix(idx, nat_ref):
    width = nat_ref.shape[1]
    nat = jnp.where(idx[3] == 0, nat_ref[0:1], nat_ref[1:2])
    return (iota((width, width), 0) == nat).astype(F32).astype(BF16)


def kept(shape, dtype):
    return (shape, dtype, None, True)


def in_hbm(value):
    return pltpu.with_memory_space_constraint(value, pltpu.HBM)


def after(value, other):
    if other is None:
        return value
    return lax.optimization_barrier((value, other))[0]


class Plan:
    def __init__(self, ny, nz, nx, piece):
        self.ny, self.nz, self.nx, self.piece = ny, nz, nx, piece
        self.count = ny * nz * nx
        self.fast = (ny, nz, nx) == (2, 4, 2) and piece % 16 == 0

    def place(self, idx, yr, zr, xr):
        y = jnp.bitwise_xor(idx[0], yr)
        x = jnp.bitwise_xor(idx[2], xr)
        z = lax.rem(idx[1] - zr + self.nz, self.nz)
        return pl.multiple_of(((y * self.nz + z) * self.nx + x) * self.piece, self.piece)

    def gather(self, groups, first):
        if not self.fast:
            return [[lax.all_gather(piece, GROUP, axis=0, tiled=True)] for piece in groups]
        half = 2 * self.piece
        out, before_line, before_last = [], None, None
        for piece in groups:
            piece = after(piece, before_line)
            rots = [lax.ppermute(piece, "z", [(i, (i + k) % 4) for i in range(4)]) for k in (1, 2, 3)]
            line = jnp.concatenate([piece] + rots, axis=0)
            line = after(line, first if before_line is None else before_last)
            before_line = line
            by_x, by_y = swap(line, "x"), swap(line, "y")
            out.append([line, by_x, by_y, swap(by_x[:half], "y"), swap(by_y[half:], "x")])
            before_last = tuple(out[-1][3:])
        return out

    def pieces(self):
        n, out = self.piece, []
        for z in range(4):
            out.append((0, z * n, 0, z, 0))
            out.append((1, z * n, 0, z, 1))
            out.append((2, z * n, 1, z, 0))
            out.append((3 + z // 2, z % 2 * n, 1, z, 1))
        return out

    def n_gathered(self):
        return 5 if self.fast else 1

    def fetch(self, idx, refs, dst, sem):
        if not self.fast:
            copies = [pltpu.make_async_copy(refs[0], dst, sem.at[0])]
        else:
            copies = []
            for k, (r, row, yr, zr, xr) in enumerate(self.pieces()):
                to = dst.at[pl.ds(self.place(idx, yr, zr, xr), self.piece)]
                copies.append(pltpu.make_async_copy(refs[r].at[pl.ds(row, self.piece)], to, sem.at[k]))
        for copy in copies:
            copy.start()
        return copies

    def shared_outs(self, width):
        if not self.fast:
            return [((self.count * self.piece, width), BF16, HBM)]
        return [((8 * self.piece, width // 2), BF16, HBM)] * 4

    def n_shared(self):
        return 4 if self.fast else 1

    def emit(self, idx, src, refs, sem):
        if not self.fast:
            copies = [pltpu.make_async_copy(src, refs[0], sem.at[0])]
        else:
            copies, n, half = [], self.piece, src.shape[1] // 2
            for zr in range(4):
                for yr in range(2):
                    for xr in range(2):
                        at = self.place(idx, yr, zr, xr)
                        for lanes, ref, row in (
                            (0, refs[2 - 2 * xr], yr * 4 + zr),
                            (half, refs[3 - 2 * yr], xr * 4 + zr),
                        ):
                            copies.append(
                                pltpu.make_async_copy(
                                    src.at[pl.ds(at, n), pl.ds(lanes, half)],
                                    ref.at[pl.ds(row * n, n)],
                                    sem.at[len(copies)],
                                )
                            )
        for copy in copies:
            copy.start()
        return copies

    def reduce1(self, shared, tag):
        if not self.fast:
            return shared
        a_send, b_send, a_keep, b_keep = shared
        n, half = self.piece, a_send.shape[1]
        a_got, b_got = swap(a_send, "x"), swap(b_send, "y")
        shape = ((4 * n, half), BF16)
        return call(add_kernel, [shape] * 4, [a_keep, a_got, b_keep, b_got], name="add1_" + tag, us=1)

    def reduce2(self, sums, tag):
        if not self.fast:
            return sums
        a_send, a_keep, b_send, b_keep = sums
        n, half = self.piece, a_send.shape[1]
        a_got, b_got = swap(a_send, "y"), swap(b_send, "x")
        outs = [((n, 2 * half), BF16)] * 4
        return call(line_kernel, outs, [a_keep, a_got, b_keep, b_got], name="add2_" + tag, us=1)

    def reduce3(self, parts):
        if not self.fast:
            shares = parts[0].reshape(self.count, self.piece, -1)
            shares = lax.all_to_all(shares, GROUP, split_axis=0, concat_axis=0, tiled=True)
            return [shares.astype(F32).sum(axis=0)]
        rots = [lax.ppermute(parts[k], "z", [(i, (i - k) % 4) for i in range(4)]) for k in (1, 2, 3)]
        return [parts[0]] + rots


def add_kernel(a, a_in, b, b_in, a_send, a_keep, b_send, b_keep):
    cut = a_send.shape[0]
    for one, two, send, keep in ((a, a_in, a_send, a_keep), (b, b_in, b_send, b_keep)):
        send[...] = (one[cut:].astype(F32) + two[cut:].astype(F32)).astype(BF16)
        keep[...] = (one[:cut].astype(F32) + two[:cut].astype(F32)).astype(BF16)


def line_kernel(a, a_in, b, b_in, *outs):
    n, half = outs[0].shape[0], a.shape[1]
    for k, out in enumerate(outs):
        span = slice(k * n, (k + 1) * n)
        out[:, :half] = (a[span].astype(F32) + a_in[span].astype(F32)).astype(BF16)
        out[:, half:] = (b[span].astype(F32) + b_in[span].astype(F32)).astype(BF16)


def pack_kernel(
    span, idx, in_proj, norm, moe, router, taps, cbias, select, step, sbias, decay, skip, up,
    mine_o, send_o, ch_o, up_o, rows_s, block_s, sem,
):
    copy = pltpu.make_async_copy(up.at[0, pl.ds(0, up_o.shape[0])], up_o, sem)
    copy.start()
    dr = in_proj.shape[0]
    er, sel_n = select.shape
    rank, states = step.shape[0], decay.shape[0]
    inner2 = mine_o.shape[1] - LANES
    first = idx[3] == 0
    for k in range(inner2 // span):
        low = in_proj[:, 2 * k * span : (2 * k + 1) * span]
        high = in_proj[:, (2 * k + 1) * span : (2 * k + 2) * span]
        mine_o[:, k * span : (k + 1) * span] = jnp.where(first, low, high)
        send_o[:, k * span : (k + 1) * span] = jnp.where(first, high, low)
    rows_s[...] = jnp.zeros_like(rows_s)
    rows_s[0:4, :er] = taps[...].astype(F32)
    rows_s[ROW_BIAS : ROW_BIAS + 1, :er] = cbias[...].astype(F32)
    rows_s[ROW_STEP : ROW_STEP + 1, :er] = sbias[...].astype(F32)
    rows_s[ROW_SKIP : ROW_SKIP + 1, :er] = skip[...].astype(F32)
    rows_s[ROW_DECAY : ROW_DECAY + states, :er] = decay[...].astype(F32)
    ch_o[:, LANES:] = jnp.transpose(rows_s[...])[:er].astype(BF16)
    rows_s[...] = jnp.zeros_like(rows_s)
    rows_s[LANES - rank :, :er] = step[...].astype(F32)
    block_s[...] = jnp.zeros_like(block_s)
    block_s[:er, :sel_n] = select[...].astype(F32)
    ch_o[:, :LANES] = (block_s[:er] + jnp.transpose(rows_s[...])[:er]).astype(BF16)
    rows_s[...] = jnp.zeros_like(rows_s)
    rows_s[ROW_FEATURE : ROW_FEATURE + 1, :dr] = norm[...].astype(F32)
    rows_s[ROW_FEATURE + 1 : ROW_FEATURE + 2, :dr] = moe[...].astype(F32)
    rows_s[ROW_FEATURE + 2 : ROW_FEATURE + 2 + router.shape[0], :dr] = router[...].astype(F32)
    feature = jnp.transpose(rows_s[...])[:dr].astype(BF16)
    mine_o[:, inner2:] = feature
    send_o[:, inner2:] = feature
    copy.wait()


def cut_rows(sizes, hidden):
    parts, at = [], 0
    for size in sizes:
        spans, end = [], at + size
        if at < hidden:
            spans.append((0, at, 0, min(end, hidden) - at))
        if end > hidden:
            low = max(at, hidden)
            spans.append((1, low - hidden, low - at, end - low))
        parts.append(spans)
        at = end
    return parts


def split_kernel(parts, up, down, *refs):
    outs, sem = refs[:-1], refs[-1]
    copies = []
    for spans, out in zip(parts, outs, strict=True):
        for which, row, at, size in spans:
            source = (up, down)[which].at[0, pl.ds(row, size)]
            copies.append(pltpu.make_async_copy(source, out.at[pl.ds(at, size)], sem.at[len(copies)]))
    for copy in copies:
        copy.start()
    for copy in copies:
        copy.wait()


def merge_kernel(mine, got, ch, out_proj, one_o, two_o):
    inner = out_proj.shape[1]
    both = jnp.concatenate([mine[...].astype(F32), got[...].astype(F32)], axis=0).astype(BF16)
    one_o[:, :inner] = both[:, :inner]
    one_o[:, inner : inner + LANES] = ch[:, :LANES]
    one_o[:, inner + LANES :] = ch[:, LANES:] + both[:, 2 * inner :]
    two_o[:, :inner] = both[:, inner : 2 * inner]
    two_o[:, inner:] = out_proj[...]


def enter_kernel(plan, idx, lens, tok2, nat, *refs):
    n = plan.n_gathered()
    pieces = refs[:n]
    u_o, xin_o, xc_o, sel_o, small_o, dnat_o, g1, sem = refs[n:]
    copies = plan.fetch(idx, pieces, g1, sem)
    rows, width = tok2.shape
    tok = rows // 2
    inner = xin_o.shape[1]
    perm = perm_matrix(idx, nat)
    vals = tok2[...].astype(F32)
    scale = lax.rsqrt(jnp.mean(vals * vals, axis=1, keepdims=True) + EPS)
    offset = both_offsets(lens, tok)
    for copy in copies:
        copy.wait()
    table = g1[:, inner + LANES :]
    dnat = mm(table, perm, (((0,), (1,)), ((), ())))[ROW_FEATURE:]
    dnat_o[...] = dnat[: dnat_o.shape[0]]
    u = (vals * scale * dnat[0:1]).astype(BF16)
    u = mm(u, perm).astype(BF16)
    u_o[...] = u
    xin = mm(u, g1[:, :inner])
    xin_o[...] = xin
    small = jnp.transpose(table.astype(F32))[: small_o.shape[0]]
    small_o[...] = small
    conv = conv_of(xin, small, offset)
    xc = (conv * sigmoid(conv)).astype(BF16)
    xc_o[...] = xc
    sel_o[...] = mm(xc, g1[:, inner : inner + LANES])


def conv_of(xin, small, offset):
    conv = small[ROW_BIAS : ROW_BIAS + 1] + small[3:4] * xin
    for lag in range(1, 4):
        moved = pltpu.roll(xin, lag, 0)
        conv = conv + jnp.where(offset >= lag, small[3 - lag : 4 - lag] * moved, 0.0)
    return conv


def swap_halves(rows):
    half = rows.shape[0] // 2
    return jnp.concatenate([rows[half:], rows[:half]], axis=0)


GROUP_TOKENS = 16


def spread_rows(sel, first, states):
    rows, n = sel.shape[0], GROUP_TOKENS
    wide = (LANES, n * states)
    pick = (iota(wide, 0) == first + iota(wide, 1) % states).astype(F32).astype(BF16)
    values = split_mm(sel, pick)
    own = iota((rows, n * states), 1) // states == iota((rows, n * states), 0) % n
    values = jnp.where(own, values, 0.0).reshape(rows // n, n, n * states)
    high = values.astype(BF16).astype(F32)
    return jnp.concatenate([high, values - high], axis=1).astype(BF16)


def two_terms(block):
    high = block.astype(BF16).astype(F32)
    return jnp.concatenate([high, block - high], axis=0).astype(BF16)


def halves(block):
    n = block.shape[0] // 2
    return block[:n] + block[n:]


def scan_kernel(
    rank, states, lens, sel_a, sel_b, xc, g1sel, small,
    ys_o, step_o, sel_o, keep_o, check_o,
    dm_s, dx_s, wr_s, rd_s, rate_s, h_s,
):
    rows, inner = ys_o.shape
    tok = rows // 2
    sel = sel_a[...] + swap_halves(sel_b[...])
    sel_o[...] = sel
    lane = iota((rows, LANES), 1)
    tail = LANES - rank
    q = jnp.where(lane >= tail, pltpu.roll(sel, tail, 1), 0.0).astype(BF16)
    step_pre = mm(q, g1sel[...], NT) + small[ROW_STEP : ROW_STEP + 1]
    step_o[...] = step_pre
    delta = softplus(step_pre)
    offset = both_offsets(lens, tok)
    xcf = xc[...].astype(F32)
    dm_s[...] = jnp.where(offset > 0, delta, 1e30)
    keep_o[...] = jnp.broadcast_to((offset > 0).astype(F32), keep_o.shape)
    dx_s[...] = delta * xcf
    for b in range(2):
        turned = jnp.transpose(sel[b * tok : (b + 1) * tok])
        wr_s[b] = turned[rank : rank + states]
        rd_s[b] = turned[rank + states : rank + 2 * states]
    rate_s[...] = jnp.exp(small[ROW_DECAY : ROW_DECAY + states]) * (-LOG2E)
    h_s[...] = jnp.zeros_like(h_s)
    half = states // 2

    def chunk(ci, carry):
        t0 = pl.multiple_of(ci * 8, 8)
        for b in range(2):
            at = pl.multiple_of(b * tok + t0, 8)
            wr8 = pltpu.roll(wr_s[b], tok - t0, 1)
            rd8 = pltpu.roll(rd_s[b], tok - t0, 1)
            wcol = [jnp.broadcast_to(wr8[:, j : j + 1], (states, LANES)) for j in range(8)]
            rcol = [jnp.broadcast_to(rd8[:, j : j + 1], (states, LANES)) for j in range(8)]
            for g in range(inner // LANES):
                lanes = slice(g * LANES, (g + 1) * LANES)
                h = h_s[b, :, lanes]
                check_o[ci * 2 + b, :, lanes] = h
                rate = rate_s[:, lanes]
                dm8 = dm_s[pl.ds(at, 8), lanes]
                dx8 = dx_s[pl.ds(at, 8), lanes]
                parts = []
                for j in range(8):
                    d = jnp.broadcast_to(dm8[j : j + 1], (states, LANES))
                    x = jnp.broadcast_to(dx8[j : j + 1], (states, LANES))
                    h = jnp.exp2(d * rate) * h + wcol[j] * x
                    p = rcol[j] * h
                    parts.append(p[:half] + p[half:])
                ys_o[pl.ds(at, 8), lanes] = fold(parts)
                h_s[b, :, lanes] = h
        return carry

    lax.fori_loop(0, tok // 8, chunk, 0)


def gate_kernel(plan, idx, u, xc, ys, small, *refs):
    n = plan.n_gathered()
    pieces = refs[:n]
    gated_o, zg_o, mine_o, send_o, g2, sem = refs[n:]
    copies = plan.fetch(idx, pieces, g2, sem)
    for copy in copies:
        copy.wait()
    inner = ys.shape[1]
    tok = mine_o.shape[0]
    zg = mm(u[...], g2[:, :inner])
    zg_o[...] = zg
    gated = (ys[...] + small[ROW_SKIP : ROW_SKIP + 1] * xc[...].astype(F32)) * (zg * sigmoid(zg))
    gated = gated.astype(BF16)
    gated_o[...] = gated
    branch = mm(gated, g2[:, inner:])
    mine_o[...] = branch[:tok]
    send_o[...] = branch[tok:]


def route_tables(lens, routes, experts, capacity, tok):
    _, valid = positions(lens, 0, tok)
    valid_f = valid.astype(F32)
    width = max(LANES, experts)
    hot = (routes == iota((tok, width), 1)).astype(F32)
    live = hot * valid_f
    earlier = (iota((tok, tok), 1) < iota((tok, tok), 0)).astype(F32).astype(BF16)
    before = mm(earlier, live.astype(BF16))
    rank = jnp.sum(before * hot, axis=1, keepdims=True).astype(jnp.int32)
    kept = valid & (rank < capacity)
    return valid_f, hot, rank, kept


def column_of(row):
    n = row.shape[1]
    square = iota((n, n), 0) == iota((n, n), 1)
    return jnp.sum(jnp.where(square, row[...].astype(F32), 0.0), axis=1, keepdims=True).astype(jnp.int32)


class Slots:
    def __init__(self, capacity, width):
        self.full, left = divmod(capacity, 8)
        self.split = 0 < left <= 4
        if left > 4:
            self.full += 1
        self.width = width
        self.lanes = self.full * width + (width // 2 if self.split else 0)

    def rows(self, groups):
        return groups * 8 * self.full + (groups * 4 if self.split else 0)

    def hot(self, routes, rank, kept, experts, first, low, high):
        shape = (rank.shape[0], 8 * experts)
        place = iota(shape, 1)
        row = place % 8
        inside = kept & (routes == place // 8) & (rank == first + row - low)
        return jnp.where(inside & (row >= low) & (row < high), 1.0, 0.0).astype(BF16)

    def hots(self, routes, rank, kept, experts):
        args = (routes, rank, kept, experts)
        whole = [self.hot(*args, 8 * i, 0, 8) for i in range(self.full)]
        last = [self.hot(*args, 8 * self.full, 4 * i, 4 * i + 4) for i in range(2)] if self.split else []
        return whole, last

    def unpack(self, groups, both, tail_s):
        at, width, height = 0, self.width, groups[0].shape[0]
        for group in groups:
            for i in range(self.full):
                both[at : at + height] = group[:, i * width : (i + 1) * width]
                at += height
        if self.split:
            half, start, count = width // 2, 0, height // 8
            for group in groups:
                block = group[:, self.full * width :].astype(F32)
                for k in range(count):
                    tail_s[start + 4 * k : start + 4 * k + 4, :half] = block[8 * k : 8 * k + 4]
                    tail_s[start + 4 * k : start + 4 * k + 4, half:] = block[8 * k + 4 : 8 * k + 8]
                start += 4 * count
            both[at : at + start] = tail_s[:start].astype(BF16)

    def pack(self, rows, which, count, out, tail_s):
        width, height = self.width, out.shape[0]
        at = which * self.full * height
        for i in range(self.full):
            out[:, i * width : (i + 1) * width] = rows[at : at + height].astype(out.dtype)
            at += height
        if self.split:
            half = width // 2
            at = count * self.full * height + which * height // 2
            for k in range(height // 8):
                tail_s[8 * k : 8 * k + 4, :half] = rows[at + 4 * k : at + 4 * k + 4, :half]
                tail_s[8 * k + 4 : 8 * k + 8, :half] = rows[at + 4 * k : at + 4 * k + 4, half:]
            out[:, self.full * width :] = tail_s[:height, :half].astype(out.dtype)


def moe_enter_kernel(slots, experts, capacity, lens, tok, cot, routes, mine, got, dnat, disp_o, hidden_o, gate_o):
    rows, width = tok.shape
    routes = column_of(routes)
    hidden = tok[...].astype(F32) + (mine[...] + got[...])
    hidden_o[...] = hidden
    scale = lax.rsqrt(jnp.mean(hidden * hidden, axis=1, keepdims=True) + EPS)
    mv = (hidden * scale * dnat[1:2]).astype(BF16)
    logits = mm(mv, dnat[...].astype(BF16), NT)
    hot = (routes + 2 == iota(logits.shape, 1)).astype(F32)
    gate = sigmoid(jnp.sum(logits * hot, axis=1, keepdims=True))
    gate_o[...] = jnp.broadcast_to(gate, gate_o.shape)
    valid_f, _, rank, kept = route_tables(lens, routes, experts, capacity, rows)
    back = (cot[...].astype(F32) * valid_f * (gate * kept.astype(F32))).astype(BF16)
    both = jnp.concatenate([mv, back], axis=1)
    whole, last = slots.hots(routes, rank, kept, experts)
    span = slots.width
    for i, hot in enumerate(whole):
        disp_o[:, i * span : (i + 1) * span] = mm(hot, both, TN).astype(BF16)
    if last:
        end = mm(last[0], both[:, : span // 2], TN) + mm(last[1], both[:, span // 2 :], TN)
        disp_o[:, slots.full * span :] = end.astype(BF16)


def half_units(both, up, span):
    width = up.shape[1]
    pre = mm(both[:, :width], up[span], NT)
    sq = pre * pre
    th = jnp.tanh(GELU_C * (pre + GELU_K * sq * pre))
    act = (0.5 * pre * (1.0 + th)).astype(BF16)
    return act, 0.5 * (1.0 + th) + 0.5 * pre * (1.0 - th * th) * (GELU_C * (1.0 + 3.0 * GELU_K * sq))


def moves_of(parts, refs, targets, which_of):
    moves = []
    for spans, ref in zip(parts, refs, strict=True):
        for which, row, at, size in spans:
            if which in which_of:
                moves.append((ref.at[pl.ds(at, size)], targets[which].at[pl.ds(row, size)]))
    return moves


PART = 256


def expert_own_kernel(slots, parts, own, peer, up, down, *refs):
    others = refs[: len(parts)]
    both, acc, act_o, slope_o, up_o, up_s, down_s, tail_s, sem = refs[len(parts) :]
    moves = [(up.at[0], up_s), (down.at[0], down_s)] + moves_of(parts, others, (up_o, None), (0,))
    copies = [pltpu.make_async_copy(a, b, sem.at[k]) for k, (a, b) in enumerate(moves)]
    for copy in copies:
        copy.start()
    slots.unpack((own, peer), both, tail_s)
    width = up.shape[2]
    for copy in copies:
        copy.wait()
    for f in range(0, up_s.shape[0], PART):
        span = slice(f, f + PART)
        act, slope = half_units(both, up_s, span)
        g_pre = (mm(both[:, width:], down_s[span], NT) * slope).astype(BF16)
        e_part = mm(act, down_s[span])
        i_part = mm(g_pre, up_s[span])
        if f == 0:
            acc[:, :width] = e_part
            acc[:, width:] = i_part
        else:
            acc[:, :width] += e_part
            acc[:, width:] += i_part
        act, slope = half_units(both, up_o, span)
        act_o[:, span] = act
        slope_o[:, span] = slope


def expert_other_kernel(slots, parts, both, acc, act, slope, up, *refs):
    others = refs[: len(parts)]
    out_own, out_peer, acc_s, down_s, tail_s, sem = refs[len(parts) :]
    moves = moves_of(parts, others, (None, down_s), (1,))
    copies = [pltpu.make_async_copy(a, b, sem.at[k]) for k, (a, b) in enumerate(moves)]
    for copy in copies:
        copy.start()
    width = up.shape[1]
    for copy in copies:
        copy.wait()
    for f in range(0, up.shape[0], PART):
        span = slice(f, f + PART)
        g_pre = (mm(both[:, width:], down_s[span], NT) * slope[:, span]).astype(BF16)
        e_part = mm(act[:, span], down_s[span])
        i_part = mm(g_pre, up[span])
        old = acc if f == 0 else acc_s
        acc_s[:, :width] = old[:, :width] + e_part
        acc_s[:, width:] = old[:, width:] + i_part
    slots.pack(acc_s, 1, 2, out_peer, tail_s)
    slots.pack(acc_s, 0, 2, out_own, tail_s)


def unit_grads(both, up, down, up_g, down_g, more):
    width = up.shape[2]
    for f in range(0, up.shape[1], PART):
        span = slice(f, f + PART)
        act, slope = half_units(both, up.at[0], span)
        g_pre = (mm(both[:, width:], down[0, span], NT) * slope).astype(BF16)
        to_down = mm(act, both[:, width:], TN)
        to_up = mm(g_pre, both[:, :width], TN)
        if more is not None:
            to_up, to_down = to_up + more[0][0, span], to_down + more[1][0, span]
        down_g[0, span] = to_down
        up_g[0, span] = to_up


def near_grad_kernel(both, up, down, up_g, down_g):
    unit_grads(both, up, down, up_g, down_g, None)


def far_grad_kernel(slots, own_y, peer_y, up, down, up_near, down_near, up_g, down_g, both_s, tail_s):
    slots.unpack((own_y, peer_y), both_s, tail_s)
    unit_grads(both_s, up, down, up_g, down_g, (up_near, down_near))


def moe_leave_kernel(
    slots, experts, capacity, lens, routes, cot, hidden, gate_in, dnat, back,
    out_o, ghid_o, gbr_o, dgrad_o,
):
    rows, width = hidden.shape
    routes = column_of(routes)
    valid_f, _, rank, kept = route_tables(lens, routes, experts, capacity, rows)
    kept_f = kept.astype(F32)
    gate = gate_in[:, 0:1]
    whole, last = slots.hots(routes, rank, kept, experts)
    span = slots.width
    picked = jnp.zeros((rows, 2 * width), F32)
    for i, hot in enumerate(whole):
        picked = picked + mm(hot, back[:, i * span : (i + 1) * span])
    if last:
        end = back[:, slots.full * span :]
        picked = picked + jnp.concatenate([mm(last[0], end), mm(last[1], end)], axis=1)
    ex_out = picked[:, :width]
    sent = picked[:, width:]
    hid = hidden[...]
    out_o[...] = (valid_f * (hid + gate * ex_out)).astype(BF16)
    gy = cot[...].astype(F32) * valid_f
    g_gate = jnp.sum(gy * ex_out, axis=1, keepdims=True)
    chosen = g_gate * gate * (1.0 - gate)
    small_rows = dnat.shape[0]
    hot = (routes + 2 == iota((rows, small_rows), 1)).astype(F32)
    g_logit = (chosen * hot).astype(BF16)
    g_mv = mm(g_logit, dnat[...].astype(BF16)) + sent
    scale = lax.rsqrt(jnp.mean(hid * hid, axis=1, keepdims=True) + EPS)
    hat = hid * scale
    gain = dnat[1:2]
    mv = (hat * gain).astype(BF16)
    router_g = mm(g_logit, mv, TN)
    gain_g = jnp.sum(g_mv * hat, axis=0, keepdims=True)
    dgrad_o[...] = jnp.where(iota(dgrad_o.shape, 0) == 1, gain_g, router_g)
    gg = g_mv * gain
    mean = jnp.sum(gg * hat, axis=1, keepdims=True) * (1.0 / width)
    ghid = gy + scale * (gg - hat * mean)
    ghid_o[...] = ghid
    gbr_o[...] = ghid.astype(BF16)


def gate_back_kernel(plan, idx, gbr_a, gbr_b, g2, gated, xc, ys, zg, small, u, *refs):
    n = plan.n_shared()
    gy_o, gzg_o = refs[:2]
    shared = refs[2 : 2 + n]
    grad_s, sem = refs[2 + n :]
    inner = ys.shape[1]
    gbr = jnp.concatenate([gbr_a[...], gbr_b[...]], axis=0)
    g_gated = mm(gbr, g2[:, inner:], NT)
    skip = small[ROW_SKIP : ROW_SKIP + 1]
    sig = sigmoid(zg[...])
    gy_o[...] = g_gated * (zg[...] * sig)
    gzg = g_gated * (ys[...] + skip * xc[...].astype(F32)) * (sig * (1.0 + zg[...] * (1.0 - sig)))
    gzg = gzg.astype(BF16)
    gzg_o[...] = gzg
    grad_s[:, :inner] = mm(u[...], gzg, TN).astype(BF16)
    grad_s[:, inner:] = mm(gated[...], gbr, TN).astype(BF16)
    for copy in plan.emit(idx, grad_s, shared, sem):
        copy.wait()


def scan_back_kernel(
    rank, states, gy_s, xc, step_pre, sel, keep, small, g1sel, check,
    gsel_o, gxcs_o, gsr_o, q_o, smallg_o,
    dm_s, dx_s, gdx_s, gdl_s, wr_s, rd_s, gwr_s, grd_s, rate_s, lam_s, ga_s, write_s, hb_s, lb_s, wb_s,
):
    rows, inner = gy_s.shape
    tok = rows // 2
    xcf = xc[...].astype(F32)
    skip = small[ROW_SKIP : ROW_SKIP + 1]
    delta = softplus(step_pre[...])
    dm_s[...] = jnp.where(keep[:, 0:1] > 0.0, delta, 1e30)
    dx_s[...] = delta * xcf
    for b in range(2):
        turned = jnp.transpose(sel[b * tok : (b + 1) * tok])
        wr_s[b] = turned[rank : rank + states]
        rd_s[b] = turned[rank + states : rank + 2 * states]
    rate_s[...] = jnp.exp(small[ROW_DECAY : ROW_DECAY + states]) * (-LOG2E)
    lam_s[...] = jnp.zeros_like(lam_s)
    ga_s[...] = jnp.zeros_like(ga_s)
    write_s[...] = spread_rows(sel[...], rank, states)
    shape = (states, LANES)
    n = GROUP_TOKENS
    count = tok // n
    wide = (n, n * states)
    own = iota(wide, 1) // states == iota(wide, 0)
    group = own.astype(F32).astype(BF16)
    for ref in (hb_s, lb_s, wb_s):
        ref[...] = jnp.zeros_like(ref)

    def sums(b, ci):
        span = pl.ds(pl.multiple_of(b * tok + ci * n, n), n)
        gdx_s[span, :] = halves(mm(write_s[b * count + ci], lb_s[b]))
        gdl_s[span, :] = mm(group, wb_s[b])
        grd_s[span, :] = jnp.where(own, halves(mm(two_terms(gy_s[span, :]), hb_s[b], NT)), 0.0)
        gwr_s[span, :] = jnp.where(own, halves(mm(two_terms(dx_s[span, :]), lb_s[b], NT)), 0.0)

    def chunk(i, carry):
        ci = count - 1 - i
        sums(1, jnp.minimum(ci + 1, count - 1))
        for b in range(2):
            for part in range(n // 8 - 1, -1, -1):
                t0 = pl.multiple_of(ci * n + part * 8, 8)
                at = pl.multiple_of(b * tok + t0, 8)
                wr8 = pltpu.roll(wr_s[b], tok - t0, 1)
                rd8 = pltpu.roll(rd_s[b], tok - t0, 1)
                wcol = [jnp.broadcast_to(wr8[:, j : j + 1], shape) for j in range(8)]
                rcol = [jnp.broadcast_to(rd8[:, j : j + 1], shape) for j in range(8)]
                for g in range(inner // LANES):
                    lanes = slice(g * LANES, (g + 1) * LANES)
                    h = check[(ci * (n // 8) + part) * 2 + b, :, lanes]
                    rate = rate_s[:, lanes]
                    dm8 = dm_s[pl.ds(at, 8), lanes]
                    dx8 = dx_s[pl.ds(at, 8), lanes]
                    gy8 = gy_s[pl.ds(at, 8), lanes]
                    decays, olds = [], []
                    for j in range(8):
                        k = part * 8 + j
                        d = jnp.broadcast_to(dm8[j : j + 1], shape)
                        x = jnp.broadcast_to(dx8[j : j + 1], shape)
                        a = jnp.exp2(d * rate)
                        old = a * h
                        h = old + wcol[j] * x
                        hb_s[b, k * states : (k + 1) * states, lanes] = h.astype(BF16)
                        decays.append(a)
                        olds.append(old)
                    lam_in = lam_s[b, :, lanes]
                    ga = ga_s[:, lanes]
                    for j in range(7, -1, -1):
                        k = part * 8 + j
                        lam = rcol[j] * jnp.broadcast_to(gy8[j : j + 1], shape) + lam_in
                        lam_in = decays[j] * lam
                        w = lam * olds[j]
                        ga = ga + w * jnp.broadcast_to(dm8[j : j + 1], shape)
                        lb_s[b, k * states : (k + 1) * states, lanes] = lam.astype(BF16)
                        wb_s[b, k * states : (k + 1) * states, lanes] = (w * rate).astype(BF16)
                    lam_s[b, :, lanes] = lam_in
                    ga_s[:, lanes] = ga
            if b == 0:
                sums(0, ci)
        return carry

    lax.fori_loop(0, count, chunk, 0)
    sums(1, 0)
    delta = softplus(step_pre[...])
    gdx = gdx_s[...]
    xcf = xc[...].astype(F32)
    gy = gy_s[...]
    gxcs_o[...] = gy * skip + gdx * delta
    g_step = (gdx * xcf + LN2 * gdl_s[...]) * sigmoid(step_pre[...])
    gsr = g_step.astype(BF16)
    gsr_o[...] = gsr
    lane = iota((rows, LANES), 1)
    tail = LANES - rank
    q_o[...] = jnp.where(lane >= tail, pltpu.roll(sel[...], tail, 1), 0.0).astype(BF16)
    back = jnp.where(lane >= tail, mm(gsr, g1sel[...]), 0.0)
    back = pltpu.roll(back, rank, 1)
    tall = (n * states, LANES)
    place = iota(tall, 0) % states
    to_wr = (iota(tall, 1) == rank + place).astype(F32).astype(BF16)
    to_rd = (iota(tall, 1) == rank + states + place).astype(F32).astype(BF16)
    gsel_o[...] = back + split_mm(gwr_s[...], to_wr) + split_mm(grd_s[...], to_rd)
    smallg_o[0:ROW_STEP] = jnp.zeros((ROW_STEP, inner), F32)
    smallg_o[ROW_STEP : ROW_STEP + 1] = jnp.sum(g_step, axis=0, keepdims=True)
    smallg_o[ROW_SKIP : ROW_SKIP + 1] = jnp.sum(gy * xcf, axis=0, keepdims=True)
    smallg_o[ROW_SKIP + 1 : ROW_DECAY] = jnp.zeros((ROW_DECAY - ROW_SKIP - 1, inner), F32)
    smallg_o[ROW_DECAY : ROW_DECAY + states] = ga_s[...] * rate_s[...] * LN2
    rest = smallg_o.shape[0] - ROW_DECAY - states
    if rest:
        smallg_o[ROW_DECAY + states :] = jnp.zeros((rest, inner), F32)


def leave_kernel(
    plan, idx, lens, nat, gsel_a, gsel_b, gxcs, gsr, q, smallg, xin, xc, u, small, g1, dgrad, gxin_o, *refs
):
    n = plan.n_shared()
    shared = refs[:n]
    grad_s, sem = refs[n:]
    rows, inner = xin.shape
    tok = rows // 2
    perm = perm_matrix(idx, nat)
    g_sel = (gsel_a[...] + swap_halves(gsel_b[...])).astype(BF16)
    selblk = g1[:, inner : inner + LANES]
    block = mm(xc[...], g_sel, TN) + mm(gsr[...], q[...], TN)
    grad_s[:, inner : inner + LANES] = block.astype(BF16)
    g_xc = mm(g_sel, selblk, NT) + gxcs[...]
    offset = both_offsets(lens, tok)
    x = xin[...]
    sm = small[...]
    conv = conv_of(x, sm, offset)
    sig = sigmoid(conv)
    g_conv = g_xc * (sig * (1.0 + conv * (1.0 - sig)))
    g_xin = sm[3:4] * g_conv
    taps = [None, None, None, jnp.sum(g_conv * x, axis=0, keepdims=True)]
    for lag in range(1, 4):
        held = jnp.where(offset >= lag, g_conv, 0.0)
        g_xin = g_xin + sm[3 - lag : 4 - lag] * pltpu.roll(held, rows - lag, 0)
        taps[3 - lag] = jnp.sum(held * pltpu.roll(x, lag, 0), axis=0, keepdims=True)
    g_bias = jnp.sum(g_conv, axis=0, keepdims=True)
    g_xin = g_xin.astype(BF16)
    gxin_o[...] = g_xin
    grad_s[:, :inner] = mm(u[...], g_xin, TN).astype(BF16)
    dg = split_mm(dgrad[...], perm)
    top = jnp.concatenate(taps + [g_bias, jnp.zeros((3, inner), F32)], axis=0)
    gap = jnp.zeros((ROW_FEATURE - smallg.shape[0], inner), F32)
    end = jnp.zeros((LANES - ROW_FEATURE - dg.shape[0], inner), F32)
    table = jnp.concatenate([smallg[0:8] + top, smallg[8:], gap, dg, end], axis=0)
    grad_s[:, inner + LANES :] = jnp.transpose(table).astype(BF16)
    for copy in plan.emit(idx, grad_s, shared, sem):
        copy.wait()


def back_kernel(idx, nat, gxin, gzg, g1x, g2z, mine_o, send_o):
    tok = mine_o.shape[0]
    gn = mm(gxin[...], g1x[...], NT) + mm(gzg[...], g2z[...], NT)
    gn = split_mm(gn, perm_matrix(idx, nat), NT)
    mine_o[...] = gn[:tok]
    send_o[...] = gn[tok:]


def final_kernel(tok, mine, got, ghid, dnat, out_o):
    width = tok.shape[1]
    vals = tok[...].astype(F32)
    scale = lax.rsqrt(jnp.mean(vals * vals, axis=1, keepdims=True) + EPS)
    hat = vals * scale
    gg = (mine[...] + got[...]) * dnat[0:1]
    mean = jnp.sum(gg * hat, axis=1, keepdims=True) * (1.0 / width)
    out_o[...] = ghid[...] + scale * (gg - hat * mean)


def swap(values, axis):
    return lax.ppermute(values, axis, [(0, 1), (1, 0)])


def exchange(rows, count):
    parts = rows.reshape(count, 8, rows.shape[1])
    parts = lax.all_to_all(parts, ("z", "x"), split_axis=0, concat_axis=0, tiled=True)
    return parts.reshape(rows.shape)


def share_kernel(n1, n2, rank, states, *refs):
    one, two = refs[:n1], refs[n1 : n1 + n2]
    keep_o, send_o, outg_o, select_o, step_o, taps_o, cbias_o, sbias_o, skip_o, decay_o, square_s = refs[n1 + n2 :]
    er = outg_o.shape[0]
    dr = keep_o.shape[0]

    def total(parts):
        acc = parts[0][...].astype(F32)
        for part in parts[1:]:
            acc = acc + part[...].astype(F32)
        return acc

    x = total(one)
    inner = x.shape[1] - 2 * LANES
    z = total(two)
    for out, at in ((keep_o, 0), (send_o, dr)):
        out[:, :inner] = x[at : at + dr, :inner]
        out[:, inner : 2 * inner] = z[at : at + dr, :inner]
        out[:, 2 * inner :] = x[at : at + dr, inner + LANES :]
    outg_o[...] = z[:, inner:]
    select_o[...] = x[:, inner : inner + select_o.shape[1]]
    square_s[...] = jnp.zeros_like(square_s)
    square_s[:er] = x[:, inner : inner + LANES]
    step_o[...] = jnp.transpose(square_s[...])[LANES - rank :, :er]
    square_s[:er] = x[:, inner + LANES :]
    table = jnp.transpose(square_s[...])[:, :er]
    taps_o[...] = table[0:4]
    cbias_o[...] = table[ROW_BIAS : ROW_BIAS + 1]
    sbias_o[...] = table[ROW_STEP : ROW_STEP + 1]
    skip_o[...] = table[ROW_SKIP : ROW_SKIP + 1]
    decay_o[...] = table[ROW_DECAY : ROW_DECAY + states]


def spread_kernel(span, idx, keep, got, in_proj, norm, in_o, norm_o, moe_o, router_o, square_s):
    dr = keep.shape[0]
    inner2 = keep.shape[1] - LANES
    first = idx[3] == 0
    acc = jnp.zeros((dr, LANES), F32)
    for k in range(inner2 // span):
        mine = keep[:, k * span : (k + 1) * span]
        peer = got[:, k * span : (k + 1) * span]
        for at, part in ((2 * k * span, jnp.where(first, mine, peer)), ((2 * k + 1) * span, jnp.where(first, peer, mine))):
            in_o[:, at : at + span] = part
            terms = part * in_proj[:, at : at + span].astype(F32)
            for j in range(0, span, LANES):
                acc = acc + terms[:, j : j + LANES]
    table = keep[:, inner2:] + got[:, inner2:]
    at = ROW_FEATURE
    total = jnp.sum(acc, axis=1, keepdims=True)
    square_s[...] = jnp.zeros_like(square_s)
    square_s[:dr] = jnp.where(iota(table.shape, 1) == at, total, table)
    flat = jnp.transpose(square_s[...])[:, :dr]
    norm_o[...] = flat[at : at + 1] / norm[...].astype(F32)
    moe_o[...] = flat[at + 1 : at + 2]
    router_o[...] = flat[at + 2 : at + 2 + router_o.shape[0]]


def body(
    sizes,
    tokens,
    cotangent,
    seq_lens,
    routes,
    norm_gain,
    input_proj,
    conv_weight,
    conv_bias,
    select_proj,
    step_proj,
    step_bias,
    decay_log,
    skip_gain,
    output_proj,
    moe_gain,
    router_weight,
    up_weight,
    down_weight,
):
    ny, nz, nx = sizes
    nf = nz * nx
    ng = ny * nf
    tok, width = tokens.shape
    rank, er = step_proj.shape
    states = decay_log.shape[0]
    experts = router_weight.shape[1]
    capacity = 5 * tok // (4 * experts)
    dr = norm_gain.shape[0]
    inner = ng * er
    rows = 2 * tok
    small_n = -(-(ROW_DECAY + states) // 8) * 8
    dn = -(-(2 + experts) // 8) * 8
    plan = Plan(ny, nz, nx, er)
    idx = jnp.stack([lax.axis_index(a) for a in ("y", "z", "x", "c")]).astype(jnp.int32)

    order = np.arange(width).reshape(ny, 2, nf, dr).transpose(0, 2, 1, 3)
    nat = np.stack([order.reshape(width), order[:, :, ::-1].reshape(width)])
    nat = jnp.asarray(nat, jnp.int32)

    span = nf * er
    hid = up_weight.shape[1]
    sizes = [hid * 26 // 48, hid * 28 // 48]
    sizes.append(2 * hid - sum(sizes))
    parts = cut_rows(sizes, hid)
    mine_w, send_w, ch, up_send = call(
        functools.partial(pack_kernel, span),
        [((dr, 2 * inner + LANES), BF16), ((dr, 2 * inner + LANES), BF16), ((er, 2 * LANES), BF16), ((sizes[0], width), BF16)],
        [idx]
        + [
            in_hbm(v)
            for v in (input_proj, norm_gain[None], moe_gain[None], router_weight.T, conv_weight, conv_bias[None], select_proj, step_proj, step_bias[None], decay_log, skip_gain[None], up_weight)
        ],
        [SMEM] + [None] * 11 + [HBM],
        scratch=[pltpu.VMEM((LANES, LANES), F32), pltpu.VMEM((LANES, LANES), F32), pltpu.SemaphoreType.DMA],
        name="pack",
        us=1,
    )
    got_w = swap(send_w, "c")
    group1, group2 = call(
        merge_kernel,
        [((er, inner + 2 * LANES), BF16), ((er, inner + width), BF16)],
        [mine_w, got_w, ch, output_proj],
        name="merge",
        us=1,
    )
    tok2 = jnp.concatenate([tokens, swap(tokens, "c")], axis=0)
    lens2 = jnp.concatenate([seq_lens, swap(seq_lens, "c")], axis=0)
    up_one = swap(up_send, "y")
    sends = call(
        functools.partial(split_kernel, parts[1:]),
        [((size, width), BF16) for size in sizes[1:]],
        [in_hbm(after(up_weight, group1)), in_hbm(down_weight)],
        [HBM, HBM],
        scratch=[pltpu.SemaphoreType.DMA((2 * len(sizes),))],
        name="split",
        us=2,
    )
    up_one = after(up_one, sends[0])
    pieces1, pieces2 = plan.gather([group1, group2], (up_one, tok2, lens2))

    fetch_sem = pltpu.SemaphoreType.DMA((ng,))
    emit_sem = pltpu.SemaphoreType.DMA((2 * ng,))
    u, xin, xc, selp, small_t, dnat, g1 = call(
        functools.partial(enter_kernel, plan),
        [((rows, width), BF16), kept((rows, inner), F32), ((rows, inner), BF16), ((rows, LANES), F32), ((small_n, inner), F32), kept((dn, width), F32), ((inner, inner + 2 * LANES), BF16)],
        [idx, lens2, tok2, nat] + pieces1,
        [SMEM, SMEM, None, None] + [HBM] * len(pieces1),
        scratch=[fetch_sem],
        name="enter",
    )
    selq = swap(selp, "c")
    middle = (pieces2[min(2, len(pieces2) - 1)], xc)
    part_two = swap(after(sends[0], middle), "y")
    part_three = swap(after(sends[1], middle), "y")
    g1sel_spec = pl.BlockSpec((inner, LANES), lambda i: (0, inner // LANES))
    chunks = tok // 8
    ys, step_pre, sel, keep, check = call(
        functools.partial(scan_kernel, rank, states),
        [((rows, inner), F32), kept((rows, inner), F32), kept((rows, LANES), F32), kept((rows, LANES), F32), kept((2 * chunks, states, inner), F32)],
        [lens2, selp, selq, xc, g1, small_t],
        [SMEM, None, None, None, g1sel_spec, None],
        scratch=[pltpu.VMEM((rows, inner), F32), pltpu.VMEM((rows, inner), F32), pltpu.VMEM((2, states, tok), F32), pltpu.VMEM((2, states, tok), F32), pltpu.VMEM((states, inner), F32), pltpu.VMEM((2, states, inner), F32)],
        name="scan",
        us=9,
    )
    gated, zg, br_mine, br_send, g2 = call(
        functools.partial(gate_kernel, plan),
        [kept((rows, inner), BF16), kept((rows, inner), F32), ((tok, width), F32), ((tok, width), F32), ((inner, inner + width), BF16)],
        [idx, u, xc, ys, small_t] + pieces2,
        [SMEM] + [None] * 4 + [HBM] * len(pieces2),
        scratch=[fetch_sem],
        name="gate",
    )
    br_got = swap(br_send, "c")
    slots = Slots(capacity, 2 * width)
    disp, hidden, gate = call(
        functools.partial(moe_enter_kernel, slots, experts, capacity),
        [kept((8 * experts, slots.lanes), BF16), kept((tok, width), F32), kept((tok, LANES), F32)],
        [seq_lens, tokens, in_hbm(cotangent), routes.T, br_mine, br_got, in_hbm(dnat)],
        [SMEM] + [None] * 6,
        name="moe_enter",
    )
    disp = after(disp, part_two)
    line = exchange(disp, nf)
    peer = swap(line, "c")
    line_y = swap(line, "y")
    total = slots.rows(2 * nf)
    tail = max(slots.rows(2 * nf), 8)
    weight_s = pltpu.VMEM((hid, width), BF16)
    tail_s = pltpu.VMEM((tail, 2 * width), F32)
    early = sum(1 for spans in parts for span in spans if span[0] == 0)
    both, acc, act, slope, up_near = call(
        functools.partial(expert_own_kernel, slots, parts[:-1]),
        [((total, 2 * width), BF16), ((total, 2 * width), F32), ((total, hid), BF16), ((total, hid), F32), ((hid, width), BF16)],
        [line, peer, in_hbm(up_weight), in_hbm(down_weight), up_one, part_two],
        [None, None] + [HBM] * 4,
        scratch=[weight_s, weight_s, tail_s, pltpu.SemaphoreType.DMA((2 + early,))],
        name="expert_own",
        us=6,
    )
    out_own, out_peer = call(
        functools.partial(expert_other_kernel, slots, parts[1:]),
        [(line.shape, F32), (line.shape, BF16)],
        [both, acc, act, slope, up_near, part_two, part_three],
        [None] * 5 + [HBM] * 2,
        scratch=[pltpu.VMEM((total, 2 * width), F32), weight_s, tail_s, pltpu.SemaphoreType.DMA((3,))],
        name="expert_other",
        us=3,
    )
    grads = [((1, hid, width), F32)] * 2
    weights = [in_hbm(up_weight), in_hbm(down_weight)]
    near = call(near_grad_kernel, grads, [both] + weights, name="near_grad", us=4)
    peer_y = swap(after(line_y, near[0]), "c")
    up_grad, down_grad = call(
        functools.partial(far_grad_kernel, slots),
        grads,
        [line_y, peer_y] + weights + near,
        scratch=[pltpu.VMEM((total, 2 * width), BF16), tail_s],
        name="far_grad",
        us=8,
    )
    summed = (out_own + swap(out_peer, "c").astype(F32)).astype(BF16)
    back = exchange(summed, nf)
    back = after(back, up_grad)
    result, ghid, gbr, dgrad = call(
        functools.partial(moe_leave_kernel, slots, experts, capacity),
        [((tok, width), BF16), ((tok, width), F32), ((tok, width), BF16), ((dn, width), F32)],
        [in_hbm(seq_lens), in_hbm(routes.T), in_hbm(cotangent), in_hbm(hidden), in_hbm(gate), in_hbm(dnat), back],
        [SMEM] + [None] * 6,
        name="moe_leave",
    )
    gbr_got = swap(gbr, "c")
    gy, gzg, *shared2 = call(
        functools.partial(gate_back_kernel, plan),
        [((rows, inner), F32), ((rows, inner), BF16)] + plan.shared_outs(inner + width),
        [idx, gbr, gbr_got, g2, gated, xc, ys, zg, small_t, u],
        [SMEM] + [None] * 9,
        scratch=[pltpu.VMEM((inner, inner + width), BF16), emit_sem],
        name="gate_back",
    )
    gsel, gxcs, gsr, q, smallg = call(
        functools.partial(scan_back_kernel, rank, states),
        [((rows, LANES), F32), ((rows, inner), F32), ((rows, inner), BF16), ((rows, LANES), BF16), ((small_n, inner), F32)],
        [gy, xc, step_pre, sel, keep, small_t, g1, in_hbm(check)],
        [None] * 6 + [g1sel_spec, None],
        scratch=[pltpu.VMEM((rows, inner), F32)] * 4 + [pltpu.VMEM((2, states, tok), F32)] * 2 + [pltpu.VMEM((rows, GROUP_TOKENS * states), F32)] * 2 + [pltpu.VMEM((states, inner), F32), pltpu.VMEM((2, states, inner), F32), pltpu.VMEM((states, inner), F32), pltpu.VMEM((rows // GROUP_TOKENS, 2 * GROUP_TOKENS, GROUP_TOKENS * states), BF16)] + [pltpu.VMEM((2, GROUP_TOKENS * states, inner), BF16)] * 3,
        name="scan_back",
        us=16,
    )
    shared2[-1] = after(shared2[-1], gsel)
    sums2 = plan.reduce1(shared2, "two")
    gsel = after(gsel, sums2[0])
    gsel_got = swap(gsel, "c")
    gxin, *shared1 = call(
        functools.partial(leave_kernel, plan),
        [((rows, inner), BF16)] + plan.shared_outs(inner + 2 * LANES),
        [idx, lens2, nat, gsel, gsel_got, gxcs, gsr, q, smallg, xin, xc, u, small_t, g1, dgrad],
        [SMEM, SMEM] + [None] * 13,
        scratch=[pltpu.VMEM((inner, inner + 2 * LANES), BF16), emit_sem],
        name="leave",
        us=5,
    )
    square_spec = pl.BlockSpec((inner, inner), lambda i: (0, 0))
    gn_mine, gn_send = call(
        back_kernel,
        [((tok, width), F32), ((tok, width), F32)],
        [idx, nat, gxin, gzg, g1, g2],
        [SMEM, None, None, None, square_spec, square_spec],
        name="back",
        us=3,
    )
    sums2 = plan.reduce2(sums2, "two")
    parts2 = plan.reduce3(sums2)
    shared1 = [after(part, sums2[0]) for part in shared1]
    sums1 = plan.reduce1(shared1, "one")
    if plan.fast:
        sums1[-1] = after(sums1[-1], tuple(parts2))
    parts1 = plan.reduce3(plan.reduce2(sums1, "one"))
    gn_got = swap(gn_send, "c")
    (input_grad,) = call(
        final_kernel, [((tok, width), F32)], [tokens, gn_mine, gn_got, ghid, dnat], name="final", us=2
    )
    sel_n = select_proj.shape[1]
    keep_w, send_back, out_grad, select_grad, step_grad, taps_grad, cb, sb, sk, decay_grad = call(
        functools.partial(share_kernel, len(parts1), len(parts2), rank, states),
        [((dr, 2 * inner + LANES), F32)] * 2
        + [((er, width), F32), ((er, sel_n), F32), ((rank, er), F32), ((4, er), F32), ((1, er), F32), ((1, er), F32), ((1, er), F32), ((states, er), F32)],
        list(parts1) + list(parts2),
        scratch=[pltpu.VMEM((LANES, LANES), F32)],
        name="share",
        us=1,
    )
    in_grad, norm_grad, moe_grad, router_grad = call(
        functools.partial(spread_kernel, span),
        [((dr, 4 * inner), F32), ((1, dr), F32), ((1, dr), F32), ((experts, dr), F32)],
        [idx, keep_w, swap(send_back, "c"), input_proj, norm_gain[None]],
        [SMEM, None, None, None, None],
        scratch=[pltpu.VMEM((LANES, LANES), F32)],
        name="spread",
        us=1,
    )
    return (
        result,
        input_grad,
        norm_grad[0],
        in_grad,
        taps_grad,
        cb[0],
        select_grad,
        step_grad,
        sb[0],
        decay_grad,
        sk[0],
        out_grad,
        moe_grad[0],
        router_grad.T,
        up_grad,
        down_grad,
    )


def solution(mesh):
    dp, fsdp = mesh.shape["dp"], mesh.shape["fsdp"]
    ny, nx = dp // 2, 2
    nz = fsdp // nx
    fine = Mesh(mesh.devices.reshape(ny, 2, nz, nx), ALL)
    tok = P(ALL, None)
    vec = P(ALL)
    col = P(None, ALL)
    exp = P(("z", "x"), ("y", "c"), None)
    in_specs = (tok, tok, tok, tok, vec, tok, col, vec, tok, col, vec, col, vec, tok, vec, tok, exp, exp)
    out_specs = (tok, tok, vec, tok, col, vec, tok, col, vec, col, vec, tok, vec, tok, exp, exp)
    return jax.shard_map(
        functools.partial(body, (ny, nz, nx)), mesh=fine, in_specs=in_specs, out_specs=out_specs, check_vma=False
    )
```

```python
import functools

import jax
import jax.numpy as jnp
import numpy as np
from jax import lax
from jax.experimental import pallas as pl
from jax.experimental.pallas import tpu as pltpu
from jax.sharding import Mesh
from jax.sharding import PartitionSpec as P

EPS = 1e-05
F32 = jnp.float32
BF16 = jnp.bfloat16
LANES = 128
LOG2E = 1.4426950408889634
LN2 = 0.6931471805599453
GELU_C = 0.7978845608028654
GELU_K = 0.044715
ALL = ("y", "c", "z", "x")
GROUP = ("y", "z", "x")
ROW_BIAS, ROW_STEP, ROW_SKIP, ROW_DECAY = 4, 5, 6, 8
ROW_FEATURE = 64
NN = (((1,), (0,)), ((), ()))
NT = (((1,), (1,)), ((), ()))
TN = (((0,), (0,)), ((), ()))


def mm(left, right, dims=NN):
    return lax.dot_general(left, right, dims, preferred_element_type=F32)


def split_mm(left, right, dims=NN):
    high = left.astype(BF16)
    rest = left - high.astype(F32)
    mid = rest.astype(BF16)
    low = (rest - mid.astype(F32)).astype(BF16)
    return mm(high, right, dims) + (mm(mid, right, dims) + mm(low, right, dims))


def iota(shape, dim):
    return lax.broadcasted_iota(jnp.int32, shape, dim)


def sigmoid(v):
    return 1.0 / (1.0 + jnp.exp(-v))


def softplus(v):
    return jnp.maximum(v, 0.0) + jnp.log1p(jnp.exp(-jnp.abs(v)))


def positions(lens_ref, row, tok):
    pos = iota((tok, 1), 0)
    end = jnp.int32(0)
    start = jnp.zeros((tok, 1), jnp.int32)
    for j in range(lens_ref.shape[1]):
        length = lens_ref[row, j]
        end = end + length
        start = start + jnp.where(pos >= end, length, 0)
    return pos - start, pos < end


def both_offsets(lens_ref, tok):
    return jnp.concatenate([positions(lens_ref, row, tok)[0] for row in range(2)], axis=0)


def fold(parts):
    rows = iota((8, LANES), 0)
    step = 1
    while len(parts) > 1:
        first = (rows & step) == 0
        merged = []
        for k in range(0, len(parts), 2):
            a, b = parts[k], parts[k + 1]
            merged.append(jnp.where(first, a, b) + pltpu.roll(jnp.where(first, b, a), step, 0))
        parts = merged
        step *= 2
    return parts[0]


def call(kernel, outs, args, specs=None, scratch=(), name=None, us=5, vmem=32):
    whole = pl.BlockSpec(memory_space=pltpu.VMEM)
    specs = [None] * len(args) if specs is None else specs
    windowed = any(s is not None and s.block_shape is not None for s in specs)
    results = pl.pallas_call(
        kernel,
        grid=(1,) if windowed else (),
        out_shape=[(pltpu.HBM if len(o) > 3 else jax.ShapeDtypeStruct)(o[0], o[1]) for o in outs],
        in_specs=[whole if s is None else s for s in specs],
        out_specs=[whole if len(o) < 3 or o[2] is None else o[2] for o in outs],
        scratch_shapes=list(scratch),
        name=name,
        cost_estimate=pl.CostEstimate(flops=us * 300000000, bytes_accessed=us * 900000, transcendentals=0),
        compiler_params=pltpu.CompilerParams(vmem_limit_bytes=vmem << 20),
    )(*args)
    return list(results)


SMEM = pl.BlockSpec(memory_space=pltpu.SMEM)
HBM = pl.BlockSpec(memory_space=pl.ANY)


def perm_matrix(idx, nat_ref):
    width = nat_ref.shape[1]
    nat = jnp.where(idx[3] == 0, nat_ref[0:1], nat_ref[1:2])
    return (iota((width, width), 0) == nat).astype(F32).astype(BF16)


def kept(shape, dtype):
    return (shape, dtype, None, True)


def in_hbm(value):
    return pltpu.with_memory_space_constraint(value, pltpu.HBM)


def after(value, other):
    if other is None:
        return value
    return lax.optimization_barrier((value, other))[0]


class Plan:
    def __init__(self, ny, nz, nx, piece):
        self.ny, self.nz, self.nx, self.piece = ny, nz, nx, piece
        self.count = ny * nz * nx
        self.fast = (ny, nz, nx) == (2, 4, 2) and piece % 16 == 0

    def place(self, idx, yr, zr, xr):
        y = jnp.bitwise_xor(idx[0], yr)
        x = jnp.bitwise_xor(idx[2], xr)
        z = lax.rem(idx[1] - zr + self.nz, self.nz)
        return pl.multiple_of(((y * self.nz + z) * self.nx + x) * self.piece, self.piece)

    def gather(self, groups, first):
        if not self.fast:
            return [[lax.all_gather(piece, GROUP, axis=0, tiled=True)] for piece in groups]
        half = 2 * self.piece
        out, before_line, before_last = [], None, None
        for piece in groups:
            piece = after(piece, before_line)
            rots = [lax.ppermute(piece, "z", [(i, (i + k) % 4) for i in range(4)]) for k in (1, 2, 3)]
            line = jnp.concatenate([piece] + rots, axis=0)
            line = after(line, first if before_line is None else before_last)
            before_line = line
            by_x, by_y = swap(line, "x"), swap(line, "y")
            out.append([line, by_x, by_y, swap(by_x[:half], "y"), swap(by_y[half:], "x")])
            before_last = tuple(out[-1][3:])
        return out

    def pieces(self):
        n, out = self.piece, []
        for z in range(4):
            out.append((0, z * n, 0, z, 0))
            out.append((1, z * n, 0, z, 1))
            out.append((2, z * n, 1, z, 0))
            out.append((3 + z // 2, z % 2 * n, 1, z, 1))
        return out

    def n_gathered(self):
        return 5 if self.fast else 1

    def fetch(self, idx, refs, dst, sem):
        if not self.fast:
            copies = [pltpu.make_async_copy(refs[0], dst, sem.at[0])]
        else:
            copies = []
            for k, (r, row, yr, zr, xr) in enumerate(self.pieces()):
                to = dst.at[pl.ds(self.place(idx, yr, zr, xr), self.piece)]
                copies.append(pltpu.make_async_copy(refs[r].at[pl.ds(row, self.piece)], to, sem.at[k]))
        for copy in copies:
            copy.start()
        return copies

    def shared_outs(self, width):
        if not self.fast:
            return [((self.count * self.piece, width), BF16, HBM)]
        return [((8 * self.piece, width // 2), BF16, HBM)] * 4

    def n_shared(self):
        return 4 if self.fast else 1

    def emit(self, idx, src, refs, sem):
        if not self.fast:
            copies = [pltpu.make_async_copy(src, refs[0], sem.at[0])]
        else:
            copies, n, half = [], self.piece, src.shape[1] // 2
            for zr in range(4):
                for yr in range(2):
                    for xr in range(2):
                        at = self.place(idx, yr, zr, xr)
                        for lanes, ref, row in (
                            (0, refs[2 - 2 * xr], yr * 4 + zr),
                            (half, refs[3 - 2 * yr], xr * 4 + zr),
                        ):
                            copies.append(
                                pltpu.make_async_copy(
                                    src.at[pl.ds(at, n), pl.ds(lanes, half)],
                                    ref.at[pl.ds(row * n, n)],
                                    sem.at[len(copies)],
                                )
                            )
        for copy in copies:
            copy.start()
        return copies

    def reduce1(self, shared, tag):
        if not self.fast:
            return shared
        a_send, b_send, a_keep, b_keep = shared
        n, half = self.piece, a_send.shape[1]
        a_got, b_got = swap(a_send, "x"), swap(b_send, "y")
        shape = ((4 * n, half), BF16)
        return call(add_kernel, [shape] * 4, [a_keep, a_got, b_keep, b_got], name="add1_" + tag, us=1)

    def reduce2(self, sums, tag):
        if not self.fast:
            return sums
        a_send, a_keep, b_send, b_keep = sums
        n, half = self.piece, a_send.shape[1]
        a_got, b_got = swap(a_send, "y"), swap(b_send, "x")
        outs = [((n, 2 * half), BF16)] * 4
        return call(line_kernel, outs, [a_keep, a_got, b_keep, b_got], name="add2_" + tag, us=1)

    def reduce3(self, parts):
        if not self.fast:
            shares = parts[0].reshape(self.count, self.piece, -1)
            shares = lax.all_to_all(shares, GROUP, split_axis=0, concat_axis=0, tiled=True)
            return [shares.astype(F32).sum(axis=0)]
        rots = [lax.ppermute(parts[k], "z", [(i, (i - k) % 4) for i in range(4)]) for k in (1, 2, 3)]
        return [parts[0]] + rots


def add_kernel(a, a_in, b, b_in, a_send, a_keep, b_send, b_keep):
    cut = a_send.shape[0]
    for one, two, send, keep in ((a, a_in, a_send, a_keep), (b, b_in, b_send, b_keep)):
        send[...] = (one[cut:].astype(F32) + two[cut:].astype(F32)).astype(BF16)
        keep[...] = (one[:cut].astype(F32) + two[:cut].astype(F32)).astype(BF16)


def line_kernel(a, a_in, b, b_in, *outs):
    n, half = outs[0].shape[0], a.shape[1]
    for k, out in enumerate(outs):
        span = slice(k * n, (k + 1) * n)
        out[:, :half] = (a[span].astype(F32) + a_in[span].astype(F32)).astype(BF16)
        out[:, half:] = (b[span].astype(F32) + b_in[span].astype(F32)).astype(BF16)


def pack_kernel(
    span, idx, in_proj, norm, moe, router, taps, cbias, select, step, sbias, decay, skip, up,
    mine_o, send_o, ch_o, up_o, rows_s, block_s, sem,
):
    copy = pltpu.make_async_copy(up.at[0, pl.ds(0, up_o.shape[0])], up_o, sem)
    copy.start()
    dr = in_proj.shape[0]
    er, sel_n = select.shape
    rank, states = step.shape[0], decay.shape[0]
    inner2 = mine_o.shape[1] - LANES
    first = idx[3] == 0
    for k in range(inner2 // span):
        low = in_proj[:, 2 * k * span : (2 * k + 1) * span]
        high = in_proj[:, (2 * k + 1) * span : (2 * k + 2) * span]
        mine_o[:, k * span : (k + 1) * span] = jnp.where(first, low, high)
        send_o[:, k * span : (k + 1) * span] = jnp.where(first, high, low)
    rows_s[...] = jnp.zeros_like(rows_s)
    rows_s[0:4, :er] = taps[...].astype(F32)
    rows_s[ROW_BIAS : ROW_BIAS + 1, :er] = cbias[...].astype(F32)
    rows_s[ROW_STEP : ROW_STEP + 1, :er] = sbias[...].astype(F32)
    rows_s[ROW_SKIP : ROW_SKIP + 1, :er] = skip[...].astype(F32)
    rows_s[ROW_DECAY : ROW_DECAY + states, :er] = decay[...].astype(F32)
    ch_o[:, LANES:] = jnp.transpose(rows_s[...])[:er].astype(BF16)
    rows_s[...] = jnp.zeros_like(rows_s)
    rows_s[LANES - rank :, :er] = step[...].astype(F32)
    block_s[...] = jnp.zeros_like(block_s)
    block_s[:er, :sel_n] = select[...].astype(F32)
    ch_o[:, :LANES] = (block_s[:er] + jnp.transpose(rows_s[...])[:er]).astype(BF16)
    rows_s[...] = jnp.zeros_like(rows_s)
    rows_s[ROW_FEATURE : ROW_FEATURE + 1, :dr] = norm[...].astype(F32)
    rows_s[ROW_FEATURE + 1 : ROW_FEATURE + 2, :dr] = moe[...].astype(F32)
    rows_s[ROW_FEATURE + 2 : ROW_FEATURE + 2 + router.shape[0], :dr] = router[...].astype(F32)
    feature = jnp.transpose(rows_s[...])[:dr].astype(BF16)
    mine_o[:, inner2:] = feature
    send_o[:, inner2:] = feature
    copy.wait()


def cut_rows(sizes, hidden):
    parts, at = [], 0
    for size in sizes:
        spans, end = [], at + size
        if at < hidden:
            spans.append((0, at, 0, min(end, hidden) - at))
        if end > hidden:
            low = max(at, hidden)
            spans.append((1, low - hidden, low - at, end - low))
        parts.append(spans)
        at = end
    return parts


def split_kernel(parts, up, down, *refs):
    outs, sem = refs[:-1], refs[-1]
    copies = []
    for spans, out in zip(parts, outs, strict=True):
        for which, row, at, size in spans:
            source = (up, down)[which].at[0, pl.ds(row, size)]
            copies.append(pltpu.make_async_copy(source, out.at[pl.ds(at, size)], sem.at[len(copies)]))
    for copy in copies:
        copy.start()
    for copy in copies:
        copy.wait()


def merge_kernel(mine, got, ch, out_proj, one_o, two_o):
    inner = out_proj.shape[1]
    both = jnp.concatenate([mine[...].astype(F32), got[...].astype(F32)], axis=0).astype(BF16)
    one_o[:, :inner] = both[:, :inner]
    one_o[:, inner : inner + LANES] = ch[:, :LANES]
    one_o[:, inner + LANES :] = ch[:, LANES:] + both[:, 2 * inner :]
    two_o[:, :inner] = both[:, inner : 2 * inner]
    two_o[:, inner:] = out_proj[...]


def enter_kernel(plan, idx, lens, tok2, nat, *refs):
    n = plan.n_gathered()
    pieces = refs[:n]
    u_o, xin_o, xc_o, sel_o, small_o, dnat_o, g1, sem = refs[n:]
    copies = plan.fetch(idx, pieces, g1, sem)
    rows, width = tok2.shape
    tok = rows // 2
    inner = xin_o.shape[1]
    perm = perm_matrix(idx, nat)
    vals = tok2[...].astype(F32)
    scale = lax.rsqrt(jnp.mean(vals * vals, axis=1, keepdims=True) + EPS)
    offset = both_offsets(lens, tok)
    for copy in copies:
        copy.wait()
    table = g1[:, inner + LANES :]
    dnat = mm(table, perm, (((0,), (1,)), ((), ())))[ROW_FEATURE:]
    dnat_o[...] = dnat[: dnat_o.shape[0]]
    u = (vals * scale * dnat[0:1]).astype(BF16)
    u = mm(u, perm).astype(BF16)
    u_o[...] = u
    xin = mm(u, g1[:, :inner])
    xin_o[...] = xin
    small = jnp.transpose(table.astype(F32))[: small_o.shape[0]]
    small_o[...] = small
    conv = conv_of(xin, small, offset)
    xc = (conv * sigmoid(conv)).astype(BF16)
    xc_o[...] = xc
    sel_o[...] = mm(xc, g1[:, inner : inner + LANES])


def conv_of(xin, small, offset):
    conv = small[ROW_BIAS : ROW_BIAS + 1] + small[3:4] * xin
    for lag in range(1, 4):
        moved = pltpu.roll(xin, lag, 0)
        conv = conv + jnp.where(offset >= lag, small[3 - lag : 4 - lag] * moved, 0.0)
    return conv


def swap_halves(rows):
    half = rows.shape[0] // 2
    return jnp.concatenate([rows[half:], rows[:half]], axis=0)


GROUP_TOKENS = 16


def spread_rows(sel, first, states):
    rows, n = sel.shape[0], GROUP_TOKENS
    wide = (LANES, n * states)
    pick = (iota(wide, 0) == first + iota(wide, 1) % states).astype(F32).astype(BF16)
    values = split_mm(sel, pick)
    own = iota((rows, n * states), 1) // states == iota((rows, n * states), 0) % n
    values = jnp.where(own, values, 0.0).reshape(rows // n, n, n * states)
    high = values.astype(BF16).astype(F32)
    return jnp.concatenate([high, values - high], axis=1).astype(BF16)


def two_terms(block):
    high = block.astype(BF16).astype(F32)
    return jnp.concatenate([high, block - high], axis=0).astype(BF16)


def halves(block):
    n = block.shape[0] // 2
    return block[:n] + block[n:]


def step_inputs(sel, rank):
    tail = LANES - rank
    return jnp.where(iota(sel.shape, 1) >= tail, pltpu.roll(sel, tail, 1), 0.0).astype(BF16)


def step_of(q, g1sel, small):
    return mm(q, g1sel[...], NT) + small[ROW_STEP : ROW_STEP + 1]


def scan_kernel(
    rank, states, lens, sel_a, sel_b, xc, g1sel, small,
    ys_o, sel_o, check_o,
    dm_s, dx_s, wr_s, rd_s, rate_s, h_s, check_s, sem,
):
    rows, inner = ys_o.shape
    tok = rows // 2
    sel = sel_a[...] + swap_halves(sel_b[...])
    sel_o[...] = sel
    delta = softplus(step_of(step_inputs(sel, rank), g1sel, small))
    offset = both_offsets(lens, tok)
    xcf = xc[...].astype(F32)
    dm_s[...] = jnp.where(offset > 0, delta, 1e30)
    dx_s[...] = delta * xcf
    for b in range(2):
        turned = jnp.transpose(sel[b * tok : (b + 1) * tok])
        wr_s[b] = turned[rank : rank + states]
        rd_s[b] = turned[rank + states : rank + 2 * states]
    rate_s[...] = jnp.exp(small[ROW_DECAY : ROW_DECAY + states]) * (-LOG2E)
    h_s[...] = jnp.zeros_like(h_s)
    half = states // 2

    def chunk(ci, carry):
        t0 = pl.multiple_of(ci * 8, 8)
        for b in range(2):
            at = pl.multiple_of(b * tok + t0, 8)
            wr8 = pltpu.roll(wr_s[b], tok - t0, 1)
            rd8 = pltpu.roll(rd_s[b], tok - t0, 1)
            wcol = [jnp.broadcast_to(wr8[:, j : j + 1], (states, LANES)) for j in range(8)]
            rcol = [jnp.broadcast_to(rd8[:, j : j + 1], (states, LANES)) for j in range(8)]
            for g in range(inner // LANES):
                lanes = slice(g * LANES, (g + 1) * LANES)
                h = h_s[b, :, lanes]
                check_s[ci * 2 + b, :, lanes] = h
                rate = rate_s[:, lanes]
                dm8 = dm_s[pl.ds(at, 8), lanes]
                dx8 = dx_s[pl.ds(at, 8), lanes]
                parts = []
                for j in range(8):
                    d = jnp.broadcast_to(dm8[j : j + 1], (states, LANES))
                    x = jnp.broadcast_to(dx8[j : j + 1], (states, LANES))
                    h = jnp.exp2(d * rate) * h + wcol[j] * x
                    p = rcol[j] * h
                    parts.append(p[:half] + p[half:])
                ys_o[pl.ds(at, 8), lanes] = fold(parts)
                h_s[b, :, lanes] = h
        saved(ci).start()
        return carry

    def saved(ci):
        pair = pl.ds(2 * ci, 2)
        return pltpu.make_async_copy(check_s.at[pair], check_o.at[pair], sem.at[ci])

    lax.fori_loop(0, tok // 8, chunk, 0)
    for ci in range(tok // 8):
        saved(ci).wait()


def gate_kernel(plan, idx, u, xc, ys, small, *refs):
    n = plan.n_gathered()
    pieces = refs[:n]
    mine_o, send_o, g2, sem = refs[n:]
    copies = plan.fetch(idx, pieces, g2, sem)
    for copy in copies:
        copy.wait()
    inner = ys.shape[1]
    tok = mine_o.shape[0]
    zg = mm(u[...], g2[:, :inner])
    gated = (ys[...] + small[ROW_SKIP : ROW_SKIP + 1] * xc[...].astype(F32)) * (zg * sigmoid(zg))
    gated = gated.astype(BF16)
    branch = mm(gated, g2[:, inner:])
    mine_o[...] = branch[:tok]
    send_o[...] = branch[tok:]


def route_tables(lens, routes, experts, capacity, tok):
    _, valid = positions(lens, 0, tok)
    valid_f = valid.astype(F32)
    width = max(LANES, experts)
    hot = (routes == iota((tok, width), 1)).astype(F32)
    live = hot * valid_f
    earlier = (iota((tok, tok), 1) < iota((tok, tok), 0)).astype(F32).astype(BF16)
    before = mm(earlier, live.astype(BF16))
    rank = jnp.sum(before * hot, axis=1, keepdims=True).astype(jnp.int32)
    kept = valid & (rank < capacity)
    return valid_f, hot, rank, kept


def column_of(row):
    n = row.shape[1]
    square = iota((n, n), 0) == iota((n, n), 1)
    return jnp.sum(jnp.where(square, row[...].astype(F32), 0.0), axis=1, keepdims=True).astype(jnp.int32)


class Slots:
    def __init__(self, capacity, width):
        self.full, left = divmod(capacity, 8)
        self.split = 0 < left <= 4
        if left > 4:
            self.full += 1
        self.width = width
        self.lanes = self.full * width + (width // 2 if self.split else 0)

    def rows(self, groups):
        return groups * 8 * self.full + (groups * 4 if self.split else 0)

    def hot(self, routes, rank, kept, experts, first, low, high):
        shape = (rank.shape[0], 8 * experts)
        place = iota(shape, 1)
        row = place % 8
        inside = kept & (routes == place // 8) & (rank == first + row - low)
        return jnp.where(inside & (row >= low) & (row < high), 1.0, 0.0).astype(BF16)

    def hots(self, routes, rank, kept, experts):
        args = (routes, rank, kept, experts)
        whole = [self.hot(*args, 8 * i, 0, 8) for i in range(self.full)]
        last = [self.hot(*args, 8 * self.full, 4 * i, 4 * i + 4) for i in range(2)] if self.split else []
        return whole, last

    def unpack(self, groups, both, tail_s):
        at, width, height = 0, self.width, groups[0].shape[0]
        for group in groups:
            for i in range(self.full):
                both[at : at + height] = group[:, i * width : (i + 1) * width]
                at += height
        if self.split:
            half, start, count = width // 2, 0, height // 8
            for group in groups:
                block = group[:, self.full * width :].astype(F32)
                for k in range(count):
                    tail_s[start + 4 * k : start + 4 * k + 4, :half] = block[8 * k : 8 * k + 4]
                    tail_s[start + 4 * k : start + 4 * k + 4, half:] = block[8 * k + 4 : 8 * k + 8]
                start += 4 * count
            both[at : at + start] = tail_s[:start].astype(BF16)

    def pack(self, rows, which, count, out, tail_s):
        width, height = self.width, out.shape[0]
        at = which * self.full * height
        for i in range(self.full):
            out[:, i * width : (i + 1) * width] = rows[at : at + height].astype(out.dtype)
            at += height
        if self.split:
            half = width // 2
            at = count * self.full * height + which * height // 2
            for k in range(height // 8):
                tail_s[8 * k : 8 * k + 4, :half] = rows[at + 4 * k : at + 4 * k + 4, :half]
                tail_s[8 * k + 4 : 8 * k + 8, :half] = rows[at + 4 * k : at + 4 * k + 4, half:]
            out[:, self.full * width :] = tail_s[:height, :half].astype(out.dtype)


def moe_enter_kernel(slots, experts, capacity, lens, tok, cot, routes, mine, got, dnat, disp_o, hidden_o, gate_o):
    rows, width = tok.shape
    routes = column_of(routes)
    hidden = tok[...].astype(F32) + (mine[...] + got[...])
    hidden_o[...] = hidden
    scale = lax.rsqrt(jnp.mean(hidden * hidden, axis=1, keepdims=True) + EPS)
    mv = (hidden * scale * dnat[1:2]).astype(BF16)
    logits = mm(mv, dnat[...].astype(BF16), NT)
    hot = (routes + 2 == iota(logits.shape, 1)).astype(F32)
    gate = sigmoid(jnp.sum(logits * hot, axis=1, keepdims=True))
    gate_o[...] = jnp.broadcast_to(gate, gate_o.shape)
    valid_f, _, rank, kept = route_tables(lens, routes, experts, capacity, rows)
    back = (cot[...].astype(F32) * valid_f * (gate * kept.astype(F32))).astype(BF16)
    both = jnp.concatenate([mv, back], axis=1)
    whole, last = slots.hots(routes, rank, kept, experts)
    span = slots.width
    for i, hot in enumerate(whole):
        disp_o[:, i * span : (i + 1) * span] = mm(hot, both, TN).astype(BF16)
    if last:
        end = mm(last[0], both[:, : span // 2], TN) + mm(last[1], both[:, span // 2 :], TN)
        disp_o[:, slots.full * span :] = end.astype(BF16)


def half_units(both, up, span):
    width = up.shape[1]
    pre = mm(both[:, :width], up[span], NT)
    sq = pre * pre
    th = jnp.tanh(GELU_C * (pre + GELU_K * sq * pre))
    act = (0.5 * pre * (1.0 + th)).astype(BF16)
    return act, 0.5 * (1.0 + th) + 0.5 * pre * (1.0 - th * th) * (GELU_C * (1.0 + 3.0 * GELU_K * sq))


def moves_of(parts, refs, targets, which_of):
    moves = []
    for spans, ref in zip(parts, refs, strict=True):
        for which, row, at, size in spans:
            if which in which_of:
                moves.append((ref.at[pl.ds(at, size)], targets[which].at[pl.ds(row, size)]))
    return moves


PART = 256


def expert_own_kernel(slots, parts, own, peer, up, down, *refs):
    others = refs[: len(parts)]
    both, acc, act_o, slope_o, up_o, up_s, down_s, tail_s, sem = refs[len(parts) :]
    moves = [(up.at[0], up_s), (down.at[0], down_s)] + moves_of(parts, others, (up_o, None), (0,))
    copies = [pltpu.make_async_copy(a, b, sem.at[k]) for k, (a, b) in enumerate(moves)]
    for copy in copies:
        copy.start()
    slots.unpack((own, peer), both, tail_s)
    width = up.shape[2]
    for copy in copies:
        copy.wait()
    for f in range(0, up_s.shape[0], PART):
        span = slice(f, f + PART)
        act, slope = half_units(both, up_s, span)
        g_pre = (mm(both[:, width:], down_s[span], NT) * slope).astype(BF16)
        e_part = mm(act, down_s[span])
        i_part = mm(g_pre, up_s[span])
        if f == 0:
            acc[:, :width] = e_part
            acc[:, width:] = i_part
        else:
            acc[:, :width] += e_part
            acc[:, width:] += i_part
        act, slope = half_units(both, up_o, span)
        act_o[:, span] = act
        slope_o[:, span] = slope


def expert_other_kernel(slots, parts, both, acc, act, slope, up, *refs):
    others = refs[: len(parts)]
    out_own, out_peer, acc_s, down_s, tail_s, sem = refs[len(parts) :]
    moves = moves_of(parts, others, (None, down_s), (1,))
    copies = [pltpu.make_async_copy(a, b, sem.at[k]) for k, (a, b) in enumerate(moves)]
    for copy in copies:
        copy.start()
    width = up.shape[1]
    for copy in copies:
        copy.wait()
    for f in range(0, up.shape[0], PART):
        span = slice(f, f + PART)
        g_pre = (mm(both[:, width:], down_s[span], NT) * slope[:, span]).astype(BF16)
        e_part = mm(act[:, span], down_s[span])
        i_part = mm(g_pre, up[span])
        old = acc if f == 0 else acc_s
        acc_s[:, :width] = old[:, :width] + e_part
        acc_s[:, width:] = old[:, width:] + i_part
    slots.pack(acc_s, 1, 2, out_peer, tail_s)
    slots.pack(acc_s, 0, 2, out_own, tail_s)


def unit_grads(both, up, down, up_g, down_g, more):
    width = up.shape[2]
    for f in range(0, up.shape[1], PART):
        span = slice(f, f + PART)
        act, slope = half_units(both, up.at[0], span)
        g_pre = (mm(both[:, width:], down[0, span], NT) * slope).astype(BF16)
        to_down = mm(act, both[:, width:], TN)
        to_up = mm(g_pre, both[:, :width], TN)
        if more is not None:
            to_up, to_down = to_up + more[0][0, span], to_down + more[1][0, span]
        down_g[0, span] = to_down
        up_g[0, span] = to_up


def near_grad_kernel(both, up, down, up_g, down_g):
    unit_grads(both, up, down, up_g, down_g, None)


def far_grad_kernel(slots, own_y, peer_y, up, down, up_near, down_near, up_g, down_g, both_s, tail_s):
    slots.unpack((own_y, peer_y), both_s, tail_s)
    unit_grads(both_s, up, down, up_g, down_g, (up_near, down_near))


def moe_leave_kernel(
    slots, experts, capacity, lens, routes, cot, hidden, gate_in, dnat, back,
    out_o, ghid_o, gbr_o, dgrad_o,
):
    rows, width = hidden.shape
    routes = column_of(routes)
    valid_f, _, rank, kept = route_tables(lens, routes, experts, capacity, rows)
    kept_f = kept.astype(F32)
    gate = gate_in[:, 0:1]
    whole, last = slots.hots(routes, rank, kept, experts)
    span = slots.width
    picked = jnp.zeros((rows, 2 * width), F32)
    for i, hot in enumerate(whole):
        picked = picked + mm(hot, back[:, i * span : (i + 1) * span])
    if last:
        end = back[:, slots.full * span :]
        picked = picked + jnp.concatenate([mm(last[0], end), mm(last[1], end)], axis=1)
    ex_out = picked[:, :width]
    sent = picked[:, width:]
    hid = hidden[...]
    out_o[...] = (valid_f * (hid + gate * ex_out)).astype(BF16)
    gy = cot[...].astype(F32) * valid_f
    g_gate = jnp.sum(gy * ex_out, axis=1, keepdims=True)
    chosen = g_gate * gate * (1.0 - gate)
    small_rows = dnat.shape[0]
    hot = (routes + 2 == iota((rows, small_rows), 1)).astype(F32)
    g_logit = (chosen * hot).astype(BF16)
    g_mv = mm(g_logit, dnat[...].astype(BF16)) + sent
    scale = lax.rsqrt(jnp.mean(hid * hid, axis=1, keepdims=True) + EPS)
    hat = hid * scale
    gain = dnat[1:2]
    mv = (hat * gain).astype(BF16)
    router_g = mm(g_logit, mv, TN)
    gain_g = jnp.sum(g_mv * hat, axis=0, keepdims=True)
    dgrad_o[...] = jnp.where(iota(dgrad_o.shape, 0) == 1, gain_g, router_g)
    gg = g_mv * gain
    mean = jnp.sum(gg * hat, axis=1, keepdims=True) * (1.0 / width)
    ghid = gy + scale * (gg - hat * mean)
    ghid_o[...] = ghid
    gbr_o[...] = ghid.astype(BF16)


def gate_back_kernel(plan, idx, gbr_a, gbr_b, g2, xc, ys, small, u, *refs):
    n = plan.n_shared()
    gy_o, gzg_o = refs[:2]
    shared = refs[2 : 2 + n]
    grad_s, sem = refs[2 + n :]
    inner = ys.shape[1]
    gbr = jnp.concatenate([gbr_a[...], gbr_b[...]], axis=0)
    g_gated = mm(gbr, g2[:, inner:], NT)
    skip = small[ROW_SKIP : ROW_SKIP + 1]
    zg = mm(u[...], g2[:, :inner])
    sig = sigmoid(zg)
    silu = zg * sig
    out = ys[...] + skip * xc[...].astype(F32)
    gy_o[...] = g_gated * silu
    gzg = (g_gated * out * (sig * (1.0 + zg * (1.0 - sig)))).astype(BF16)
    gzg_o[...] = gzg
    grad_s[:, :inner] = mm(u[...], gzg, TN).astype(BF16)
    grad_s[:, inner:] = mm((out * silu).astype(BF16), gbr, TN).astype(BF16)
    for copy in plan.emit(idx, grad_s, shared, sem):
        copy.wait()


def scan_back_kernel(
    rank, states, lens, gy_s, xc, sel, small, g1sel, check_in,
    gsel_o, gxcs_o, gsr_o, q_o, smallg_o,
    dm_s, dx_s, gdx_s, gdl_s, wr_s, rd_s, gwr_s, grd_s, rate_s, lam_s, ga_s, write_s, hb_s, lb_s, wb_s, delta_s, sig_s,
    check, sem,
):
    copy = pltpu.make_async_copy(check_in, check, sem)
    copy.start()
    rows, inner = gy_s.shape
    tok = rows // 2
    xcf = xc[...].astype(F32)
    skip = small[ROW_SKIP : ROW_SKIP + 1]
    q = step_inputs(sel[...], rank)
    q_o[...] = q
    step_pre = step_of(q, g1sel, small)
    delta_s[...] = softplus(step_pre)
    sig_s[...] = sigmoid(step_pre)
    delta = delta_s[...]
    dm_s[...] = jnp.where(both_offsets(lens, tok) > 0, delta, 1e30)
    dx_s[...] = delta * xcf
    for b in range(2):
        turned = jnp.transpose(sel[b * tok : (b + 1) * tok])
        wr_s[b] = turned[rank : rank + states]
        rd_s[b] = turned[rank + states : rank + 2 * states]
    rate_s[...] = jnp.exp(small[ROW_DECAY : ROW_DECAY + states]) * (-LOG2E)
    lam_s[...] = jnp.zeros_like(lam_s)
    ga_s[...] = jnp.zeros_like(ga_s)
    write_s[...] = spread_rows(sel[...], rank, states)
    shape = (states, LANES)
    n = GROUP_TOKENS
    count = tok // n
    wide = (n, n * states)
    own = iota(wide, 1) // states == iota(wide, 0)
    group = own.astype(F32).astype(BF16)
    for ref in (hb_s, lb_s, wb_s):
        ref[1] = jnp.zeros(ref.shape[1:], BF16)

    def sums(b, ci):
        span = pl.ds(pl.multiple_of(b * tok + ci * n, n), n)
        gdx_s[span, :] = halves(mm(write_s[b * count + ci], lb_s[b]))
        gdl_s[span, :] = mm(group, wb_s[b])
        grd_s[span, :] = jnp.where(own, halves(mm(two_terms(gy_s[span, :]), hb_s[b], NT)), 0.0)
        gwr_s[span, :] = jnp.where(own, halves(mm(two_terms(dx_s[span, :]), lb_s[b], NT)), 0.0)

    def chunk(i, carry):
        ci = count - 1 - i
        sums(1, jnp.minimum(ci + 1, count - 1))
        for b in range(2):
            for part in range(n // 8 - 1, -1, -1):
                t0 = pl.multiple_of(ci * n + part * 8, 8)
                at = pl.multiple_of(b * tok + t0, 8)
                wr8 = pltpu.roll(wr_s[b], tok - t0, 1)
                rd8 = pltpu.roll(rd_s[b], tok - t0, 1)
                wcol = [jnp.broadcast_to(wr8[:, j : j + 1], shape) for j in range(8)]
                rcol = [jnp.broadcast_to(rd8[:, j : j + 1], shape) for j in range(8)]
                for g in range(inner // LANES):
                    lanes = slice(g * LANES, (g + 1) * LANES)
                    h = check[(ci * (n // 8) + part) * 2 + b, :, lanes]
                    rate = rate_s[:, lanes]
                    dm8 = dm_s[pl.ds(at, 8), lanes]
                    dx8 = dx_s[pl.ds(at, 8), lanes]
                    gy8 = gy_s[pl.ds(at, 8), lanes]
                    decays, olds = [], []
                    for j in range(8):
                        k = part * 8 + j
                        d = jnp.broadcast_to(dm8[j : j + 1], shape)
                        x = jnp.broadcast_to(dx8[j : j + 1], shape)
                        a = jnp.exp2(d * rate)
                        old = a * h
                        h = old + wcol[j] * x
                        hb_s[b, k * states : (k + 1) * states, lanes] = h.astype(BF16)
                        decays.append(a)
                        olds.append(old)
                    lam_in = lam_s[b, :, lanes]
                    ga = ga_s[:, lanes]
                    for j in range(7, -1, -1):
                        k = part * 8 + j
                        lam = rcol[j] * jnp.broadcast_to(gy8[j : j + 1], shape) + lam_in
                        lam_in = decays[j] * lam
                        w = lam * olds[j]
                        ga = ga + w * jnp.broadcast_to(dm8[j : j + 1], shape)
                        lb_s[b, k * states : (k + 1) * states, lanes] = lam.astype(BF16)
                        wb_s[b, k * states : (k + 1) * states, lanes] = (w * rate).astype(BF16)
                    lam_s[b, :, lanes] = lam_in
                    ga_s[:, lanes] = ga
            if b == 0:
                sums(0, ci)
        return carry

    copy.wait()
    lax.fori_loop(0, count, chunk, 0)
    sums(1, 0)
    delta = delta_s[...]
    gdx = gdx_s[...]
    xcf = xc[...].astype(F32)
    gy = gy_s[...]
    gxcs_o[...] = gy * skip + gdx * delta
    g_step = (gdx * xcf + LN2 * gdl_s[...]) * sig_s[...]
    gsr = g_step.astype(BF16)
    gsr_o[...] = gsr
    lane = iota((rows, LANES), 1)
    tail = LANES - rank
    back = jnp.where(lane >= tail, mm(gsr, g1sel[...]), 0.0)
    back = pltpu.roll(back, rank, 1)
    tall = (n * states, LANES)
    place = iota(tall, 0) % states
    to_wr = (iota(tall, 1) == rank + place).astype(F32).astype(BF16)
    to_rd = (iota(tall, 1) == rank + states + place).astype(F32).astype(BF16)
    gsel_o[...] = back + split_mm(gwr_s[...], to_wr) + split_mm(grd_s[...], to_rd)
    smallg_o[0:ROW_STEP] = jnp.zeros((ROW_STEP, inner), F32)
    smallg_o[ROW_STEP : ROW_STEP + 1] = jnp.sum(g_step, axis=0, keepdims=True)
    smallg_o[ROW_SKIP : ROW_SKIP + 1] = jnp.sum(gy * xcf, axis=0, keepdims=True)
    smallg_o[ROW_SKIP + 1 : ROW_DECAY] = jnp.zeros((ROW_DECAY - ROW_SKIP - 1, inner), F32)
    smallg_o[ROW_DECAY : ROW_DECAY + states] = ga_s[...] * rate_s[...] * LN2
    rest = smallg_o.shape[0] - ROW_DECAY - states
    if rest:
        smallg_o[ROW_DECAY + states :] = jnp.zeros((rest, inner), F32)


def leave_kernel(
    plan, idx, lens, nat, gsel_a, gsel_b, gxcs, gsr, q, smallg, xin, xc, u, small, g1, dgrad, gxin_o, *refs
):
    n = plan.n_shared()
    shared = refs[:n]
    grad_s, sem = refs[n:]
    rows, inner = xin.shape
    tok = rows // 2
    perm = perm_matrix(idx, nat)
    g_sel = (gsel_a[...] + swap_halves(gsel_b[...])).astype(BF16)
    selblk = g1[:, inner : inner + LANES]
    block = mm(xc[...], g_sel, TN) + mm(gsr[...], q[...], TN)
    grad_s[:, inner : inner + LANES] = block.astype(BF16)
    g_xc = mm(g_sel, selblk, NT) + gxcs[...]
    offset = both_offsets(lens, tok)
    x = xin[...]
    sm = small[...]
    conv = conv_of(x, sm, offset)
    sig = sigmoid(conv)
    g_conv = g_xc * (sig * (1.0 + conv * (1.0 - sig)))
    g_xin = sm[3:4] * g_conv
    taps = [None, None, None, jnp.sum(g_conv * x, axis=0, keepdims=True)]
    for lag in range(1, 4):
        held = jnp.where(offset >= lag, g_conv, 0.0)
        g_xin = g_xin + sm[3 - lag : 4 - lag] * pltpu.roll(held, rows - lag, 0)
        taps[3 - lag] = jnp.sum(held * pltpu.roll(x, lag, 0), axis=0, keepdims=True)
    g_bias = jnp.sum(g_conv, axis=0, keepdims=True)
    g_xin = g_xin.astype(BF16)
    gxin_o[...] = g_xin
    grad_s[:, :inner] = mm(u[...], g_xin, TN).astype(BF16)
    dg = split_mm(dgrad[...], perm)
    top = jnp.concatenate(taps + [g_bias, jnp.zeros((3, inner), F32)], axis=0)
    gap = jnp.zeros((ROW_FEATURE - smallg.shape[0], inner), F32)
    end = jnp.zeros((LANES - ROW_FEATURE - dg.shape[0], inner), F32)
    table = jnp.concatenate([smallg[0:8] + top, smallg[8:], gap, dg, end], axis=0)
    grad_s[:, inner + LANES :] = jnp.transpose(table).astype(BF16)
    for copy in plan.emit(idx, grad_s, shared, sem):
        copy.wait()


def back_kernel(idx, nat, gxin, gzg, g1x, g2z, mine_o, send_o):
    tok = mine_o.shape[0]
    gn = mm(gxin[...], g1x[...], NT) + mm(gzg[...], g2z[...], NT)
    gn = split_mm(gn, perm_matrix(idx, nat), NT)
    mine_o[...] = gn[:tok]
    send_o[...] = gn[tok:]


def final_kernel(tok, mine, got, ghid, dnat, out_o):
    width = tok.shape[1]
    vals = tok[...].astype(F32)
    scale = lax.rsqrt(jnp.mean(vals * vals, axis=1, keepdims=True) + EPS)
    hat = vals * scale
    gg = (mine[...] + got[...]) * dnat[0:1]
    mean = jnp.sum(gg * hat, axis=1, keepdims=True) * (1.0 / width)
    out_o[...] = ghid[...] + scale * (gg - hat * mean)


def swap(values, axis):
    return lax.ppermute(values, axis, [(0, 1), (1, 0)])


def exchange(rows, count):
    parts = rows.reshape(count, 8, rows.shape[1])
    parts = lax.all_to_all(parts, ("z", "x"), split_axis=0, concat_axis=0, tiled=True)
    return parts.reshape(rows.shape)


def share_kernel(n1, n2, rank, states, *refs):
    one, two = refs[:n1], refs[n1 : n1 + n2]
    keep_o, send_o, outg_o, select_o, step_o, taps_o, cbias_o, sbias_o, skip_o, decay_o, square_s = refs[n1 + n2 :]
    er = outg_o.shape[0]
    dr = keep_o.shape[0]

    def total(parts):
        acc = parts[0][...].astype(F32)
        for part in parts[1:]:
            acc = acc + part[...].astype(F32)
        return acc

    x = total(one)
    inner = x.shape[1] - 2 * LANES
    z = total(two)
    for out, at in ((keep_o, 0), (send_o, dr)):
        out[:, :inner] = x[at : at + dr, :inner]
        out[:, inner : 2 * inner] = z[at : at + dr, :inner]
        out[:, 2 * inner :] = x[at : at + dr, inner + LANES :]
    outg_o[...] = z[:, inner:]
    select_o[...] = x[:, inner : inner + select_o.shape[1]]
    square_s[...] = jnp.zeros_like(square_s)
    square_s[:er] = x[:, inner : inner + LANES]
    step_o[...] = jnp.transpose(square_s[...])[LANES - rank :, :er]
    square_s[:er] = x[:, inner + LANES :]
    table = jnp.transpose(square_s[...])[:, :er]
    taps_o[...] = table[0:4]
    cbias_o[...] = table[ROW_BIAS : ROW_BIAS + 1]
    sbias_o[...] = table[ROW_STEP : ROW_STEP + 1]
    skip_o[...] = table[ROW_SKIP : ROW_SKIP + 1]
    decay_o[...] = table[ROW_DECAY : ROW_DECAY + states]


def spread_kernel(span, idx, keep, got, in_proj, norm, in_o, norm_o, moe_o, router_o, square_s):
    dr = keep.shape[0]
    inner2 = keep.shape[1] - LANES
    first = idx[3] == 0
    acc = jnp.zeros((dr, LANES), F32)
    for k in range(inner2 // span):
        mine = keep[:, k * span : (k + 1) * span]
        peer = got[:, k * span : (k + 1) * span]
        for at, part in ((2 * k * span, jnp.where(first, mine, peer)), ((2 * k + 1) * span, jnp.where(first, peer, mine))):
            in_o[:, at : at + span] = part
            terms = part * in_proj[:, at : at + span].astype(F32)
            for j in range(0, span, LANES):
                acc = acc + terms[:, j : j + LANES]
    table = keep[:, inner2:] + got[:, inner2:]
    at = ROW_FEATURE
    total = jnp.sum(acc, axis=1, keepdims=True)
    square_s[...] = jnp.zeros_like(square_s)
    square_s[:dr] = jnp.where(iota(table.shape, 1) == at, total, table)
    flat = jnp.transpose(square_s[...])[:, :dr]
    norm_o[...] = flat[at : at + 1] / norm[...].astype(F32)
    moe_o[...] = flat[at + 1 : at + 2]
    router_o[...] = flat[at + 2 : at + 2 + router_o.shape[0]]


def body(
    sizes,
    tokens,
    cotangent,
    seq_lens,
    routes,
    norm_gain,
    input_proj,
    conv_weight,
    conv_bias,
    select_proj,
    step_proj,
    step_bias,
    decay_log,
    skip_gain,
    output_proj,
    moe_gain,
    router_weight,
    up_weight,
    down_weight,
):
    ny, nz, nx = sizes
    nf = nz * nx
    ng = ny * nf
    tok, width = tokens.shape
    rank, er = step_proj.shape
    states = decay_log.shape[0]
    experts = router_weight.shape[1]
    capacity = 5 * tok // (4 * experts)
    dr = norm_gain.shape[0]
    inner = ng * er
    rows = 2 * tok
    small_n = -(-(ROW_DECAY + states) // 8) * 8
    dn = -(-(2 + experts) // 8) * 8
    plan = Plan(ny, nz, nx, er)
    idx = jnp.stack([lax.axis_index(a) for a in ("y", "z", "x", "c")]).astype(jnp.int32)

    order = np.arange(width).reshape(ny, 2, nf, dr).transpose(0, 2, 1, 3)
    nat = np.stack([order.reshape(width), order[:, :, ::-1].reshape(width)])
    nat = jnp.asarray(nat, jnp.int32)

    span = nf * er
    hid = up_weight.shape[1]
    sizes = [hid * 26 // 48, hid * 28 // 48]
    sizes.append(2 * hid - sum(sizes))
    parts = cut_rows(sizes, hid)
    mine_w, send_w, ch, up_send = call(
        functools.partial(pack_kernel, span),
        [((dr, 2 * inner + LANES), BF16), ((dr, 2 * inner + LANES), BF16), ((er, 2 * LANES), BF16), ((sizes[0], width), BF16)],
        [idx]
        + [
            in_hbm(v)
            for v in (input_proj, norm_gain[None], moe_gain[None], router_weight.T, conv_weight, conv_bias[None], select_proj, step_proj, step_bias[None], decay_log, skip_gain[None], up_weight)
        ],
        [SMEM] + [None] * 11 + [HBM],
        scratch=[pltpu.VMEM((LANES, LANES), F32), pltpu.VMEM((LANES, LANES), F32), pltpu.SemaphoreType.DMA],
        name="pack",
        us=1,
    )
    got_w = swap(send_w, "c")
    group1, group2 = call(
        merge_kernel,
        [((er, inner + 2 * LANES), BF16), ((er, inner + width), BF16)],
        [mine_w, got_w, ch, output_proj],
        name="merge",
        us=1,
    )
    tok2 = jnp.concatenate([tokens, swap(tokens, "c")], axis=0)
    lens2 = jnp.concatenate([seq_lens, swap(seq_lens, "c")], axis=0)
    up_one = swap(up_send, "y")
    sends = call(
        functools.partial(split_kernel, parts[1:]),
        [((size, width), BF16) for size in sizes[1:]],
        [in_hbm(after(up_weight, group1)), in_hbm(down_weight)],
        [HBM, HBM],
        scratch=[pltpu.SemaphoreType.DMA((2 * len(sizes),))],
        name="split",
        us=2,
    )
    up_one = after(up_one, sends[0])
    pieces1, pieces2 = plan.gather([group1, group2], (up_one, tok2, lens2))

    fetch_sem = pltpu.SemaphoreType.DMA((ng,))
    emit_sem = pltpu.SemaphoreType.DMA((2 * ng,))
    u, xin, xc, selp, small_t, dnat, g1 = call(
        functools.partial(enter_kernel, plan),
        [((rows, width), BF16), kept((rows, inner), F32), ((rows, inner), BF16), ((rows, LANES), F32), ((small_n, inner), F32), kept((dn, width), F32), ((inner, inner + 2 * LANES), BF16)],
        [idx, lens2, tok2, nat] + pieces1,
        [SMEM, SMEM, None, None] + [HBM] * len(pieces1),
        scratch=[fetch_sem],
        name="enter",
    )
    selq = swap(selp, "c")
    middle = (pieces2[min(2, len(pieces2) - 1)], xc)
    part_two = swap(after(sends[0], middle), "y")
    part_three = swap(after(sends[1], middle), "y")
    g1sel_spec = pl.BlockSpec((inner, LANES), lambda i: (0, inner // LANES))
    chunks = tok // 8
    ys, sel, check = call(
        functools.partial(scan_kernel, rank, states),
        [((rows, inner), F32), kept((rows, LANES), F32), ((2 * chunks, states, inner), F32, HBM, True)],
        [lens2, selp, selq, xc, g1, small_t],
        [SMEM, None, None, None, g1sel_spec, None],
        scratch=[pltpu.VMEM((rows, inner), F32), pltpu.VMEM((rows, inner), F32), pltpu.VMEM((2, states, tok), F32), pltpu.VMEM((2, states, tok), F32), pltpu.VMEM((states, inner), F32), pltpu.VMEM((2, states, inner), F32), pltpu.VMEM((2 * chunks, states, inner), F32), pltpu.SemaphoreType.DMA((chunks,))],
        name="scan",
        us=9,
    )
    br_mine, br_send, g2 = call(
        functools.partial(gate_kernel, plan),
        [((tok, width), F32), ((tok, width), F32), ((inner, inner + width), BF16)],
        [idx, u, xc, ys, small_t] + pieces2,
        [SMEM] + [None] * 4 + [HBM] * len(pieces2),
        scratch=[fetch_sem],
        name="gate",
    )
    br_got = swap(br_send, "c")
    slots = Slots(capacity, 2 * width)
    disp, hidden, gate = call(
        functools.partial(moe_enter_kernel, slots, experts, capacity),
        [kept((8 * experts, slots.lanes), BF16), kept((tok, width), F32), kept((tok, LANES), F32)],
        [seq_lens, tokens, in_hbm(cotangent), routes.T, br_mine, br_got, in_hbm(dnat)],
        [SMEM] + [None] * 6,
        name="moe_enter",
    )
    disp = after(disp, part_two)
    line = exchange(disp, nf)
    peer = swap(line, "c")
    line_y = swap(line, "y")
    total = slots.rows(2 * nf)
    tail = max(slots.rows(2 * nf), 8)
    weight_s = pltpu.VMEM((hid, width), BF16)
    tail_s = pltpu.VMEM((tail, 2 * width), F32)
    early = sum(1 for spans in parts for span in spans if span[0] == 0)
    both, acc, act, slope, up_near = call(
        functools.partial(expert_own_kernel, slots, parts[:-1]),
        [((total, 2 * width), BF16), ((total, 2 * width), F32), ((total, hid), BF16), ((total, hid), F32), ((hid, width), BF16)],
        [line, peer] + [in_hbm(w) for w in (up_weight, down_weight, up_one, part_two)],
        [None, None] + [HBM] * 4,
        scratch=[weight_s, weight_s, tail_s, pltpu.SemaphoreType.DMA((2 + early,))],
        name="expert_own",
        us=6,
    )
    out_own, out_peer = call(
        functools.partial(expert_other_kernel, slots, parts[1:]),
        [(line.shape, F32), (line.shape, BF16)],
        [both, acc, act, slope, up_near, part_two, part_three],
        [None] * 5 + [HBM] * 2,
        scratch=[pltpu.VMEM((total, 2 * width), F32), weight_s, tail_s, pltpu.SemaphoreType.DMA((3,))],
        name="expert_other",
        us=3,
    )
    grads = [((1, hid, width), F32)] * 2
    weights = [in_hbm(up_weight), in_hbm(down_weight)]
    near = call(near_grad_kernel, grads, [both] + weights, name="near_grad", us=4)
    peer_y = swap(after(line_y, near[0]), "c")
    up_grad, down_grad = call(
        functools.partial(far_grad_kernel, slots),
        grads,
        [line_y, peer_y] + weights + near,
        scratch=[pltpu.VMEM((total, 2 * width), BF16), tail_s],
        name="far_grad",
        us=8,
    )
    summed = (out_own + swap(out_peer, "c").astype(F32)).astype(BF16)
    back = exchange(summed, nf)
    back = after(back, up_grad)
    result, ghid, gbr, dgrad = call(
        functools.partial(moe_leave_kernel, slots, experts, capacity),
        [((tok, width), BF16), ((tok, width), F32), ((tok, width), BF16), ((dn, width), F32)],
        [in_hbm(seq_lens), in_hbm(routes.T), in_hbm(cotangent), in_hbm(hidden), in_hbm(gate), in_hbm(dnat), back],
        [SMEM] + [None] * 6,
        name="moe_leave",
    )
    gbr_got = swap(gbr, "c")
    gy, gzg, *shared2 = call(
        functools.partial(gate_back_kernel, plan),
        [((rows, inner), F32), ((rows, inner), BF16)] + plan.shared_outs(inner + width),
        [idx, gbr, gbr_got, g2, xc, ys, small_t, u],
        [SMEM] + [None] * 7,
        scratch=[pltpu.VMEM((inner, inner + width), BF16), emit_sem],
        name="gate_back",
    )
    gsel, gxcs, gsr, q, smallg = call(
        functools.partial(scan_back_kernel, rank, states),
        [((rows, LANES), F32), ((rows, inner), F32), ((rows, inner), BF16), ((rows, LANES), BF16), ((small_n, inner), F32)],
        [lens2, gy, xc, sel, small_t, g1, in_hbm(check)],
        [SMEM] + [None] * 4 + [g1sel_spec, HBM],
        scratch=[pltpu.VMEM((rows, inner), F32)] * 4 + [pltpu.VMEM((2, states, tok), F32)] * 2 + [pltpu.VMEM((rows, GROUP_TOKENS * states), F32)] * 2 + [pltpu.VMEM((states, inner), F32), pltpu.VMEM((2, states, inner), F32), pltpu.VMEM((states, inner), F32), pltpu.VMEM((rows // GROUP_TOKENS, 2 * GROUP_TOKENS, GROUP_TOKENS * states), BF16)] + [pltpu.VMEM((2, GROUP_TOKENS * states, inner), BF16)] * 3 + [pltpu.VMEM((rows, inner), F32)] * 2 + [pltpu.VMEM((2 * chunks, states, inner), F32), pltpu.SemaphoreType.DMA],
        name="scan_back",
        us=16,
    )
    shared2[-1] = after(shared2[-1], gsel)
    sums2 = plan.reduce1(shared2, "two")
    gsel = after(gsel, sums2[0])
    gsel_got = swap(gsel, "c")
    gxin, *shared1 = call(
        functools.partial(leave_kernel, plan),
        [((rows, inner), BF16)] + plan.shared_outs(inner + 2 * LANES),
        [idx, lens2, nat, gsel, gsel_got, gxcs, gsr, q, smallg, xin, xc, u, small_t, g1, dgrad],
        [SMEM, SMEM] + [None] * 13,
        scratch=[pltpu.VMEM((inner, inner + 2 * LANES), BF16), emit_sem],
        name="leave",
        us=5,
    )
    square_spec = pl.BlockSpec((inner, inner), lambda i: (0, 0))
    gn_mine, gn_send = call(
        back_kernel,
        [((tok, width), F32), ((tok, width), F32)],
        [idx, nat, gxin, gzg, g1, g2],
        [SMEM, None, None, None, square_spec, square_spec],
        name="back",
        us=3,
    )
    sums2 = plan.reduce2(sums2, "two")
    parts2 = plan.reduce3(sums2)
    shared1 = [after(part, sums2[0]) for part in shared1]
    sums1 = plan.reduce1(shared1, "one")
    if plan.fast:
        sums1[-1] = after(sums1[-1], tuple(parts2))
    parts1 = plan.reduce3(plan.reduce2(sums1, "one"))
    gn_got = swap(gn_send, "c")
    (input_grad,) = call(
        final_kernel, [((tok, width), F32)], [tokens, gn_mine, gn_got, ghid, dnat], name="final", us=2
    )
    sel_n = select_proj.shape[1]
    keep_w, send_back, out_grad, select_grad, step_grad, taps_grad, cb, sb, sk, decay_grad = call(
        functools.partial(share_kernel, len(parts1), len(parts2), rank, states),
        [((dr, 2 * inner + LANES), F32)] * 2
        + [((er, width), F32), ((er, sel_n), F32), ((rank, er), F32), ((4, er), F32), ((1, er), F32), ((1, er), F32), ((1, er), F32), ((states, er), F32)],
        list(parts1) + list(parts2),
        scratch=[pltpu.VMEM((LANES, LANES), F32)],
        name="share",
        us=1,
    )
    in_grad, norm_grad, moe_grad, router_grad = call(
        functools.partial(spread_kernel, span),
        [((dr, 4 * inner), F32), ((1, dr), F32), ((1, dr), F32), ((experts, dr), F32)],
        [idx, keep_w, swap(send_back, "c"), input_proj, norm_gain[None]],
        [SMEM, None, None, None, None],
        scratch=[pltpu.VMEM((LANES, LANES), F32)],
        name="spread",
        us=1,
    )
    return (
        result,
        input_grad,
        norm_grad[0],
        in_grad,
        taps_grad,
        cb[0],
        select_grad,
        step_grad,
        sb[0],
        decay_grad,
        sk[0],
        out_grad,
        moe_grad[0],
        router_grad.T,
        up_grad,
        down_grad,
    )


def solution(mesh):
    dp, fsdp = mesh.shape["dp"], mesh.shape["fsdp"]
    ny, nx = dp // 2, 2
    nz = fsdp // nx
    fine = Mesh(mesh.devices.reshape(ny, 2, nz, nx), ALL)
    tok = P(ALL, None)
    vec = P(ALL)
    col = P(None, ALL)
    exp = P(("z", "x"), ("y", "c"), None)
    in_specs = (tok, tok, tok, tok, vec, tok, col, vec, tok, col, vec, col, vec, tok, vec, tok, exp, exp)
    out_specs = (tok, tok, vec, tok, col, vec, tok, col, vec, col, vec, tok, vec, tok, exp, exp)
    return jax.shard_map(
        functools.partial(body, (ny, nz, nx)), mesh=fine, in_specs=in_specs, out_specs=out_specs, check_vma=False
    )
```

```python
import functools

import jax
import jax.numpy as jnp
import numpy as np
from jax import lax
from jax.experimental import pallas as pl
from jax.experimental.pallas import tpu as pltpu
from jax.sharding import Mesh
from jax.sharding import PartitionSpec as P

EPS = 1e-05
F32 = jnp.float32
BF16 = jnp.bfloat16
LANES = 128
LOG2E = 1.4426950408889634
LN2 = 0.6931471805599453
GELU_C = 0.7978845608028654
GELU_K = 0.044715
ALL = ("y", "c", "z", "x")
GROUP = ("y", "z", "x")
ROW_BIAS, ROW_STEP, ROW_SKIP, ROW_DECAY = 4, 5, 6, 8
ROW_FEATURE = 64
NN = (((1,), (0,)), ((), ()))
NT = (((1,), (1,)), ((), ()))
TN = (((0,), (0,)), ((), ()))


def mm(left, right, dims=NN):
    return lax.dot_general(left, right, dims, preferred_element_type=F32)


def split_mm(left, right, dims=NN):
    high = left.astype(BF16)
    rest = left - high.astype(F32)
    mid = rest.astype(BF16)
    low = (rest - mid.astype(F32)).astype(BF16)
    return mm(high, right, dims) + (mm(mid, right, dims) + mm(low, right, dims))


def iota(shape, dim):
    return lax.broadcasted_iota(jnp.int32, shape, dim)


def sigmoid(v):
    return 1.0 / (1.0 + jnp.exp(-v))


def softplus(v):
    return jnp.maximum(v, 0.0) + jnp.log1p(jnp.exp(-jnp.abs(v)))


def positions(lens_ref, row, tok):
    pos = iota((tok, 1), 0)
    end = jnp.int32(0)
    start = jnp.zeros((tok, 1), jnp.int32)
    for j in range(lens_ref.shape[1]):
        length = lens_ref[row, j]
        end = end + length
        start = start + jnp.where(pos >= end, length, 0)
    return pos - start, pos < end


def both_offsets(lens_ref, tok):
    return jnp.concatenate([positions(lens_ref, row, tok)[0] for row in range(2)], axis=0)


def fold(parts):
    rows = iota((8, LANES), 0)
    step = 1
    while len(parts) > 1:
        first = (rows & step) == 0
        merged = []
        for k in range(0, len(parts), 2):
            a, b = parts[k], parts[k + 1]
            merged.append(jnp.where(first, a, b) + pltpu.roll(jnp.where(first, b, a), step, 0))
        parts = merged
        step *= 2
    return parts[0]


def call(kernel, outs, args, specs=None, scratch=(), name=None, us=5, vmem=32):
    whole = pl.BlockSpec(memory_space=pltpu.VMEM)
    specs = [None] * len(args) if specs is None else specs
    windowed = any(s is not None and s.block_shape is not None for s in specs)
    results = pl.pallas_call(
        kernel,
        grid=(1,) if windowed else (),
        out_shape=[(pltpu.HBM if len(o) > 3 else jax.ShapeDtypeStruct)(o[0], o[1]) for o in outs],
        in_specs=[whole if s is None else s for s in specs],
        out_specs=[whole if len(o) < 3 or o[2] is None else o[2] for o in outs],
        scratch_shapes=list(scratch),
        name=name,
        cost_estimate=pl.CostEstimate(flops=us * 300000000, bytes_accessed=us * 900000, transcendentals=0),
        compiler_params=pltpu.CompilerParams(vmem_limit_bytes=vmem << 20),
    )(*args)
    return list(results)


SMEM = pl.BlockSpec(memory_space=pltpu.SMEM)
HBM = pl.BlockSpec(memory_space=pl.ANY)


def perm_matrix(idx, nat_ref):
    width = nat_ref.shape[1]
    nat = jnp.where(idx[3] == 0, nat_ref[0:1], nat_ref[1:2])
    return (iota((width, width), 0) == nat).astype(F32).astype(BF16)


def kept(shape, dtype):
    return (shape, dtype, None, True)


def in_hbm(value):
    return pltpu.with_memory_space_constraint(value, pltpu.HBM)


def after(value, other):
    if other is None:
        return value
    return lax.optimization_barrier((value, other))[0]


class Plan:
    def __init__(self, ny, nz, nx, piece):
        self.ny, self.nz, self.nx, self.piece = ny, nz, nx, piece
        self.count = ny * nz * nx
        self.fast = (ny, nz, nx) == (2, 4, 2) and piece % 16 == 0

    def place(self, idx, yr, zr, xr):
        y = jnp.bitwise_xor(idx[0], yr)
        x = jnp.bitwise_xor(idx[2], xr)
        z = lax.rem(idx[1] - zr + self.nz, self.nz)
        return pl.multiple_of(((y * self.nz + z) * self.nx + x) * self.piece, self.piece)

    def gather(self, groups, first):
        if not self.fast:
            return [[lax.all_gather(piece, GROUP, axis=0, tiled=True)] for piece in groups]
        half = 2 * self.piece
        out, before_line, before_last = [], None, None
        for piece in groups:
            piece = after(piece, before_line)
            rots = [lax.ppermute(piece, "z", [(i, (i + k) % 4) for i in range(4)]) for k in (1, 2, 3)]
            line = jnp.concatenate([piece] + rots, axis=0)
            line = after(line, first if before_line is None else before_last)
            before_line = line
            by_x, by_y = swap(line, "x"), swap(line, "y")
            out.append([line, by_x, by_y, swap(by_x[:half], "y"), swap(by_y[half:], "x")])
            before_last = tuple(out[-1][3:])
        return out

    def pieces(self):
        n, out = self.piece, []
        for z in range(4):
            out.append((0, z * n, 0, z, 0))
            out.append((1, z * n, 0, z, 1))
            out.append((2, z * n, 1, z, 0))
            out.append((3 + z // 2, z % 2 * n, 1, z, 1))
        return out

    def n_gathered(self):
        return 5 if self.fast else 1

    def fetch(self, idx, refs, dst, sem):
        if not self.fast:
            copies = [pltpu.make_async_copy(refs[0], dst, sem.at[0])]
        else:
            copies = []
            for k, (r, row, yr, zr, xr) in enumerate(self.pieces()):
                to = dst.at[pl.ds(self.place(idx, yr, zr, xr), self.piece)]
                copies.append(pltpu.make_async_copy(refs[r].at[pl.ds(row, self.piece)], to, sem.at[k]))
        for copy in copies:
            copy.start()
        return copies

    def shared_outs(self, width):
        if not self.fast:
            return [((self.count * self.piece, width), BF16, HBM)]
        return [((8 * self.piece, width // 2), BF16, HBM)] * 4

    def n_shared(self):
        return 4 if self.fast else 1

    def emit(self, idx, src, refs, sem):
        if not self.fast:
            copies = [pltpu.make_async_copy(src, refs[0], sem.at[0])]
        else:
            copies, n, half = [], self.piece, src.shape[1] // 2
            for zr in range(4):
                for yr in range(2):
                    for xr in range(2):
                        at = self.place(idx, yr, zr, xr)
                        for lanes, ref, row in (
                            (0, refs[2 - 2 * xr], yr * 4 + zr),
                            (half, refs[3 - 2 * yr], xr * 4 + zr),
                        ):
                            copies.append(
                                pltpu.make_async_copy(
                                    src.at[pl.ds(at, n), pl.ds(lanes, half)],
                                    ref.at[pl.ds(row * n, n)],
                                    sem.at[len(copies)],
                                )
                            )
        for copy in copies:
            copy.start()
        return copies

    def reduce1(self, shared, tag):
        if not self.fast:
            return shared
        a_send, b_send, a_keep, b_keep = shared
        n, half = self.piece, a_send.shape[1]
        a_got, b_got = swap(a_send, "x"), swap(b_send, "y")
        shape = ((4 * n, half), BF16)
        return call(add_kernel, [shape] * 4, [a_keep, a_got, b_keep, b_got], name="add1_" + tag, us=1)

    def reduce2(self, sums, tag):
        if not self.fast:
            return sums
        a_send, a_keep, b_send, b_keep = sums
        n, half = self.piece, a_send.shape[1]
        a_got, b_got = swap(a_send, "y"), swap(b_send, "x")
        outs = [((n, 2 * half), BF16)] * 4
        return call(line_kernel, outs, [a_keep, a_got, b_keep, b_got], name="add2_" + tag, us=1)

    def reduce3(self, parts):
        if not self.fast:
            shares = parts[0].reshape(self.count, self.piece, -1)
            shares = lax.all_to_all(shares, GROUP, split_axis=0, concat_axis=0, tiled=True)
            return [shares.astype(F32).sum(axis=0)]
        rots = [lax.ppermute(parts[k], "z", [(i, (i - k) % 4) for i in range(4)]) for k in (1, 2, 3)]
        return [parts[0]] + rots


def add_kernel(a, a_in, b, b_in, a_send, a_keep, b_send, b_keep):
    cut = a_send.shape[0]
    for one, two, send, keep in ((a, a_in, a_send, a_keep), (b, b_in, b_send, b_keep)):
        send[...] = (one[cut:].astype(F32) + two[cut:].astype(F32)).astype(BF16)
        keep[...] = (one[:cut].astype(F32) + two[:cut].astype(F32)).astype(BF16)


def line_kernel(a, a_in, b, b_in, *outs):
    n, half = outs[0].shape[0], a.shape[1]
    for k, out in enumerate(outs):
        span = slice(k * n, (k + 1) * n)
        out[:, :half] = (a[span].astype(F32) + a_in[span].astype(F32)).astype(BF16)
        out[:, half:] = (b[span].astype(F32) + b_in[span].astype(F32)).astype(BF16)


def pack_kernel(
    span, idx, in_proj, norm, moe, router, taps, cbias, select, step, sbias, decay, skip, up,
    mine_o, send_o, ch_o, up_o, rows_s, block_s, sem,
):
    copy = pltpu.make_async_copy(up.at[0, pl.ds(0, up_o.shape[0])], up_o, sem)
    copy.start()
    dr = in_proj.shape[0]
    er, sel_n = select.shape
    rank, states = step.shape[0], decay.shape[0]
    inner2 = mine_o.shape[1] - LANES
    first = idx[3] == 0
    for k in range(inner2 // span):
        low = in_proj[:, 2 * k * span : (2 * k + 1) * span]
        high = in_proj[:, (2 * k + 1) * span : (2 * k + 2) * span]
        mine_o[:, k * span : (k + 1) * span] = jnp.where(first, low, high)
        send_o[:, k * span : (k + 1) * span] = jnp.where(first, high, low)
    rows_s[...] = jnp.zeros_like(rows_s)
    rows_s[0:4, :er] = taps[...].astype(F32)
    rows_s[ROW_BIAS : ROW_BIAS + 1, :er] = cbias[...].astype(F32)
    rows_s[ROW_STEP : ROW_STEP + 1, :er] = sbias[...].astype(F32)
    rows_s[ROW_SKIP : ROW_SKIP + 1, :er] = skip[...].astype(F32)
    rows_s[ROW_DECAY : ROW_DECAY + states, :er] = decay[...].astype(F32)
    ch_o[:, LANES:] = jnp.transpose(rows_s[...])[:er].astype(BF16)
    rows_s[...] = jnp.zeros_like(rows_s)
    rows_s[LANES - rank :, :er] = step[...].astype(F32)
    block_s[...] = jnp.zeros_like(block_s)
    block_s[:er, :sel_n] = select[...].astype(F32)
    ch_o[:, :LANES] = (block_s[:er] + jnp.transpose(rows_s[...])[:er]).astype(BF16)
    rows_s[...] = jnp.zeros_like(rows_s)
    rows_s[ROW_FEATURE : ROW_FEATURE + 1, :dr] = norm[...].astype(F32)
    rows_s[ROW_FEATURE + 1 : ROW_FEATURE + 2, :dr] = moe[...].astype(F32)
    rows_s[ROW_FEATURE + 2 : ROW_FEATURE + 2 + router.shape[0], :dr] = router[...].astype(F32)
    feature = jnp.transpose(rows_s[...])[:dr].astype(BF16)
    mine_o[:, inner2:] = feature
    send_o[:, inner2:] = feature
    copy.wait()


def cut_rows(sizes, hidden):
    parts, at = [], 0
    for size in sizes:
        spans, end = [], at + size
        if at < hidden:
            spans.append((0, at, 0, min(end, hidden) - at))
        if end > hidden:
            low = max(at, hidden)
            spans.append((1, low - hidden, low - at, end - low))
        parts.append(spans)
        at = end
    return parts


def split_kernel(parts, up, down, *refs):
    outs, sem = refs[:-1], refs[-1]
    copies = []
    for spans, out in zip(parts, outs, strict=True):
        for which, row, at, size in spans:
            source = (up, down)[which].at[0, pl.ds(row, size)]
            copies.append(pltpu.make_async_copy(source, out.at[pl.ds(at, size)], sem.at[len(copies)]))
    for copy in copies:
        copy.start()
    for copy in copies:
        copy.wait()


def merge_kernel(mine, got, ch, out_proj, one_o, two_o):
    inner = out_proj.shape[1]
    both = jnp.concatenate([mine[...].astype(F32), got[...].astype(F32)], axis=0).astype(BF16)
    one_o[:, :inner] = both[:, :inner]
    one_o[:, inner : inner + LANES] = ch[:, :LANES]
    one_o[:, inner + LANES :] = ch[:, LANES:] + both[:, 2 * inner :]
    two_o[:, :inner] = both[:, inner : 2 * inner]
    two_o[:, inner:] = out_proj[...]


def enter_kernel(plan, idx, lens, tok2, nat, *refs):
    n = plan.n_gathered()
    pieces = refs[:n]
    u_o, xin_o, xc_o, sel_o, small_o, dnat_o, g1, sem = refs[n:]
    copies = plan.fetch(idx, pieces, g1, sem)
    rows, width = tok2.shape
    tok = rows // 2
    inner = xin_o.shape[1]
    perm = perm_matrix(idx, nat)
    vals = tok2[...].astype(F32)
    scale = lax.rsqrt(jnp.mean(vals * vals, axis=1, keepdims=True) + EPS)
    offset = both_offsets(lens, tok)
    for copy in copies:
        copy.wait()
    table = g1[:, inner + LANES :]
    dnat = mm(table, perm, (((0,), (1,)), ((), ())))[ROW_FEATURE:]
    dnat_o[...] = dnat[: dnat_o.shape[0]]
    u = (vals * scale * dnat[0:1]).astype(BF16)
    u = mm(u, perm).astype(BF16)
    u_o[...] = u
    xin = mm(u, g1[:, :inner])
    xin_o[...] = xin
    small = jnp.transpose(table.astype(F32))[: small_o.shape[0]]
    small_o[...] = small
    conv = conv_of(xin, small, offset)
    xc = (conv * sigmoid(conv)).astype(BF16)
    xc_o[...] = xc
    sel_o[...] = mm(xc, g1[:, inner : inner + LANES])


def conv_of(xin, small, offset):
    conv = small[ROW_BIAS : ROW_BIAS + 1] + small[3:4] * xin
    for lag in range(1, 4):
        moved = pltpu.roll(xin, lag, 0)
        conv = conv + jnp.where(offset >= lag, small[3 - lag : 4 - lag] * moved, 0.0)
    return conv


def swap_halves(rows):
    half = rows.shape[0] // 2
    return jnp.concatenate([rows[half:], rows[:half]], axis=0)


GROUP_TOKENS = 16


def spread_rows(sel, first, states):
    rows, n = sel.shape[0], GROUP_TOKENS
    wide = (LANES, n * states)
    pick = (iota(wide, 0) == first + iota(wide, 1) % states).astype(F32).astype(BF16)
    values = split_mm(sel, pick)
    own = iota((rows, n * states), 1) // states == iota((rows, n * states), 0) % n
    values = jnp.where(own, values, 0.0).reshape(rows // n, n, n * states)
    high = values.astype(BF16).astype(F32)
    return jnp.concatenate([high, values - high], axis=1).astype(BF16)


def two_terms(block):
    high = block.astype(BF16).astype(F32)
    return jnp.concatenate([high, block - high], axis=0).astype(BF16)


def halves(block):
    n = block.shape[0] // 2
    return block[:n] + block[n:]


def step_inputs(sel, rank):
    tail = LANES - rank
    return jnp.where(iota(sel.shape, 1) >= tail, pltpu.roll(sel, tail, 1), 0.0).astype(BF16)


def step_of(q, g1sel, small):
    return mm(q, g1sel[...], NT) + small[ROW_STEP : ROW_STEP + 1]


def scan_kernel(
    rank, states, lens, sel_a, sel_b, xc, g1sel, small,
    ys_o, sel_o, check_o,
    dm_s, dx_s, wr_s, rd_s, rate_s, h_s, check_s, sem,
):
    rows, inner = ys_o.shape
    tok = rows // 2
    sel = sel_a[...] + swap_halves(sel_b[...])
    sel_o[...] = sel
    delta = softplus(step_of(step_inputs(sel, rank), g1sel, small))
    offset = both_offsets(lens, tok)
    xcf = xc[...].astype(F32)
    dm_s[...] = jnp.where(offset > 0, delta, 1e30)
    dx_s[...] = delta * xcf
    for b in range(2):
        turned = jnp.transpose(sel[b * tok : (b + 1) * tok])
        wr_s[b] = turned[rank : rank + states]
        rd_s[b] = turned[rank + states : rank + 2 * states]
    rate_s[...] = jnp.exp(small[ROW_DECAY : ROW_DECAY + states]) * (-LOG2E)
    h_s[...] = jnp.zeros_like(h_s)
    half = states // 2

    def chunk(ci, carry):
        t0 = pl.multiple_of(ci * 8, 8)
        for b in range(2):
            at = pl.multiple_of(b * tok + t0, 8)
            wr8 = pltpu.roll(wr_s[b], tok - t0, 1)
            rd8 = pltpu.roll(rd_s[b], tok - t0, 1)
            wcol = [jnp.broadcast_to(wr8[:, j : j + 1], (states, LANES)) for j in range(8)]
            rcol = [jnp.broadcast_to(rd8[:, j : j + 1], (states, LANES)) for j in range(8)]
            for g in range(inner // LANES):
                lanes = slice(g * LANES, (g + 1) * LANES)
                h = h_s[b, :, lanes]
                check_s[ci * 2 + b, :, lanes] = h
                rate = rate_s[:, lanes]
                dm8 = dm_s[pl.ds(at, 8), lanes]
                dx8 = dx_s[pl.ds(at, 8), lanes]
                parts = []
                for j in range(8):
                    d = jnp.broadcast_to(dm8[j : j + 1], (states, LANES))
                    x = jnp.broadcast_to(dx8[j : j + 1], (states, LANES))
                    h = jnp.exp2(d * rate) * h + wcol[j] * x
                    p = rcol[j] * h
                    parts.append(p[:half] + p[half:])
                ys_o[pl.ds(at, 8), lanes] = fold(parts)
                h_s[b, :, lanes] = h
        saved(ci).start()
        return carry

    def saved(ci):
        pair = pl.ds(2 * ci, 2)
        return pltpu.make_async_copy(check_s.at[pair], check_o.at[pair], sem.at[ci])

    lax.fori_loop(0, tok // 8, chunk, 0)
    for ci in range(tok // 8):
        saved(ci).wait()


def gate_kernel(plan, idx, u, xc, ys, small, *refs):
    n = plan.n_gathered()
    pieces = refs[:n]
    mine_o, send_o, g2, sem = refs[n:]
    copies = plan.fetch(idx, pieces, g2, sem)
    for copy in copies:
        copy.wait()
    inner = ys.shape[1]
    tok = mine_o.shape[0]
    zg = mm(u[...], g2[:, :inner])
    gated = (ys[...] + small[ROW_SKIP : ROW_SKIP + 1] * xc[...].astype(F32)) * (zg * sigmoid(zg))
    gated = gated.astype(BF16)
    branch = mm(gated, g2[:, inner:])
    mine_o[...] = branch[:tok]
    send_o[...] = branch[tok:]


def route_tables(lens, routes, experts, capacity, tok):
    _, valid = positions(lens, 0, tok)
    valid_f = valid.astype(F32)
    width = max(LANES, experts)
    hot = (routes == iota((tok, width), 1)).astype(F32)
    live = hot * valid_f
    earlier = (iota((tok, tok), 1) < iota((tok, tok), 0)).astype(F32).astype(BF16)
    before = mm(earlier, live.astype(BF16))
    rank = jnp.sum(before * hot, axis=1, keepdims=True).astype(jnp.int32)
    kept = valid & (rank < capacity)
    return valid_f, hot, rank, kept


def column_of(row):
    n = row.shape[1]
    square = iota((n, n), 0) == iota((n, n), 1)
    return jnp.sum(jnp.where(square, row[...].astype(F32), 0.0), axis=1, keepdims=True).astype(jnp.int32)


class Slots:
    def __init__(self, capacity, width):
        self.full, left = divmod(capacity, 8)
        self.split = 0 < left <= 4
        if left > 4:
            self.full += 1
        self.width = width
        self.lanes = self.full * width + (width // 2 if self.split else 0)

    def rows(self, groups):
        return groups * 8 * self.full + (groups * 4 if self.split else 0)

    def hot(self, routes, rank, kept, experts, first, low, high):
        shape = (rank.shape[0], 8 * experts)
        place = iota(shape, 1)
        row = place % 8
        inside = kept & (routes == place // 8) & (rank == first + row - low)
        return jnp.where(inside & (row >= low) & (row < high), 1.0, 0.0).astype(BF16)

    def hots(self, routes, rank, kept, experts):
        args = (routes, rank, kept, experts)
        whole = [self.hot(*args, 8 * i, 0, 8) for i in range(self.full)]
        last = [self.hot(*args, 8 * self.full, 4 * i, 4 * i + 4) for i in range(2)] if self.split else []
        return whole, last

    def unpack(self, groups, both, tail_s):
        at, width, height = 0, self.width, groups[0].shape[0]
        for group in groups:
            for i in range(self.full):
                both[at : at + height] = group[:, i * width : (i + 1) * width]
                at += height
        if self.split:
            half, start, count = width // 2, 0, height // 8
            for group in groups:
                block = group[:, self.full * width :].astype(F32)
                for k in range(count):
                    tail_s[start + 4 * k : start + 4 * k + 4, :half] = block[8 * k : 8 * k + 4]
                    tail_s[start + 4 * k : start + 4 * k + 4, half:] = block[8 * k + 4 : 8 * k + 8]
                start += 4 * count
            both[at : at + start] = tail_s[:start].astype(BF16)

    def pack(self, rows, which, count, out, tail_s):
        width, height = self.width, out.shape[0]
        at = which * self.full * height
        for i in range(self.full):
            out[:, i * width : (i + 1) * width] = rows[at : at + height].astype(out.dtype)
            at += height
        if self.split:
            half = width // 2
            at = count * self.full * height + which * height // 2
            for k in range(height // 8):
                tail_s[8 * k : 8 * k + 4, :half] = rows[at + 4 * k : at + 4 * k + 4, :half]
                tail_s[8 * k + 4 : 8 * k + 8, :half] = rows[at + 4 * k : at + 4 * k + 4, half:]
            out[:, self.full * width :] = tail_s[:height, :half].astype(out.dtype)


def moe_enter_kernel(slots, experts, capacity, lens, tok, cot, routes, mine, got, dnat, disp_o, hidden_o, gate_o):
    rows, width = tok.shape
    routes = column_of(routes)
    hidden = tok[...].astype(F32) + (mine[...] + got[...])
    hidden_o[...] = hidden
    scale = lax.rsqrt(jnp.mean(hidden * hidden, axis=1, keepdims=True) + EPS)
    mv = (hidden * scale * dnat[1:2]).astype(BF16)
    logits = mm(mv, dnat[...].astype(BF16), NT)
    hot = (routes + 2 == iota(logits.shape, 1)).astype(F32)
    gate = sigmoid(jnp.sum(logits * hot, axis=1, keepdims=True))
    gate_o[...] = jnp.broadcast_to(gate, gate_o.shape)
    valid_f, _, rank, kept = route_tables(lens, routes, experts, capacity, rows)
    back = (cot[...].astype(F32) * valid_f * (gate * kept.astype(F32))).astype(BF16)
    both = jnp.concatenate([mv, back], axis=1)
    whole, last = slots.hots(routes, rank, kept, experts)
    span = slots.width
    for i, hot in enumerate(whole):
        disp_o[:, i * span : (i + 1) * span] = mm(hot, both, TN).astype(BF16)
    if last:
        end = mm(last[0], both[:, : span // 2], TN) + mm(last[1], both[:, span // 2 :], TN)
        disp_o[:, slots.full * span :] = end.astype(BF16)


def half_units(both, up, span):
    width = up.shape[1]
    pre = mm(both[:, :width], up[span], NT)
    sq = pre * pre
    th = jnp.tanh(GELU_C * (pre + GELU_K * sq * pre))
    act = (0.5 * pre * (1.0 + th)).astype(BF16)
    return act, 0.5 * (1.0 + th) + 0.5 * pre * (1.0 - th * th) * (GELU_C * (1.0 + 3.0 * GELU_K * sq))


def moves_of(parts, refs, targets, which_of):
    moves = []
    for spans, ref in zip(parts, refs, strict=True):
        for which, row, at, size in spans:
            if which in which_of:
                moves.append((ref.at[pl.ds(at, size)], targets[which].at[pl.ds(row, size)]))
    return moves


PART = 768


def expert_own_kernel(slots, parts, own, peer, up, down, *refs):
    others = refs[: len(parts)]
    both, acc, act_o, slope_o, up_o, up_s, down_s, tail_s, sem = refs[len(parts) :]
    moves = [(up.at[0], up_s), (down.at[0], down_s)] + moves_of(parts, others, (up_o, None), (0,))
    copies = [pltpu.make_async_copy(a, b, sem.at[k]) for k, (a, b) in enumerate(moves)]
    for copy in copies:
        copy.start()
    slots.unpack((own, peer), both, tail_s)
    width = up.shape[2]
    for copy in copies:
        copy.wait()
    for f in range(0, up_s.shape[0], PART):
        span = slice(f, f + PART)
        act, slope = half_units(both, up_s, span)
        g_pre = (mm(both[:, width:], down_s[span], NT) * slope).astype(BF16)
        e_part = mm(act, down_s[span])
        i_part = mm(g_pre, up_s[span])
        if f == 0:
            acc[:, :width] = e_part
            acc[:, width:] = i_part
        else:
            acc[:, :width] += e_part
            acc[:, width:] += i_part
        act, slope = half_units(both, up_o, span)
        act_o[:, span] = act
        slope_o[:, span] = slope


def expert_other_kernel(slots, parts, both, acc, act, slope, up, *refs):
    others = refs[: len(parts)]
    out_own, out_peer, acc_s, down_s, tail_s, sem = refs[len(parts) :]
    moves = moves_of(parts, others, (None, down_s), (1,))
    copies = [pltpu.make_async_copy(a, b, sem.at[k]) for k, (a, b) in enumerate(moves)]
    for copy in copies:
        copy.start()
    width = up.shape[1]
    for copy in copies:
        copy.wait()
    for f in range(0, up.shape[0], PART):
        span = slice(f, f + PART)
        g_pre = (mm(both[:, width:], down_s[span], NT) * slope[:, span]).astype(BF16)
        e_part = mm(act[:, span], down_s[span])
        i_part = mm(g_pre, up[span])
        old = acc if f == 0 else acc_s
        acc_s[:, :width] = old[:, :width] + e_part
        acc_s[:, width:] = old[:, width:] + i_part
    slots.pack(acc_s, 1, 2, out_peer, tail_s)
    slots.pack(acc_s, 0, 2, out_own, tail_s)


def unit_grads(both, up, down, up_g, down_g, more):
    width = up.shape[2]
    for f in range(0, up.shape[1], PART):
        span = slice(f, f + PART)
        act, slope = half_units(both, up.at[0], span)
        g_pre = (mm(both[:, width:], down[0, span], NT) * slope).astype(BF16)
        to_down = mm(act, both[:, width:], TN)
        to_up = mm(g_pre, both[:, :width], TN)
        if more is not None:
            to_up, to_down = to_up + more[0][0, span], to_down + more[1][0, span]
        down_g[0, span] = to_down
        up_g[0, span] = to_up


def near_grad_kernel(both, up, down, up_g, down_g):
    unit_grads(both, up, down, up_g, down_g, None)


def far_grad_kernel(slots, own_y, peer_y, up, down, up_near, down_near, up_g, down_g, both_s, tail_s):
    slots.unpack((own_y, peer_y), both_s, tail_s)
    unit_grads(both_s, up, down, up_g, down_g, (up_near, down_near))


def moe_leave_kernel(
    slots, experts, capacity, lens, routes, cot, hidden, gate_in, dnat, back,
    out_o, ghid_o, gbr_o, dgrad_o,
):
    rows, width = hidden.shape
    routes = column_of(routes)
    valid_f, _, rank, kept = route_tables(lens, routes, experts, capacity, rows)
    kept_f = kept.astype(F32)
    gate = gate_in[:, 0:1]
    whole, last = slots.hots(routes, rank, kept, experts)
    span = slots.width
    picked = jnp.zeros((rows, 2 * width), F32)
    for i, hot in enumerate(whole):
        picked = picked + mm(hot, back[:, i * span : (i + 1) * span])
    if last:
        end = back[:, slots.full * span :]
        picked = picked + jnp.concatenate([mm(last[0], end), mm(last[1], end)], axis=1)
    ex_out = picked[:, :width]
    sent = picked[:, width:]
    hid = hidden[...]
    out_o[...] = (valid_f * (hid + gate * ex_out)).astype(BF16)
    gy = cot[...].astype(F32) * valid_f
    g_gate = jnp.sum(gy * ex_out, axis=1, keepdims=True)
    chosen = g_gate * gate * (1.0 - gate)
    small_rows = dnat.shape[0]
    hot = (routes + 2 == iota((rows, small_rows), 1)).astype(F32)
    g_logit = (chosen * hot).astype(BF16)
    g_mv = mm(g_logit, dnat[...].astype(BF16)) + sent
    scale = lax.rsqrt(jnp.mean(hid * hid, axis=1, keepdims=True) + EPS)
    hat = hid * scale
    gain = dnat[1:2]
    mv = (hat * gain).astype(BF16)
    router_g = mm(g_logit, mv, TN)
    gain_g = jnp.sum(g_mv * hat, axis=0, keepdims=True)
    dgrad_o[...] = jnp.where(iota(dgrad_o.shape, 0) == 1, gain_g, router_g)
    gg = g_mv * gain
    mean = jnp.sum(gg * hat, axis=1, keepdims=True) * (1.0 / width)
    ghid = gy + scale * (gg - hat * mean)
    ghid_o[...] = ghid
    gbr_o[...] = ghid.astype(BF16)


def gate_back_kernel(plan, idx, gbr_a, gbr_b, g2, xc, ys, small, u, *refs):
    n = plan.n_shared()
    gy_o, gzg_o = refs[:2]
    shared = refs[2 : 2 + n]
    grad_s, sem = refs[2 + n :]
    inner = ys.shape[1]
    gbr = jnp.concatenate([gbr_a[...], gbr_b[...]], axis=0)
    g_gated = mm(gbr, g2[:, inner:], NT)
    skip = small[ROW_SKIP : ROW_SKIP + 1]
    zg = mm(u[...], g2[:, :inner])
    sig = sigmoid(zg)
    silu = zg * sig
    out = ys[...] + skip * xc[...].astype(F32)
    gy_o[...] = g_gated * silu
    gzg = (g_gated * out * (sig * (1.0 + zg * (1.0 - sig)))).astype(BF16)
    gzg_o[...] = gzg
    grad_s[:, :inner] = mm(u[...], gzg, TN).astype(BF16)
    grad_s[:, inner:] = mm((out * silu).astype(BF16), gbr, TN).astype(BF16)
    for copy in plan.emit(idx, grad_s, shared, sem):
        copy.wait()


def scan_back_kernel(
    rank, states, lens, gy_s, xc, sel, small, g1sel, check_in,
    gsel_o, gxcs_o, gsr_o, q_o, smallg_o,
    dm_s, dx_s, gdx_s, gdl_s, wr_s, rd_s, gwr_s, grd_s, rate_s, lam_s, ga_s, write_s, hb_s, lb_s, wb_s, delta_s, sig_s,
    check, sem,
):
    copy = pltpu.make_async_copy(check_in, check, sem)
    copy.start()
    rows, inner = gy_s.shape
    tok = rows // 2
    xcf = xc[...].astype(F32)
    skip = small[ROW_SKIP : ROW_SKIP + 1]
    q = step_inputs(sel[...], rank)
    q_o[...] = q
    step_pre = step_of(q, g1sel, small)
    delta_s[...] = softplus(step_pre)
    sig_s[...] = sigmoid(step_pre)
    delta = delta_s[...]
    dm_s[...] = jnp.where(both_offsets(lens, tok) > 0, delta, 1e30)
    dx_s[...] = delta * xcf
    for b in range(2):
        turned = jnp.transpose(sel[b * tok : (b + 1) * tok])
        wr_s[b] = turned[rank : rank + states]
        rd_s[b] = turned[rank + states : rank + 2 * states]
    rate_s[...] = jnp.exp(small[ROW_DECAY : ROW_DECAY + states]) * (-LOG2E)
    lam_s[...] = jnp.zeros_like(lam_s)
    ga_s[...] = jnp.zeros_like(ga_s)
    write_s[...] = spread_rows(sel[...], rank, states)
    shape = (states, LANES)
    n = GROUP_TOKENS
    count = tok // n
    wide = (n, n * states)
    own = iota(wide, 1) // states == iota(wide, 0)
    group = own.astype(F32).astype(BF16)
    for ref in (hb_s, lb_s, wb_s):
        ref[1] = jnp.zeros(ref.shape[1:], BF16)

    def sums(b, ci):
        span = pl.ds(pl.multiple_of(b * tok + ci * n, n), n)
        gdx_s[span, :] = halves(mm(write_s[b * count + ci], lb_s[b]))
        gdl_s[span, :] = mm(group, wb_s[b])
        grd_s[span, :] = jnp.where(own, halves(mm(two_terms(gy_s[span, :]), hb_s[b], NT)), 0.0)
        gwr_s[span, :] = jnp.where(own, halves(mm(two_terms(dx_s[span, :]), lb_s[b], NT)), 0.0)

    def chunk(i, carry):
        ci = count - 1 - i
        sums(1, jnp.minimum(ci + 1, count - 1))
        for b in range(2):
            for part in range(n // 8 - 1, -1, -1):
                t0 = pl.multiple_of(ci * n + part * 8, 8)
                at = pl.multiple_of(b * tok + t0, 8)
                wr8 = pltpu.roll(wr_s[b], tok - t0, 1)
                rd8 = pltpu.roll(rd_s[b], tok - t0, 1)
                wcol = [jnp.broadcast_to(wr8[:, j : j + 1], shape) for j in range(8)]
                rcol = [jnp.broadcast_to(rd8[:, j : j + 1], shape) for j in range(8)]
                for g in range(inner // LANES):
                    lanes = slice(g * LANES, (g + 1) * LANES)
                    h = check[(ci * (n // 8) + part) * 2 + b, :, lanes]
                    rate = rate_s[:, lanes]
                    dm8 = dm_s[pl.ds(at, 8), lanes]
                    dx8 = dx_s[pl.ds(at, 8), lanes]
                    gy8 = gy_s[pl.ds(at, 8), lanes]
                    decays, olds = [], []
                    for j in range(8):
                        k = part * 8 + j
                        d = jnp.broadcast_to(dm8[j : j + 1], shape)
                        x = jnp.broadcast_to(dx8[j : j + 1], shape)
                        a = jnp.exp2(d * rate)
                        old = a * h
                        h = old + wcol[j] * x
                        hb_s[b, k * states : (k + 1) * states, lanes] = h.astype(BF16)
                        decays.append(a)
                        olds.append(old)
                    lam_in = lam_s[b, :, lanes]
                    ga = ga_s[:, lanes]
                    for j in range(7, -1, -1):
                        k = part * 8 + j
                        lam = rcol[j] * jnp.broadcast_to(gy8[j : j + 1], shape) + lam_in
                        lam_in = decays[j] * lam
                        w = lam * olds[j]
                        ga = ga + w * jnp.broadcast_to(dm8[j : j + 1], shape)
                        lb_s[b, k * states : (k + 1) * states, lanes] = lam.astype(BF16)
                        wb_s[b, k * states : (k + 1) * states, lanes] = (w * rate).astype(BF16)
                    lam_s[b, :, lanes] = lam_in
                    ga_s[:, lanes] = ga
            if b == 0:
                sums(0, ci)
        return carry

    copy.wait()
    lax.fori_loop(0, count, chunk, 0)
    sums(1, 0)
    delta = delta_s[...]
    gdx = gdx_s[...]
    xcf = xc[...].astype(F32)
    gy = gy_s[...]
    gxcs_o[...] = gy * skip + gdx * delta
    g_step = (gdx * xcf + LN2 * gdl_s[...]) * sig_s[...]
    gsr = g_step.astype(BF16)
    gsr_o[...] = gsr
    lane = iota((rows, LANES), 1)
    tail = LANES - rank
    back = jnp.where(lane >= tail, mm(gsr, g1sel[...]), 0.0)
    back = pltpu.roll(back, rank, 1)
    tall = (n * states, LANES)
    place = iota(tall, 0) % states
    to_wr = (iota(tall, 1) == rank + place).astype(F32).astype(BF16)
    to_rd = (iota(tall, 1) == rank + states + place).astype(F32).astype(BF16)
    gsel_o[...] = back + split_mm(gwr_s[...], to_wr) + split_mm(grd_s[...], to_rd)
    smallg_o[0:ROW_STEP] = jnp.zeros((ROW_STEP, inner), F32)
    smallg_o[ROW_STEP : ROW_STEP + 1] = jnp.sum(g_step, axis=0, keepdims=True)
    smallg_o[ROW_SKIP : ROW_SKIP + 1] = jnp.sum(gy * xcf, axis=0, keepdims=True)
    smallg_o[ROW_SKIP + 1 : ROW_DECAY] = jnp.zeros((ROW_DECAY - ROW_SKIP - 1, inner), F32)
    smallg_o[ROW_DECAY : ROW_DECAY + states] = ga_s[...] * rate_s[...] * LN2
    rest = smallg_o.shape[0] - ROW_DECAY - states
    if rest:
        smallg_o[ROW_DECAY + states :] = jnp.zeros((rest, inner), F32)


def leave_kernel(
    plan, idx, lens, nat, gsel_a, gsel_b, gxcs, gsr, q, smallg, xin, xc, u, small, g1, dgrad, gxin_o, *refs
):
    n = plan.n_shared()
    shared = refs[:n]
    grad_s, sem = refs[n:]
    rows, inner = xin.shape
    tok = rows // 2
    perm = perm_matrix(idx, nat)
    g_sel = (gsel_a[...] + swap_halves(gsel_b[...])).astype(BF16)
    selblk = g1[:, inner : inner + LANES]
    block = mm(xc[...], g_sel, TN) + mm(gsr[...], q[...], TN)
    grad_s[:, inner : inner + LANES] = block.astype(BF16)
    g_xc = mm(g_sel, selblk, NT) + gxcs[...]
    offset = both_offsets(lens, tok)
    x = xin[...]
    sm = small[...]
    conv = conv_of(x, sm, offset)
    sig = sigmoid(conv)
    g_conv = g_xc * (sig * (1.0 + conv * (1.0 - sig)))
    g_xin = sm[3:4] * g_conv
    taps = [None, None, None, jnp.sum(g_conv * x, axis=0, keepdims=True)]
    for lag in range(1, 4):
        held = jnp.where(offset >= lag, g_conv, 0.0)
        g_xin = g_xin + sm[3 - lag : 4 - lag] * pltpu.roll(held, rows - lag, 0)
        taps[3 - lag] = jnp.sum(held * pltpu.roll(x, lag, 0), axis=0, keepdims=True)
    g_bias = jnp.sum(g_conv, axis=0, keepdims=True)
    g_xin = g_xin.astype(BF16)
    gxin_o[...] = g_xin
    grad_s[:, :inner] = mm(u[...], g_xin, TN).astype(BF16)
    dg = split_mm(dgrad[...], perm)
    top = jnp.concatenate(taps + [g_bias, jnp.zeros((3, inner), F32)], axis=0)
    gap = jnp.zeros((ROW_FEATURE - smallg.shape[0], inner), F32)
    end = jnp.zeros((LANES - ROW_FEATURE - dg.shape[0], inner), F32)
    table = jnp.concatenate([smallg[0:8] + top, smallg[8:], gap, dg, end], axis=0)
    grad_s[:, inner + LANES :] = jnp.transpose(table).astype(BF16)
    for copy in plan.emit(idx, grad_s, shared, sem):
        copy.wait()


def back_kernel(idx, nat, gxin, gzg, g1x, g2z, mine_o, send_o):
    tok = mine_o.shape[0]
    gn = mm(gxin[...], g1x[...], NT) + mm(gzg[...], g2z[...], NT)
    gn = split_mm(gn, perm_matrix(idx, nat), NT)
    mine_o[...] = gn[:tok]
    send_o[...] = gn[tok:]


def final_kernel(tok, mine, got, ghid, dnat, out_o):
    width = tok.shape[1]
    vals = tok[...].astype(F32)
    scale = lax.rsqrt(jnp.mean(vals * vals, axis=1, keepdims=True) + EPS)
    hat = vals * scale
    gg = (mine[...] + got[...]) * dnat[0:1]
    mean = jnp.sum(gg * hat, axis=1, keepdims=True) * (1.0 / width)
    out_o[...] = ghid[...] + scale * (gg - hat * mean)


def swap(values, axis):
    return lax.ppermute(values, axis, [(0, 1), (1, 0)])


def exchange(rows, count):
    parts = rows.reshape(count, 8, rows.shape[1])
    parts = lax.all_to_all(parts, ("z", "x"), split_axis=0, concat_axis=0, tiled=True)
    return parts.reshape(rows.shape)


def share_kernel(n1, n2, rank, states, *refs):
    one, two = refs[:n1], refs[n1 : n1 + n2]
    keep_o, send_o, outg_o, select_o, step_o, taps_o, cbias_o, sbias_o, skip_o, decay_o, square_s = refs[n1 + n2 :]
    er = outg_o.shape[0]
    dr = keep_o.shape[0]

    def total(parts):
        acc = parts[0][...].astype(F32)
        for part in parts[1:]:
            acc = acc + part[...].astype(F32)
        return acc

    x = total(one)
    inner = x.shape[1] - 2 * LANES
    z = total(two)
    for out, at in ((keep_o, 0), (send_o, dr)):
        out[:, :inner] = x[at : at + dr, :inner]
        out[:, inner : 2 * inner] = z[at : at + dr, :inner]
        out[:, 2 * inner :] = x[at : at + dr, inner + LANES :]
    outg_o[...] = z[:, inner:]
    select_o[...] = x[:, inner : inner + select_o.shape[1]]
    square_s[...] = jnp.zeros_like(square_s)
    square_s[:er] = x[:, inner : inner + LANES]
    step_o[...] = jnp.transpose(square_s[...])[LANES - rank :, :er]
    square_s[:er] = x[:, inner + LANES :]
    table = jnp.transpose(square_s[...])[:, :er]
    taps_o[...] = table[0:4]
    cbias_o[...] = table[ROW_BIAS : ROW_BIAS + 1]
    sbias_o[...] = table[ROW_STEP : ROW_STEP + 1]
    skip_o[...] = table[ROW_SKIP : ROW_SKIP + 1]
    decay_o[...] = table[ROW_DECAY : ROW_DECAY + states]


def spread_kernel(span, idx, keep, got, in_proj, norm, in_o, norm_o, moe_o, router_o, square_s):
    dr = keep.shape[0]
    inner2 = keep.shape[1] - LANES
    first = idx[3] == 0
    acc = jnp.zeros((dr, LANES), F32)
    for k in range(inner2 // span):
        mine = keep[:, k * span : (k + 1) * span]
        peer = got[:, k * span : (k + 1) * span]
        for at, part in ((2 * k * span, jnp.where(first, mine, peer)), ((2 * k + 1) * span, jnp.where(first, peer, mine))):
            in_o[:, at : at + span] = part
            terms = part * in_proj[:, at : at + span].astype(F32)
            for j in range(0, span, LANES):
                acc = acc + terms[:, j : j + LANES]
    table = keep[:, inner2:] + got[:, inner2:]
    at = ROW_FEATURE
    total = jnp.sum(acc, axis=1, keepdims=True)
    square_s[...] = jnp.zeros_like(square_s)
    square_s[:dr] = jnp.where(iota(table.shape, 1) == at, total, table)
    flat = jnp.transpose(square_s[...])[:, :dr]
    norm_o[...] = flat[at : at + 1] / norm[...].astype(F32)
    moe_o[...] = flat[at + 1 : at + 2]
    router_o[...] = flat[at + 2 : at + 2 + router_o.shape[0]]


def body(
    sizes,
    tokens,
    cotangent,
    seq_lens,
    routes,
    norm_gain,
    input_proj,
    conv_weight,
    conv_bias,
    select_proj,
    step_proj,
    step_bias,
    decay_log,
    skip_gain,
    output_proj,
    moe_gain,
    router_weight,
    up_weight,
    down_weight,
):
    ny, nz, nx = sizes
    nf = nz * nx
    ng = ny * nf
    tok, width = tokens.shape
    rank, er = step_proj.shape
    states = decay_log.shape[0]
    experts = router_weight.shape[1]
    capacity = 5 * tok // (4 * experts)
    dr = norm_gain.shape[0]
    inner = ng * er
    rows = 2 * tok
    small_n = -(-(ROW_DECAY + states) // 8) * 8
    dn = -(-(2 + experts) // 8) * 8
    plan = Plan(ny, nz, nx, er)
    idx = jnp.stack([lax.axis_index(a) for a in ("y", "z", "x", "c")]).astype(jnp.int32)

    order = np.arange(width).reshape(ny, 2, nf, dr).transpose(0, 2, 1, 3)
    nat = np.stack([order.reshape(width), order[:, :, ::-1].reshape(width)])
    nat = jnp.asarray(nat, jnp.int32)

    span = nf * er
    hid = up_weight.shape[1]
    sizes = [hid * 26 // 48, hid * 28 // 48]
    sizes.append(2 * hid - sum(sizes))
    parts = cut_rows(sizes, hid)
    mine_w, send_w, ch, up_send = call(
        functools.partial(pack_kernel, span),
        [((dr, 2 * inner + LANES), BF16), ((dr, 2 * inner + LANES), BF16), ((er, 2 * LANES), BF16), ((sizes[0], width), BF16)],
        [idx]
        + [
            in_hbm(v)
            for v in (input_proj, norm_gain[None], moe_gain[None], router_weight.T, conv_weight, conv_bias[None], select_proj, step_proj, step_bias[None], decay_log, skip_gain[None], up_weight)
        ],
        [SMEM] + [None] * 11 + [HBM],
        scratch=[pltpu.VMEM((LANES, LANES), F32), pltpu.VMEM((LANES, LANES), F32), pltpu.SemaphoreType.DMA],
        name="pack",
        us=1,
    )
    got_w = swap(send_w, "c")
    group1, group2 = call(
        merge_kernel,
        [((er, inner + 2 * LANES), BF16), ((er, inner + width), BF16)],
        [mine_w, got_w, ch, output_proj],
        name="merge",
        us=1,
    )
    tok2 = jnp.concatenate([tokens, swap(tokens, "c")], axis=0)
    lens2 = jnp.concatenate([seq_lens, swap(seq_lens, "c")], axis=0)
    up_one = swap(up_send, "y")
    sends = call(
        functools.partial(split_kernel, parts[1:]),
        [((size, width), BF16) for size in sizes[1:]],
        [in_hbm(after(up_weight, group1)), in_hbm(down_weight)],
        [HBM, HBM],
        scratch=[pltpu.SemaphoreType.DMA((2 * len(sizes),))],
        name="split",
        us=2,
    )
    up_one = after(up_one, sends[0])
    pieces1, pieces2 = plan.gather([group1, group2], (up_one, tok2, lens2))

    fetch_sem = pltpu.SemaphoreType.DMA((ng,))
    emit_sem = pltpu.SemaphoreType.DMA((2 * ng,))
    u, xin, xc, selp, small_t, dnat, g1 = call(
        functools.partial(enter_kernel, plan),
        [((rows, width), BF16), kept((rows, inner), F32), ((rows, inner), BF16), ((rows, LANES), F32), ((small_n, inner), F32), kept((dn, width), F32), ((inner, inner + 2 * LANES), BF16)],
        [idx, lens2, tok2, nat] + pieces1,
        [SMEM, SMEM, None, None] + [HBM] * len(pieces1),
        scratch=[fetch_sem],
        name="enter",
    )
    selq = swap(selp, "c")
    middle = (pieces2[min(2, len(pieces2) - 1)], xc)
    part_two = swap(after(sends[0], middle), "y")
    part_three = swap(after(sends[1], middle), "y")
    g1sel_spec = pl.BlockSpec((inner, LANES), lambda i: (0, inner // LANES))
    chunks = tok // 8
    ys, sel, check = call(
        functools.partial(scan_kernel, rank, states),
        [((rows, inner), F32), kept((rows, LANES), F32), ((2 * chunks, states, inner), F32, HBM, True)],
        [lens2, selp, selq, xc, g1, small_t],
        [SMEM, None, None, None, g1sel_spec, None],
        scratch=[pltpu.VMEM((rows, inner), F32), pltpu.VMEM((rows, inner), F32), pltpu.VMEM((2, states, tok), F32), pltpu.VMEM((2, states, tok), F32), pltpu.VMEM((states, inner), F32), pltpu.VMEM((2, states, inner), F32), pltpu.VMEM((2 * chunks, states, inner), F32), pltpu.SemaphoreType.DMA((chunks,))],
        name="scan",
        us=9,
    )
    br_mine, br_send, g2 = call(
        functools.partial(gate_kernel, plan),
        [((tok, width), F32), ((tok, width), F32), ((inner, inner + width), BF16)],
        [idx, u, xc, ys, small_t] + pieces2,
        [SMEM] + [None] * 4 + [HBM] * len(pieces2),
        scratch=[fetch_sem],
        name="gate",
    )
    br_got = swap(br_send, "c")
    slots = Slots(capacity, 2 * width)
    disp, hidden, gate = call(
        functools.partial(moe_enter_kernel, slots, experts, capacity),
        [kept((8 * experts, slots.lanes), BF16), kept((tok, width), F32), kept((tok, LANES), F32)],
        [seq_lens, tokens, in_hbm(cotangent), routes.T, br_mine, br_got, in_hbm(dnat)],
        [SMEM] + [None] * 6,
        name="moe_enter",
    )
    disp = after(disp, part_two)
    line = exchange(disp, nf)
    peer = swap(line, "c")
    line_y = swap(line, "y")
    total = slots.rows(2 * nf)
    tail = max(slots.rows(2 * nf), 8)
    weight_s = pltpu.VMEM((hid, width), BF16)
    tail_s = pltpu.VMEM((tail, 2 * width), F32)
    early = sum(1 for spans in parts for span in spans if span[0] == 0)
    both, acc, act, slope, up_near = call(
        functools.partial(expert_own_kernel, slots, parts[:-1]),
        [((total, 2 * width), BF16), ((total, 2 * width), F32), ((total, hid), BF16), ((total, hid), F32), ((hid, width), BF16)],
        [line, peer] + [in_hbm(w) for w in (up_weight, down_weight, up_one, part_two)],
        [None, None] + [HBM] * 4,
        scratch=[weight_s, weight_s, tail_s, pltpu.SemaphoreType.DMA((2 + early,))],
        name="expert_own",
        us=6,
    )
    out_own, out_peer = call(
        functools.partial(expert_other_kernel, slots, parts[1:]),
        [(line.shape, F32), (line.shape, BF16)],
        [both, acc, act, slope, up_near, part_two, part_three],
        [None] * 5 + [HBM] * 2,
        scratch=[pltpu.VMEM((total, 2 * width), F32), weight_s, tail_s, pltpu.SemaphoreType.DMA((3,))],
        name="expert_other",
        us=3,
    )
    grads = [((1, hid, width), F32)] * 2
    weights = [in_hbm(up_weight), in_hbm(down_weight)]
    near = call(near_grad_kernel, grads, [both] + weights, name="near_grad", us=4)
    peer_y = swap(after(line_y, near[0]), "c")
    up_grad, down_grad = call(
        functools.partial(far_grad_kernel, slots),
        grads,
        [line_y, peer_y] + weights + near,
        scratch=[pltpu.VMEM((total, 2 * width), BF16), tail_s],
        name="far_grad",
        us=8,
    )
    summed = (out_own + swap(out_peer, "c").astype(F32)).astype(BF16)
    back = exchange(summed, nf)
    back = after(back, up_grad)
    result, ghid, gbr, dgrad = call(
        functools.partial(moe_leave_kernel, slots, experts, capacity),
        [((tok, width), BF16), ((tok, width), F32), ((tok, width), BF16), ((dn, width), F32)],
        [in_hbm(seq_lens), in_hbm(routes.T), in_hbm(cotangent), in_hbm(hidden), in_hbm(gate), in_hbm(dnat), back],
        [SMEM] + [None] * 6,
        name="moe_leave",
    )
    gbr_got = swap(gbr, "c")
    gy, gzg, *shared2 = call(
        functools.partial(gate_back_kernel, plan),
        [((rows, inner), F32), ((rows, inner), BF16)] + plan.shared_outs(inner + width),
        [idx, gbr, gbr_got, g2, xc, ys, small_t, u],
        [SMEM] + [None] * 7,
        scratch=[pltpu.VMEM((inner, inner + width), BF16), emit_sem],
        name="gate_back",
    )
    gsel, gxcs, gsr, q, smallg = call(
        functools.partial(scan_back_kernel, rank, states),
        [((rows, LANES), F32), ((rows, inner), F32), ((rows, inner), BF16), ((rows, LANES), BF16), ((small_n, inner), F32)],
        [lens2, gy, xc, sel, small_t, g1, in_hbm(check)],
        [SMEM] + [None] * 4 + [g1sel_spec, HBM],
        scratch=[pltpu.VMEM((rows, inner), F32)] * 4 + [pltpu.VMEM((2, states, tok), F32)] * 2 + [pltpu.VMEM((rows, GROUP_TOKENS * states), F32)] * 2 + [pltpu.VMEM((states, inner), F32), pltpu.VMEM((2, states, inner), F32), pltpu.VMEM((states, inner), F32), pltpu.VMEM((rows // GROUP_TOKENS, 2 * GROUP_TOKENS, GROUP_TOKENS * states), BF16)] + [pltpu.VMEM((2, GROUP_TOKENS * states, inner), BF16)] * 3 + [pltpu.VMEM((rows, inner), F32)] * 2 + [pltpu.VMEM((2 * chunks, states, inner), F32), pltpu.SemaphoreType.DMA],
        name="scan_back",
        us=16,
    )
    shared2[-1] = after(shared2[-1], gsel)
    sums2 = plan.reduce1(shared2, "two")
    gsel = after(gsel, sums2[0])
    gsel_got = swap(gsel, "c")
    gxin, *shared1 = call(
        functools.partial(leave_kernel, plan),
        [((rows, inner), BF16)] + plan.shared_outs(inner + 2 * LANES),
        [idx, lens2, nat, gsel, gsel_got, gxcs, gsr, q, smallg, xin, xc, u, small_t, g1, dgrad],
        [SMEM, SMEM] + [None] * 13,
        scratch=[pltpu.VMEM((inner, inner + 2 * LANES), BF16), emit_sem],
        name="leave",
        us=5,
    )
    square_spec = pl.BlockSpec((inner, inner), lambda i: (0, 0))
    gn_mine, gn_send = call(
        back_kernel,
        [((tok, width), F32), ((tok, width), F32)],
        [idx, nat, gxin, gzg, g1, g2],
        [SMEM, None, None, None, square_spec, square_spec],
        name="back",
        us=3,
    )
    sums2 = plan.reduce2(sums2, "two")
    parts2 = plan.reduce3(sums2)
    shared1 = [after(part, sums2[0]) for part in shared1]
    sums1 = plan.reduce1(shared1, "one")
    if plan.fast:
        sums1[-1] = after(sums1[-1], tuple(parts2))
    parts1 = plan.reduce3(plan.reduce2(sums1, "one"))
    gn_got = swap(gn_send, "c")
    (input_grad,) = call(
        final_kernel, [((tok, width), F32)], [tokens, gn_mine, gn_got, ghid, dnat], name="final", us=2
    )
    sel_n = select_proj.shape[1]
    keep_w, send_back, out_grad, select_grad, step_grad, taps_grad, cb, sb, sk, decay_grad = call(
        functools.partial(share_kernel, len(parts1), len(parts2), rank, states),
        [((dr, 2 * inner + LANES), F32)] * 2
        + [((er, width), F32), ((er, sel_n), F32), ((rank, er), F32), ((4, er), F32), ((1, er), F32), ((1, er), F32), ((1, er), F32), ((states, er), F32)],
        list(parts1) + list(parts2),
        scratch=[pltpu.VMEM((LANES, LANES), F32)],
        name="share",
        us=1,
    )
    in_grad, norm_grad, moe_grad, router_grad = call(
        functools.partial(spread_kernel, span),
        [((dr, 4 * inner), F32), ((1, dr), F32), ((1, dr), F32), ((experts, dr), F32)],
        [idx, keep_w, swap(send_back, "c"), input_proj, norm_gain[None]],
        [SMEM, None, None, None, None],
        scratch=[pltpu.VMEM((LANES, LANES), F32)],
        name="spread",
        us=1,
    )
    return (
        result,
        input_grad,
        norm_grad[0],
        in_grad,
        taps_grad,
        cb[0],
        select_grad,
        step_grad,
        sb[0],
        decay_grad,
        sk[0],
        out_grad,
        moe_grad[0],
        router_grad.T,
        up_grad,
        down_grad,
    )


def solution(mesh):
    dp, fsdp = mesh.shape["dp"], mesh.shape["fsdp"]
    ny, nx = dp // 2, 2
    nz = fsdp // nx
    fine = Mesh(mesh.devices.reshape(ny, 2, nz, nx), ALL)
    tok = P(ALL, None)
    vec = P(ALL)
    col = P(None, ALL)
    exp = P(("z", "x"), ("y", "c"), None)
    in_specs = (tok, tok, tok, tok, vec, tok, col, vec, tok, col, vec, col, vec, tok, vec, tok, exp, exp)
    out_specs = (tok, tok, vec, tok, col, vec, tok, col, vec, col, vec, tok, vec, tok, exp, exp)
    return jax.shard_map(
        functools.partial(body, (ny, nz, nx)), mesh=fine, in_specs=in_specs, out_specs=out_specs, check_vma=False
    )
```
